32 devices in a mesh: outer: 4 (over y, x), inner: 8 (over z, core).
Axes of the slice: x: 2, y: 2, z: 4, core: 2. Of those that a mesh axis runs over, the one named last changes fastest.
Arguments:
- query: bfloat16 [4096, 512], P(('outer', 'inner')), may hold values from -6 to 6
- key: bfloat16 [4096, 128], P(('outer', 'inner')), may hold values from -6 to 6
- value: bfloat16 [4096, 128], P(('outer', 'inner')), may hold values from -6 to 6
- out: bfloat16 [4096, 512], P(('outer', 'inner')), may hold values from -4 to 4
- grad_out: bfloat16 [4096, 512], P(('outer', 'inner')), may hold values from -12 to 12
- lse: float32 [4, 4096], P(None, ('outer', 'inner')), may hold values from -60 to 60, as said below
- positions: int32 [4096], P(('outer', 'inner')), may hold values from 0 to 4095, as said below
Outputs:
- grad_query: bfloat16 [4096, 512], P(('outer', 'inner'))
- grad_key: bfloat16 [4096, 128], P(('outer', 'inner'))
- grad_value: bfloat16 [4096, 128], P(('outer', 'inner'))
The draws below stay inside these ranges and needn't reach their ends.
Inputs may be any that keep to these rules, and one draw needn't show every extreme that they name: positions is a permutation of 0 to 4095; every aligned run of 64 rows holds 64 consecutive positions in increasing order, starting at a multiple of 64. lse[h, i] is the log of the sum of exp(scores[h, i, j]) over all j with positions[j] <= positions[i].
All inputs are finite; a program needn't handle non-finite values.
Results may differ from the reference program's by a relative error of at most 0.005.
Values may be sent and summed in bfloat16 or wider, within the bound.
No kernel may reach another device: no remote copies, remote signals or barrier semaphores. Data moves between devices by JAX's collectives and lax.ppermute only.
A program may use at most 64 MiB of HBM per device.

```python
import jax
import jax.numpy as jnp
from jax import lax

DH = 128
HEADS = 4
HALF = 64
SEQ = 4096


def shared_draws(key, spread):
    order = jax.random.permutation(jax.random.fold_in(key, 11), SEQ // HALF).astype(jnp.int32)
    positions = (order[:, None] * HALF + jnp.arange(HALF, dtype=jnp.int32)[None, :]).reshape(SEQ).astype(jnp.int32)
    qkey = jax.random.fold_in(key, 12)
    kkey = jax.random.fold_in(key, 13)
    normal_q = jax.random.normal(jax.random.fold_in(qkey, 1), (SEQ, HEADS * DH), jnp.float32)
    rows_q = jnp.exp(spread * jax.random.uniform(jax.random.fold_in(qkey, 3), (SEQ, 1), jnp.float32, -1.0, 1.0))
    normal_k = jax.random.normal(jax.random.fold_in(kkey, 1), (SEQ, DH), jnp.float32)
    rows_k = jnp.exp(spread * jax.random.uniform(jax.random.fold_in(kkey, 3), (SEQ, 1), jnp.float32, -1.0, 1.0))
    query = jnp.clip(1.6 * rows_q * normal_q, -6.0, 6.0).astype(jnp.bfloat16)
    key_arr = jnp.clip(1.6 * rows_k * normal_k, -6.0, 6.0).astype(jnp.bfloat16)
    q3 = query.reshape(SEQ, HEADS, DH).astype(jnp.float32)
    kf = key_arr.astype(jnp.float32)
    block = 512 if SEQ % 512 == 0 else SEQ

    def one(index):
        start = (index * block).astype(jnp.int32)
        qb = lax.dynamic_slice_in_dim(q3, start, block, 0)
        pb = lax.dynamic_slice_in_dim(positions, start, block, 0)
        scores = DH ** (-0.5) * jnp.einsum('rhd,kd->hrk', qb, kf)
        allowed = positions[None, None, :] <= pb[None, :, None]
        scores = jnp.where(allowed, scores, -1e+30)
        return jax.nn.logsumexp(scores, axis=2)
    parts = lax.map(one, jnp.arange(SEQ // block))
    lse = jnp.transpose(parts, (1, 0, 2)).reshape(HEADS, SEQ).astype(jnp.float32)
    return (positions, query, key_arr, lse)


def draw_positions(key, part):
    return shared_draws(key, 0.0)[0]


def draw_query(key, part):
    return shared_draws(key, 0.0)[1]


def draw_key(key, part):
    return shared_draws(key, 0.0)[2]


def draw_lse(key, part):
    return shared_draws(key, 0.0)[3]


def level_of(rng, extent, cuts, smallest, high):
    level, own = 1.0, jax.random.fold_in(rng, 6)
    for position, shards_of in cuts:
        heights = jnp.exp(jax.random.uniform(jax.random.fold_in(own, position), (shards_of,), jnp.float32, smallest / len(cuts), high / len(cuts)))
        level = level * jnp.repeat(heights, extent[position] // shards_of).reshape([-1 if axis == position else 1 for axis in range(len(extent))])
    return level


def normal_values(stream_key, extent, scale, reach, pieces=(), kind=jnp.bfloat16):
    result = scale * jax.random.normal(stream_key, extent, jnp.float32)
    if pieces:
        result = result * level_of(stream_key, extent, pieces, -0.22, 0.18)
    return jnp.clip(result, -reach, reach).astype(kind)


def setup_inputs(seed: int = 0) -> dict:
    seeds = jax.random.split(jax.random.key(seed), 8)
    return {
        "query": draw_query(jax.random.fold_in(seeds[7], 71), 0),
        "key": draw_key(jax.random.fold_in(seeds[7], 71), 0),
        "value": normal_values(seeds[2], (SEQ, DH), 1.0, 6.0, ((0, 32),)),
        "out": normal_values(seeds[3], (SEQ, HEADS * DH), 0.5, 4.0, ((0, 32),)),
        "grad_out": normal_values(seeds[4], (SEQ, HEADS * DH), 2.0, 12.0, ((0, 32),)),
        "lse": draw_lse(jax.random.fold_in(seeds[7], 71), 0),
        "positions": draw_positions(jax.random.fold_in(seeds[7], 71), 0),
    }


def reference(query, key, value, out, grad_out, lse, positions):
    scale = DH ** -0.5
    q3 = query.reshape(SEQ, HEADS, DH).astype(jnp.float32)
    g3 = grad_out.reshape(SEQ, HEADS, DH).astype(jnp.float32)
    o3 = out.reshape(SEQ, HEADS, DH).astype(jnp.float32)
    delta = jnp.einsum('rhd,rhd->hr', g3, o3)
    kf = key.astype(jnp.float32)
    vf = value.astype(jnp.float32)
    block = 512 if SEQ % 512 == 0 else SEQ
    count = SEQ // block

    def step(carry, index):
        acc_key, acc_value = carry
        start = (index * block).astype(jnp.int32)
        qb = lax.dynamic_slice_in_dim(q3, start, block, 0)
        gb = lax.dynamic_slice_in_dim(g3, start, block, 0)
        lb = lax.dynamic_slice_in_dim(lse, start, block, 1)
        db = lax.dynamic_slice_in_dim(delta, start, block, 1)
        pb = lax.dynamic_slice_in_dim(positions, start, block, 0)
        scores = scale * jnp.einsum('rhd,kd->hrk', qb, kf)
        allowed = positions[None, None, :] <= pb[None, :, None]
        probs = jnp.where(allowed, jnp.exp(scores - lb[:, :, None]), 0.0)
        probs_low = lax.optimization_barrier(probs.astype(jnp.bfloat16)).astype(jnp.float32)
        acc_value = acc_value + jnp.einsum('hrk,rhd->kd', probs_low, gb)
        dprobs = jnp.einsum('rhd,kd->hrk', gb, vf)
        dscores = lax.optimization_barrier((probs * (dprobs - db[:, :, None])).astype(jnp.bfloat16)).astype(jnp.float32)
        grad_q = scale * jnp.einsum('hrk,kd->rhd', dscores, kf)
        acc_key = acc_key + jnp.einsum('hrk,rhd->kd', dscores, qb)
        return (acc_key, acc_value), grad_q.astype(jnp.bfloat16)

    zeros = jnp.zeros((SEQ, DH), jnp.float32)
    (acc_key, acc_value), grads = lax.scan(step, (zeros, zeros), jnp.arange(count))
    grad_query = grads.reshape(SEQ, HEADS * DH)
    return grad_query, (scale * acc_key).astype(jnp.bfloat16), acc_value.astype(jnp.bfloat16)
```

```python
import functools
import math

import jax
import jax.numpy as jnp
from jax import lax
from jax.experimental import pallas as pl
from jax.experimental.pallas import tpu as pltpu
from jax.sharding import PartitionSpec as P

BF = jnp.bfloat16
F32 = jnp.float32
RUN = 64
LOG2E = math.log2(math.e)
VMEM = pl.BlockSpec(memory_space=pltpu.VMEM)
NT = (((1,), (1,)), ((), ()))


def swapped(block, axis, mask):
    pairs = [(i, i ^ mask) for i in range(lax.axis_size(axis))]
    return lax.ppermute(block, axis, pairs)


def three_parts(x):
    hi = x.astype(BF)
    rest = x - hi.astype(F32)
    mid = rest.astype(BF)
    low = (rest - mid.astype(F32)).astype(BF)
    return [hi, mid, low]


def dot(a, b, dims=(((1,), (0,)), ((), ()))):
    return lax.dot_general(a, b, dims, preferred_element_type=F32)


def pack_kernel(q_ref, k_ref, v_ref, o_ref, g_ref, lse_ref, pos_ref, x_ref, kv_ref):
    rows, width = k_ref.shape
    heads = q_ref.shape[1] // width
    ones = jnp.ones((8, width), BF)
    deltas = []
    for h in range(heads):
        cols = slice(h * width, (h + 1) * width)
        q = q_ref[:, cols]
        g = g_ref[:, cols]
        x_ref[h * rows : (h + 1) * rows, :] = q
        x_ref[(heads + h) * rows : (heads + h + 1) * rows, :] = g
        prod = g.astype(F32) * o_ref[:, cols].astype(F32)
        hi = prod.astype(BF)
        low = (prod - hi.astype(F32)).astype(BF)
        deltas.append((dot(ones, hi, NT) + dot(ones, low, NT))[:1])
    run = (pos_ref[...] // RUN).astype(F32)
    extra = (
        three_parts(lse_ref[...] * LOG2E)
        + three_parts(jnp.concatenate(deltas, axis=0))
        + [run.astype(BF), jnp.zeros((32 - 6 * heads - 1, rows), BF)]
    )
    x_ref[2 * heads * rows :, :] = jnp.concatenate([e.astype(F32) for e in extra], axis=0).astype(BF)
    kv_ref[:rows, :] = k_ref[...]
    kv_ref[rows : 2 * rows, :] = v_ref[...]
    lane = lax.broadcasted_iota(jnp.int32, run.shape, 1)
    ids = [
        jnp.max(jnp.where(lane == r * RUN, run, 0.0), axis=1, keepdims=True)
        for r in range(rows // RUN)
    ]
    wide = [jnp.broadcast_to(i, (1, width)) for i in ids]
    wide.append(jnp.zeros((16 - len(ids), width), F32))
    kv_ref[2 * rows :, :] = jnp.concatenate(wide, axis=0).astype(BF)


def core_kernel(nq, nk, rows, heads, scale, *refs):
    x_refs = refs[:nq]
    kv_refs = refs[nq : nq + nk]
    dq_own, dq_far, dkv_own, dkv_sib = refs[nq + nk : nq + nk + 4]
    q_s, g_s, k_s, kt_s, v_s, lse_s, del_s, run_s, krun_s, dqt_s, dk_s, dv_s = refs[nq + nk + 4 :]
    width = 128
    hr = heads * rows
    chunk = 2 * rows
    n_chunks = nk // 2
    runs = chunk // RUN
    for b in range(nq):
        q_s[b] = x_refs[b][:hr, :]
        g_s[b] = x_refs[b][hr : 2 * hr, :]
        e = x_refs[b][2 * hr :, :].astype(F32)
        lse = e[0:heads] + e[heads : 2 * heads] + e[2 * heads : 3 * heads]
        delta = e[3 * heads : 4 * heads] + e[4 * heads : 5 * heads] + e[5 * heads : 6 * heads]
        run = e[6 * heads : 6 * heads + 1]
        for h in range(heads):
            cols = slice(h * rows, (h + 1) * rows)
            lse_s[b, :, cols] = jnp.broadcast_to(lse[h : h + 1], (8, rows))
            del_s[b, :, cols] = jnp.broadcast_to(delta[h : h + 1], (8, rows))
            run_s[b, :, cols] = jnp.broadcast_to(run, (8, rows))
    for j in range(nk):
        at = slice(j * rows, (j + 1) * rows)
        k = kv_refs[j][:rows, :]
        k_s[at, :] = k
        v_s[at, :] = kv_refs[j][rows : 2 * rows, :]
        kt_s[:, at] = k.astype(F32).T.astype(BF)
        e = kv_refs[j][2 * rows :, :].astype(F32)
        for r in range(rows // RUN):
            krun_s[j * (rows // RUN) + r] = jnp.broadcast_to(e[r : r + 1], (8, width))
    dqt_s[...] = jnp.zeros_like(dqt_s)
    dk_s[...] = jnp.zeros_like(dk_s)
    dv_s[...] = jnp.zeros_like(dv_s)

    def unit(b, c, own):
        at = pl.ds(pl.multiple_of(c * chunk, chunk), chunk)
        k, v = k_s[at, :], v_s[at, :]
        q, g = q_s[b], g_s[b]
        st = dot(k, q, NT)
        dpt = dot(v, g, NT)
        lse = lse_s[b]
        delta = del_s[b]
        qrun = run_s[b]
        p_parts, d_parts = [], []
        for r in range(runs):
            sl = slice(r * RUN, (r + 1) * RUN)
            kr = krun_s[c * runs + r]
            kr = jnp.concatenate([kr] * (hr // width), axis=1)
            row = jnp.where(kr <= qrun, lse, 1e30)[:1]
            arg = st[sl] * (scale * LOG2E) - row
            if own and r < rows // RUN:
                shape = (RUN, hr)
                i = lax.rem(lax.broadcasted_iota(jnp.int32, shape, 1), rows)
                j = lax.broadcasted_iota(jnp.int32, shape, 0) + r * RUN
                same = (i >= r * RUN) & (i < (r + 1) * RUN)
                arg = jnp.where(same & (j > i), -1e30, arg)
            p = jnp.exp2(arg)
            p_parts.append(p.astype(BF))
            d_parts.append((p * (dpt[sl] - delta[:1])).astype(BF))
        p = jnp.concatenate(p_parts, axis=0)
        d = jnp.concatenate(d_parts, axis=0)
        dv_s[at, :] += dot(p, g)
        dk_s[at, :] += dot(d, q)
        dqt_s[b] += dot(kt_s[:, at], d)

    unit(0, 0, True)

    def body(n, carry):
        unit(n // n_chunks, n % n_chunks, False)
        return carry

    lax.fori_loop(1, nq * n_chunks, body, 0)
    dq_own[...] = dqt_s[0]
    for b in range(1, nq):
        dq_far[b - 1] = dqt_s[b].astype(BF)
    for c in range(n_chunks):
        here = slice(c * chunk, c * chunk + rows)
        there = slice(c * chunk + rows, (c + 1) * chunk)
        dkv_own[c, :rows, :] = dk_s[here, :]
        dkv_own[c, rows:, :] = dv_s[here, :]
        dkv_sib[c, :rows, :] = dk_s[there, :].astype(BF)
        dkv_sib[c, rows:, :] = dv_s[there, :].astype(BF)


def final_kernel(nq, nz, rows, heads, scale, dq_own, dkv_own, *refs):
    dq_refs = refs[: nq - 1]
    dkv_refs = refs[nq - 1 : nq - 1 + nz - 1]
    gq_ref, gk_ref, gv_ref = refs[nq - 1 + nz - 1 :]
    dq = dq_own[...]
    for r in dq_refs:
        dq = dq + r[...].astype(F32)
    for h in range(heads):
        part = dq[:, h * rows : (h + 1) * rows]
        gq_ref[:, h * 128 : (h + 1) * 128] = (scale * part).T.astype(BF)
    dkv = dkv_own[...]
    for r in dkv_refs:
        dkv = dkv + r[...].astype(F32)
    gk_ref[...] = (scale * dkv[:rows]).astype(BF)
    gv_ref[...] = dkv[rows:].astype(BF)


def on_device(query, key, value, out, grad_out, lse, positions):
    rows, width = key.shape
    heads = query.shape[1] // width
    hr = heads * rows
    scale = width ** (-0.5)
    nq = lax.axis_size("outer")
    nk = lax.axis_size("inner")
    nz = nk // 2
    sds = jax.ShapeDtypeStruct
    x, kv = pl.pallas_call(
        pack_kernel,
        out_shape=(sds((2 * hr + 32, width), BF), sds((2 * rows + 16, width), BF)),
        in_specs=[VMEM] * 7,
        out_specs=(VMEM, VMEM),
    )(query, key, value, out, grad_out, lse, positions[None, :])

    xs = [x] + [swapped(x, "outer", s) for s in range(1, nq)]
    mine = [kv] + [swapped(kv, "inner", 2 * s) for s in range(1, nz)]
    kvs = []
    for block in mine:
        kvs += [block, swapped(block, "inner", 1)]

    dq_own, dq_far, dkv_own, dkv_sib = pl.pallas_call(
        functools.partial(core_kernel, nq, nk, rows, heads, scale),
        out_shape=(
            sds((width, hr), F32),
            sds((nq - 1, width, hr), BF),
            sds((nz, 2 * rows, width), F32),
            sds((nz, 2 * rows, width), BF),
        ),
        in_specs=[VMEM] * (nq + nk),
        out_specs=(VMEM,) * 4,
        scratch_shapes=[
            pltpu.VMEM((nq, hr, width), BF),
            pltpu.VMEM((nq, hr, width), BF),
            pltpu.VMEM((nk * rows, width), BF),
            pltpu.VMEM((width, nk * rows), BF),
            pltpu.VMEM((nk * rows, width), BF),
            pltpu.VMEM((nq, 8, hr), F32),
            pltpu.VMEM((nq, 8, hr), F32),
            pltpu.VMEM((nq, 8, hr), F32),
            pltpu.VMEM((nk * rows // RUN, 8, width), F32),
            pltpu.VMEM((nq, width, hr), F32),
            pltpu.VMEM((nk * rows, width), F32),
            pltpu.VMEM((nk * rows, width), F32),
        ],
        compiler_params=pltpu.CompilerParams(vmem_limit_bytes=40 * 1024 * 1024),
    )(*xs, *kvs)

    dq_got = [swapped(dq_far[s - 1], "outer", s) for s in range(1, nq)]
    sib = swapped(dkv_sib, "inner", 1)
    total = dkv_own + sib.astype(F32)
    dkv_got = [swapped(total[s].astype(BF), "inner", 2 * s) for s in range(1, nz)]

    return pl.pallas_call(
        functools.partial(final_kernel, nq, nz, rows, heads, scale),
        out_shape=(sds((rows, heads * width), BF), sds((rows, width), BF), sds((rows, width), BF)),
        in_specs=[VMEM] * (2 + nq - 1 + nz - 1),
        out_specs=(VMEM,) * 3,
    )(dq_own, total[0], *dq_got, *dkv_got)


def solution(mesh):
    tokens = P(("outer", "inner"), None)
    return jax.shard_map(
        on_device,
        mesh=mesh,
        in_specs=(tokens,) * 5 + (P(None, ("outer", "inner")), P(("outer", "inner"))),
        out_specs=(tokens,) * 3,
        check_vma=False,
    )
```

```python
import functools
import math

import jax
import jax.numpy as jnp
from jax import lax
from jax.experimental import pallas as pl
from jax.experimental.pallas import tpu as pltpu
from jax.sharding import PartitionSpec as P

BF = jnp.bfloat16
F32 = jnp.float32
RUN = 64
LOG2E = math.log2(math.e)
VMEM = pl.BlockSpec(memory_space=pltpu.VMEM)
SMALL = pltpu.CompilerParams(vmem_limit_bytes=16 * 1024 * 1024)
NN = (((1,), (0,)), ((), ()))
NT = (((1,), (1,)), ((), ()))
KEYS = 256
COLS = 256


def swapped(block, axis, mask):
    pairs = [(i, i ^ mask) for i in range(lax.axis_size(axis))]
    return lax.ppermute(block, axis, pairs)


def three_parts(x):
    hi = x.astype(BF)
    rest = x - hi.astype(F32)
    mid = rest.astype(BF)
    low = (rest - mid.astype(F32)).astype(BF)
    return [hi, mid, low]


def dot(a, b, dims=NN):
    return lax.dot_general(a, b, dims, preferred_element_type=F32)


def pack_kernel(q_ref, k_ref, v_ref, o_ref, g_ref, lse_ref, pos_ref, x_ref, kv_ref):
    rows, width = k_ref.shape
    heads = q_ref.shape[1] // width
    ones = jnp.ones((8, width), BF)
    deltas = []
    for h in range(heads):
        cols = slice(h * width, (h + 1) * width)
        q = q_ref[:, cols]
        g = g_ref[:, cols]
        x_ref[h * rows : (h + 1) * rows, :] = q
        x_ref[(heads + h) * rows : (heads + h + 1) * rows, :] = g
        prod = g.astype(F32) * o_ref[:, cols].astype(F32)
        hi = prod.astype(BF)
        low = (prod - hi.astype(F32)).astype(BF)
        deltas.append((dot(ones, hi, NT) + dot(ones, low, NT))[:1])
    run = (pos_ref[...] // RUN).astype(F32)
    extra = (
        three_parts(lse_ref[...] * LOG2E)
        + three_parts(jnp.concatenate(deltas, axis=0))
        + [run.astype(BF), jnp.zeros((32 - 6 * heads - 1, rows), BF)]
    )
    x_ref[2 * heads * rows :, :] = jnp.concatenate([e.astype(F32) for e in extra], axis=0).astype(BF)
    kv_ref[:rows, :] = k_ref[...]
    kv_ref[rows : 2 * rows, :] = v_ref[...]
    lane = lax.broadcasted_iota(jnp.int32, run.shape, 1)
    ids = [
        jnp.max(jnp.where(lane == r * RUN, run, 0.0), axis=1, keepdims=True)
        for r in range(rows // RUN)
    ]
    wide = [jnp.broadcast_to(i, (1, width)) for i in ids]
    wide.append(jnp.zeros((16 - len(ids), width), F32))
    kv_ref[2 * rows :, :] = jnp.concatenate(wide, axis=0).astype(BF)


def stack_kernel(rows, *refs):
    kv_refs, (k_ref, kt_ref, v_ref, run_ref) = refs[:-4], refs[-4:]
    per = rows // RUN
    for j, kv_ref in enumerate(kv_refs):
        at = slice(j * rows, (j + 1) * rows)
        k = kv_ref[:rows, :]
        k_ref[at, :] = k
        kt_ref[:, at] = k.astype(F32).T.astype(BF)
        v_ref[at, :] = kv_ref[rows : 2 * rows, :]
        e = kv_ref[2 * rows :, :].astype(F32)
        for r in range(per):
            run_ref[j * per + r] = jnp.broadcast_to(e[r : r + 1], (8, e.shape[1]))


def pair_kernel(first, last, rows, heads, scale, *refs):
    x_refs, refs = refs[:2], refs[2:]
    (k_ref, kt_ref, v_ref, run_ref), refs = refs[:4], refs[4:]
    if not first:
        (acc_in,), refs = refs[:1], refs[1:]
    dq_ref, dq_sib_ref, acc_ref, *far_refs = refs
    keys, width = k_ref.shape
    hr = heads * rows
    per = KEYS // RUN
    dqt = [[None] * (hr // COLS) for _ in range(2)]
    rowed = []
    for b in range(2):
        e = x_refs[b][2 * hr :, :].astype(F32)
        lse = e[0:heads] + e[heads : 2 * heads] + e[2 * heads : 3 * heads]
        delta = e[3 * heads : 4 * heads] + e[4 * heads : 5 * heads] + e[5 * heads : 6 * heads]
        run = e[6 * heads : 6 * heads + 1]
        rowed.append((lse, delta, run))
    for c in range(keys // KEYS):
        at = slice(c * KEYS, (c + 1) * KEYS)
        k, kt, v = k_ref[at, :], kt_ref[:, at], v_ref[at, :]
        dk = dv = None
        for b in range(2):
            lse, delta, run = rowed[b]
            for n in range(hr // COLS):
                cols = slice(n * COLS, (n + 1) * COLS)
                q = x_refs[b][cols, :]
                g = x_refs[b][hr + n * COLS : hr + (n + 1) * COLS, :]
                st = dot(k, q, NT)
                dpt = dot(v, g, NT)
                p_rows, d_rows = [], []
                for r in range(per):
                    sl = slice(r * RUN, (r + 1) * RUN)
                    krun = run_ref[c * per + r][:1]
                    p_heads, d_heads = [], []
                    for h in range(COLS // rows):
                        hl = slice(h * rows, (h + 1) * rows)
                        head = n * (COLS // rows) + h
                        row = jnp.where(krun <= run, lse[head : head + 1], 1e30)
                        arg = st[sl, hl] * (scale * LOG2E) - row
                        start = c * KEYS + r * RUN
                        if first and b == 0 and start < rows:
                            i = lax.broadcasted_iota(jnp.int32, (RUN, rows), 1) - start
                            j = lax.broadcasted_iota(jnp.int32, (RUN, rows), 0)
                            arg = jnp.where((i >= 0) & (i < j), -1e30, arg)
                        p = jnp.exp2(arg)
                        p_heads.append(p.astype(BF))
                        d_heads.append((p * (dpt[sl, hl] - delta[head : head + 1])).astype(BF))
                    p_rows.append(jnp.concatenate(p_heads, axis=1))
                    d_rows.append(jnp.concatenate(d_heads, axis=1))
                p = jnp.concatenate(p_rows, axis=0)
                d = jnp.concatenate(d_rows, axis=0)
                dv_n, dk_n, dq_n = dot(p, g), dot(d, q), dot(kt, d)
                dv = dv_n if dv is None else dv + dv_n
                dk = dk_n if dk is None else dk + dk_n
                old = dqt[b][n]
                dqt[b][n] = dq_n if old is None else old + dq_n
        for j in range(KEYS // rows):
            block = c * (KEYS // rows) + j
            sl = slice(j * rows, (j + 1) * rows)
            dk_j, dv_j = dk[sl], dv[sl]
            if not first:
                dk_j += acc_in[block, :rows, :]
                dv_j += acc_in[block, rows:, :]
            if last and block:
                far_refs[block - 1][:rows, :] = dk_j.astype(BF)
                far_refs[block - 1][rows:, :] = dv_j.astype(BF)
            else:
                acc_ref[block, :rows, :] = dk_j
                acc_ref[block, rows:, :] = dv_j
    for n in range(hr // COLS):
        cols = slice(n * COLS, (n + 1) * COLS)
        dq_ref[:, cols] = dqt[0][n]
        dq_sib_ref[:, cols] = dqt[1][n].astype(BF)


def final_kernel(rows, heads, scale, n_dq, dq_own, acc, *refs):
    dq_refs, dkv_refs, (gq_ref, gk_ref, gv_ref) = refs[:n_dq], refs[n_dq:-3], refs[-3:]
    dq = dq_own[...]
    for r in dq_refs:
        dq = dq + r[...].astype(F32)
    for h in range(heads):
        part = dq[:, h * rows : (h + 1) * rows]
        gq_ref[:, h * 128 : (h + 1) * 128] = (scale * part).T.astype(BF)
    dkv = acc[0]
    for r in dkv_refs:
        dkv = dkv + r[...].astype(F32)
    gk_ref[...] = (scale * dkv[:rows]).astype(BF)
    gv_ref[...] = dkv[rows:].astype(BF)


def pair_call(x, x_sib, stacked, acc, last, rows, heads, scale):
    sds = jax.ShapeDtypeStruct
    keys, width = stacked[0].shape
    blocks = keys // rows
    hr = heads * rows
    first = acc is None
    far = (blocks - 1) if last else 0
    args = (x, x_sib, *stacked) + (() if first else (acc,))
    return pl.pallas_call(
        functools.partial(pair_kernel, first, last, rows, heads, scale),
        out_shape=(
            sds((width, hr), F32),
            sds((width, hr), BF),
            sds((1 if last else blocks, 2 * rows, width), F32),
        )
        + (sds((2 * rows, width), BF),) * far,
        in_specs=[VMEM] * len(args),
        out_specs=(VMEM,) * (3 + far),
        compiler_params=SMALL,
        cost_estimate=pl.CostEstimate(
            flops=20 * keys * hr * width, bytes_accessed=1 << 20, transcendentals=2 * keys * hr
        ),
    )(*args)


def on_device(query, key, value, out, grad_out, lse, positions):
    rows, width = key.shape
    heads = query.shape[1] // width
    hr = heads * rows
    scale = width ** (-0.5)
    nq = lax.axis_size("outer")
    nz = lax.axis_size("inner") // 2
    sds = jax.ShapeDtypeStruct
    x, kv = pl.pallas_call(
        pack_kernel,
        out_shape=(sds((2 * hr + 32, width), BF), sds((2 * rows + 16, width), BF)),
        in_specs=[VMEM] * 7,
        out_specs=(VMEM, VMEM),
        compiler_params=SMALL,
    )(query, key, value, out, grad_out, lse, positions[None, :])

    xs = [x] + [swapped(x, "outer", s) for s in range(1, nq)]
    kvs = [kv] + [swapped(kv, "inner", 2 * s) for s in range(1, nz)]
    xs_sib = [swapped(block, "inner", 1) for block in xs]
    per = rows // RUN
    stacked = pl.pallas_call(
        functools.partial(stack_kernel, rows),
        out_shape=(
            sds((nz * rows, width), BF),
            sds((width, nz * rows), BF),
            sds((nz * rows, width), BF),
            sds((nz * per, 8, width), F32),
        ),
        in_specs=[VMEM] * nz,
        out_specs=(VMEM,) * 4,
        compiler_params=SMALL,
    )(*kvs)

    acc = None
    got = []
    for s in range(nq):
        dq, dq_sib, acc, *far = pair_call(
            xs[s], xs_sib[s], stacked, acc, s == nq - 1, rows, heads, scale
        )
        other = swapped(dq_sib, "inner", 1)
        if s == 0:
            dq_own = dq
            got.append(other)
        else:
            got.append(swapped((dq + other.astype(F32)).astype(BF), "outer", s))
    dkv_got = [swapped(far[s - 1], "inner", 2 * s) for s in range(1, nz)]

    return pl.pallas_call(
        functools.partial(final_kernel, rows, heads, scale, len(got)),
        out_shape=(sds((rows, heads * width), BF), sds((rows, width), BF), sds((rows, width), BF)),
        in_specs=[VMEM] * (2 + len(got) + nz - 1),
        out_specs=(VMEM,) * 3,
        compiler_params=SMALL,
    )(dq_own, acc, *got, *dkv_got)


def solution(mesh):
    tokens = P(("outer", "inner"), None)
    return jax.shard_map(
        on_device,
        mesh=mesh,
        in_specs=(tokens,) * 5 + (P(None, ("outer", "inner")), P(("outer", "inner"))),
        out_specs=(tokens,) * 3,
        check_vma=False,
    )
```

```python
import functools
import math

import jax
import jax.numpy as jnp
from jax import lax
from jax.experimental import pallas as pl
from jax.experimental.pallas import tpu as pltpu
from jax.sharding import PartitionSpec as P

BF = jnp.bfloat16
F32 = jnp.float32
RUN = 64
LOG2E = math.log2(math.e)
VMEM = pl.BlockSpec(memory_space=pltpu.VMEM)
SMALL = pltpu.CompilerParams(vmem_limit_bytes=16 * 1024 * 1024)
NN = (((1,), (0,)), ((), ()))
NT = (((1,), (1,)), ((), ()))
KEYS = 256
COLS = 256


def swapped(block, axis, mask):
    pairs = [(i, i ^ mask) for i in range(lax.axis_size(axis))]
    return lax.ppermute(block, axis, pairs)


def after(x, *first):
    return lax.optimization_barrier((x, *first))[0]


def three_parts(x):
    hi = x.astype(BF)
    rest = x - hi.astype(F32)
    mid = rest.astype(BF)
    low = (rest - mid.astype(F32)).astype(BF)
    return [hi, mid, low]


def dot(a, b, dims=NN):
    return lax.dot_general(a, b, dims, preferred_element_type=F32)


def pack_kernel(q_ref, k_ref, v_ref, o_ref, g_ref, lse_ref, pos_ref, x_ref, kv_ref, o_s, lse_s, pos_s, sems):
    rows, width = k_ref.shape
    heads = q_ref.shape[1] // width
    moves = [(lse_ref, lse_s), (pos_ref, pos_s), (o_ref, o_s)]
    for h in range(heads):
        cols = pl.ds(h * width, width)
        moves.append((g_ref.at[:, cols], x_ref.at[pl.ds((heads + h) * rows, rows), :]))
    for h in range(heads):
        cols = pl.ds(h * width, width)
        moves.append((q_ref.at[:, cols], x_ref.at[pl.ds(h * rows, rows), :]))
    moves.append((k_ref, kv_ref.at[pl.ds(0, rows), :]))
    moves.append((v_ref, kv_ref.at[pl.ds(rows, rows), :]))
    copies = [pltpu.make_async_copy(a, b, sems.at[n]) for n, (a, b) in enumerate(moves)]
    for copy in copies:
        copy.start()
    for copy in copies[: 3 + heads]:
        copy.wait()
    ones = jnp.ones((8, width), BF)
    deltas = []
    for h in range(heads):
        g = x_ref[(heads + h) * rows : (heads + h + 1) * rows, :]
        prod = g.astype(F32) * o_s[:, h * width : (h + 1) * width].astype(F32)
        hi = prod.astype(BF)
        low = (prod - hi.astype(F32)).astype(BF)
        deltas.append((dot(ones, hi, NT) + dot(ones, low, NT))[:1])
    run = (pos_s[...] // RUN).astype(F32)
    extra = (
        three_parts(lse_s[...] * LOG2E)
        + three_parts(jnp.concatenate(deltas, axis=0))
        + [run.astype(BF), jnp.zeros((32 - 6 * heads - 1, rows), BF)]
    )
    x_ref[2 * heads * rows :, :] = jnp.concatenate([e.astype(F32) for e in extra], axis=0).astype(BF)
    lane = lax.broadcasted_iota(jnp.int32, run.shape, 1)
    ids = [
        jnp.max(jnp.where(lane == r * RUN, run, 0.0), axis=1, keepdims=True)
        for r in range(rows // RUN)
    ]
    wide = [jnp.broadcast_to(i, (1, width)) for i in ids]
    wide.append(jnp.zeros((16 - len(ids), width), F32))
    kv_ref[2 * rows :, :] = jnp.concatenate(wide, axis=0).astype(BF)
    for copy in copies[3 + heads :]:
        copy.wait()


def stack_kernel(rows, *refs):
    kv_refs, (k_ref, kt_ref, v_ref, run_ref) = refs[:-4], refs[-4:]
    per = rows // RUN
    for j, kv_ref in enumerate(kv_refs):
        at = slice(j * rows, (j + 1) * rows)
        k = kv_ref[:rows, :]
        k_ref[at, :] = k
        kt_ref[:, at] = k.astype(F32).T.astype(BF)
        v_ref[at, :] = kv_ref[rows : 2 * rows, :]
        e = kv_ref[2 * rows :, :].astype(F32)
        for r in range(per):
            run_ref[j * per + r] = jnp.broadcast_to(e[r : r + 1], (8, e.shape[1]))


def pair_kernel(first, last, rows, heads, scale, *refs):
    x_refs, refs = refs[:2], refs[2:]
    (k_ref, kt_ref, v_ref, run_ref), refs = refs[:4], refs[4:]
    if not first:
        (acc_in,), refs = refs[:1], refs[1:]
    dq_ref, dq_sib_ref, acc_ref, *far_refs = refs
    keys, width = k_ref.shape
    hr = heads * rows
    per = KEYS // RUN
    dqt = [[None] * (hr // COLS) for _ in range(2)]
    rowed = []
    for b in range(2):
        e = x_refs[b][2 * hr :, :].astype(F32)
        lse = e[0:heads] + e[heads : 2 * heads] + e[2 * heads : 3 * heads]
        delta = e[3 * heads : 4 * heads] + e[4 * heads : 5 * heads] + e[5 * heads : 6 * heads]
        run = e[6 * heads : 6 * heads + 1]
        rowed.append((lse, delta, run))
    for c in range(keys // KEYS):
        at = slice(c * KEYS, (c + 1) * KEYS)
        k, kt, v = k_ref[at, :], kt_ref[:, at], v_ref[at, :]
        dk = dv = None
        for b in range(2):
            lse, delta, run = rowed[b]
            for n in range(hr // COLS):
                cols = slice(n * COLS, (n + 1) * COLS)
                q = x_refs[b][cols, :]
                g = x_refs[b][hr + n * COLS : hr + (n + 1) * COLS, :]
                st = dot(k, q, NT)
                dpt = dot(v, g, NT)
                p_rows, d_rows = [], []
                for r in range(per):
                    sl = slice(r * RUN, (r + 1) * RUN)
                    krun = run_ref[c * per + r][:1]
                    p_heads, d_heads = [], []
                    for h in range(COLS // rows):
                        hl = slice(h * rows, (h + 1) * rows)
                        head = n * (COLS // rows) + h
                        row = jnp.where(krun <= run, lse[head : head + 1], 1e30)
                        arg = st[sl, hl] * (scale * LOG2E) - row
                        start = c * KEYS + r * RUN
                        if first and b == 0 and start < rows:
                            i = lax.broadcasted_iota(jnp.int32, (RUN, rows), 1) - start
                            j = lax.broadcasted_iota(jnp.int32, (RUN, rows), 0)
                            arg = jnp.where((i >= 0) & (i < j), -1e30, arg)
                        p = jnp.exp2(arg)
                        p_heads.append(p.astype(BF))
                        d_heads.append((p * (dpt[sl, hl] - delta[head : head + 1])).astype(BF))
                    p_rows.append(jnp.concatenate(p_heads, axis=1))
                    d_rows.append(jnp.concatenate(d_heads, axis=1))
                p = jnp.concatenate(p_rows, axis=0)
                d = jnp.concatenate(d_rows, axis=0)
                dv_n, dk_n, dq_n = dot(p, g), dot(d, q), dot(kt, d)
                dv = dv_n if dv is None else dv + dv_n
                dk = dk_n if dk is None else dk + dk_n
                old = dqt[b][n]
                dqt[b][n] = dq_n if old is None else old + dq_n
        for j in range(KEYS // rows):
            block = c * (KEYS // rows) + j
            sl = slice(j * rows, (j + 1) * rows)
            dk_j, dv_j = dk[sl], dv[sl]
            if not first:
                dk_j += acc_in[block, :rows, :]
                dv_j += acc_in[block, rows:, :]
            if last and block:
                far_refs[block - 1][:rows, :] = dk_j.astype(BF)
                far_refs[block - 1][rows:, :] = dv_j.astype(BF)
            else:
                acc_ref[block, :rows, :] = dk_j
                acc_ref[block, rows:, :] = dv_j
    for n in range(hr // COLS):
        cols = slice(n * COLS, (n + 1) * COLS)
        dq_ref[:, cols] = dqt[0][n]
        dq_sib_ref[:, cols] = dqt[1][n].astype(BF)


def final_kernel(rows, heads, scale, n_dq, dq_own, acc, *refs):
    dq_refs, dkv_refs, (gq_ref, gk_ref, gv_ref) = refs[:n_dq], refs[n_dq:-3], refs[-3:]
    dq = dq_own[...]
    for r in dq_refs:
        dq = dq + r[...].astype(F32)
    for h in range(heads):
        part = dq[:, h * rows : (h + 1) * rows]
        gq_ref[:, h * 128 : (h + 1) * 128] = (scale * part).T.astype(BF)
    dkv = acc[0]
    for r in dkv_refs:
        dkv = dkv + r[...].astype(F32)
    gk_ref[...] = (scale * dkv[:rows]).astype(BF)
    gv_ref[...] = dkv[rows:].astype(BF)


def pair_call(x, x_sib, stacked, acc, last, rows, heads, scale):
    sds = jax.ShapeDtypeStruct
    keys, width = stacked[0].shape
    blocks = keys // rows
    hr = heads * rows
    first = acc is None
    far = (blocks - 1) if last else 0
    args = (x, x_sib, *stacked) + (() if first else (acc,))
    return pl.pallas_call(
        functools.partial(pair_kernel, first, last, rows, heads, scale),
        out_shape=(
            sds((width, hr), F32),
            sds((width, hr), BF),
            sds((1 if last else blocks, 2 * rows, width), F32),
        )
        + (sds((2 * rows, width), BF),) * far,
        in_specs=[VMEM] * len(args),
        out_specs=(VMEM,) * (3 + far),
        compiler_params=SMALL,
        cost_estimate=pl.CostEstimate(
            flops=20 * keys * hr * width, bytes_accessed=1 << 20, transcendentals=2 * keys * hr
        ),
    )(*args)


def on_device(query, key, value, out, grad_out, lse, positions):
    rows, width = key.shape
    heads = query.shape[1] // width
    hr = heads * rows
    scale = width ** (-0.5)
    nq = lax.axis_size("outer")
    nz = lax.axis_size("inner") // 2
    sds = jax.ShapeDtypeStruct
    x, kv = pl.pallas_call(
        pack_kernel,
        out_shape=(sds((2 * hr + 32, width), BF), sds((2 * rows + 16, width), BF)),
        in_specs=[pl.BlockSpec(memory_space=pltpu.HBM)] * 7,
        out_specs=(VMEM, VMEM),
        scratch_shapes=[
            pltpu.VMEM(out.shape, BF),
            pltpu.VMEM(lse.shape, F32),
            pltpu.VMEM((1, rows), jnp.int32),
            pltpu.SemaphoreType.DMA((5 + 2 * heads,)),
        ],
        compiler_params=SMALL,
    )(query, key, value, out, grad_out, lse, positions[None, :])

    x_sib = swapped(x, "inner", 1)
    kvs = [kv] + [None] * (nz - 1)
    for s in range(nz - 1, 1, -1):
        kvs[s] = swapped(kv, "inner", 2 * s)
    kvs[1] = swapped(after(kv, x_sib), "inner", 2)
    xs = [x] + [swapped(x if s < 3 else after(x, kvs[1]), "outer", s) for s in range(1, nq)]
    xs_sib = [x_sib] + [swapped(block, "inner", 1) for block in xs[1:]]
    per = rows // RUN
    stacked = pl.pallas_call(
        functools.partial(stack_kernel, rows),
        out_shape=(
            sds((nz * rows, width), BF),
            sds((width, nz * rows), BF),
            sds((nz * rows, width), BF),
            sds((nz * per, 8, width), F32),
        ),
        in_specs=[VMEM] * nz,
        out_specs=(VMEM,) * 4,
        compiler_params=SMALL,
    )(*kvs)

    acc = None
    got = []
    others = []
    for s in range(nq):
        block = after(xs[s], others[s - 2]) if s > 1 else xs[s]
        dq, dq_sib, acc, *far = pair_call(
            block, xs_sib[s], stacked, acc, s == nq - 1, rows, heads, scale
        )
        others.append(swapped(dq_sib, "inner", 1))
        if s == 0:
            dq_own = dq
            got.append(others[0])
        else:
            total = (dq + others[s].astype(F32)).astype(BF)
            got.append(swapped(total, "outer", s))
    dkv_got = [swapped(far[s - 1], "inner", 2 * s) for s in range(1, nz)]

    return pl.pallas_call(
        functools.partial(final_kernel, rows, heads, scale, len(got)),
        out_shape=(sds((rows, heads * width), BF), sds((rows, width), BF), sds((rows, width), BF)),
        in_specs=[VMEM] * (2 + len(got) + nz - 1),
        out_specs=(VMEM,) * 3,
        compiler_params=SMALL,
    )(dq_own, acc, *got, *dkv_got)


def solution(mesh):
    tokens = P(("outer", "inner"), None)
    return jax.shard_map(
        on_device,
        mesh=mesh,
        in_specs=(tokens,) * 5 + (P(None, ("outer", "inner")), P(("outer", "inner"))),
        out_specs=(tokens,) * 3,
        check_vma=False,
    )
```

```python
import functools
import math

import jax
import jax.numpy as jnp
from jax import lax
from jax.experimental import pallas as pl
from jax.experimental.pallas import tpu as pltpu
from jax.sharding import PartitionSpec as P

BF = jnp.bfloat16
F32 = jnp.float32
RUN = 64
LOG2E = math.log2(math.e)
VMEM = pl.BlockSpec(memory_space=pltpu.VMEM)
SMALL = pltpu.CompilerParams(vmem_limit_bytes=16 * 1024 * 1024)
NN = (((1,), (0,)), ((), ()))
NT = (((1,), (1,)), ((), ()))
QUICK = pl.CostEstimate(flops=1000, bytes_accessed=1000, transcendentals=0)
COLS = 256


def swapped(block, axis, mask):
    pairs = [(i, i ^ mask) for i in range(lax.axis_size(axis))]
    return lax.ppermute(block, axis, pairs)


def three_parts(x):
    hi = x.astype(BF)
    rest = x - hi.astype(F32)
    mid = rest.astype(BF)
    low = (rest - mid.astype(F32)).astype(BF)
    return [hi, mid, low]


def dot(a, b, dims=NN):
    return lax.dot_general(a, b, dims, preferred_element_type=F32)


def pack_kernel(q_ref, k_ref, v_ref, o_ref, g_ref, lse_ref, pos_ref, x_ref, kv_ref, o_s, lse_s, pos_s, sems):
    rows, width = k_ref.shape
    heads = q_ref.shape[1] // width
    moves = [(lse_ref, lse_s), (pos_ref, pos_s), (o_ref, o_s)]
    for h in range(heads):
        cols = pl.ds(h * width, width)
        moves.append((g_ref.at[:, cols], x_ref.at[pl.ds((heads + h) * rows, rows), :]))
    for h in range(heads):
        cols = pl.ds(h * width, width)
        moves.append((q_ref.at[:, cols], x_ref.at[pl.ds(h * rows, rows), :]))
    moves.append((k_ref, kv_ref.at[pl.ds(0, rows), :]))
    moves.append((v_ref, kv_ref.at[pl.ds(rows, rows), :]))
    copies = [pltpu.make_async_copy(a, b, sems.at[n]) for n, (a, b) in enumerate(moves)]
    for copy in copies:
        copy.start()
    for copy in copies[: 3 + heads]:
        copy.wait()
    ones = jnp.ones((8, width), BF)
    deltas = []
    for h in range(heads):
        g = x_ref[(heads + h) * rows : (heads + h + 1) * rows, :]
        prod = g.astype(F32) * o_s[:, h * width : (h + 1) * width].astype(F32)
        hi = prod.astype(BF)
        low = (prod - hi.astype(F32)).astype(BF)
        deltas.append((dot(ones, hi, NT) + dot(ones, low, NT))[:1])
    run = (pos_s[...] // RUN).astype(F32)
    extra = (
        three_parts(lse_s[...] * LOG2E)
        + three_parts(jnp.concatenate(deltas, axis=0))
        + [run.astype(BF), jnp.zeros((32 - 6 * heads - 1, rows), BF)]
    )
    x_ref[2 * heads * rows :, :] = jnp.concatenate([e.astype(F32) for e in extra], axis=0).astype(BF)
    lane = lax.broadcasted_iota(jnp.int32, run.shape, 1)
    ids = [
        jnp.max(jnp.where(lane == r * RUN, run, 0.0), axis=1, keepdims=True)
        for r in range(rows // RUN)
    ]
    wide = [jnp.broadcast_to(i, (1, width)) for i in ids]
    wide.append(jnp.zeros((16 - len(ids), width), F32))
    kv_ref[2 * rows :, :] = jnp.concatenate(wide, axis=0).astype(BF)
    for copy in copies[3 + heads :]:
        copy.wait()


def blocks_kernel(plan, rows, heads, scale, *refs):
    x_refs = refs[: plan["queries"]]
    refs = refs[plan["queries"] :]
    kv_refs = refs[: plan["kv"]]
    refs = refs[plan["kv"] :]
    acc_refs = refs[: plan["acc"]]
    refs = refs[plan["acc"] :]
    dq_in = None
    if plan["dq_in"]:
        dq_in, refs = refs[0], refs[1:]
    dq_refs, dkv_ref = refs[:-1], refs[-1]
    width = x_refs[0].shape[1]
    hr = heads * rows
    per = rows // RUN
    step = COLS // rows
    slots = plan["slots"]
    rowed = []
    for x_ref in x_refs:
        e = x_ref[2 * hr :, :].astype(F32)
        lse = e[0:heads] + e[heads : 2 * heads] + e[2 * heads : 3 * heads]
        delta = e[3 * heads : 4 * heads] + e[4 * heads : 5 * heads] + e[5 * heads : 6 * heads]
        rowed.append((lse, delta, e[6 * heads : 6 * heads + 1]))
    dqt = [[None] * (hr // COLS) for _ in x_refs]
    for c in range(0, len(slots), 2):
        ks, vs, runs = [], [], []
        for n, start in (s[:2] for s in slots[c : c + 2]):
            ks.append(kv_refs[n][start : start + rows, :])
            vs.append(kv_refs[n][start + rows : start + 2 * rows, :])
            e = kv_refs[n][start + 2 * rows : start + 2 * rows + 16, :].astype(F32)
            runs += [e[r : r + 1] for r in range(per)]
        k = jnp.concatenate(ks, axis=0)
        v = jnp.concatenate(vs, axis=0)
        kt = jnp.concatenate([b.astype(F32).T.astype(BF) for b in ks], axis=1)
        dk = dv = None
        for b, x_ref in enumerate(x_refs):
            lse, delta, run = rowed[b]
            for n in range(hr // COLS):
                q = x_ref[n * COLS : (n + 1) * COLS, :]
                g = x_ref[hr + n * COLS : hr + (n + 1) * COLS, :]
                st = dot(k, q, NT)
                dpt = dot(v, g, NT)
                p_rows, d_rows = [], []
                for r in range(2 * per):
                    sl = slice(r * RUN, (r + 1) * RUN)
                    p_heads, d_heads = [], []
                    for h in range(step):
                        hl = slice(h * rows, (h + 1) * rows)
                        head = n * step + h
                        row = jnp.where(runs[r] <= run, lse[head : head + 1], 1e30)
                        arg = st[sl, hl] * (scale * LOG2E) - row
                        if plan["diagonal"] and b == 0 and c == 0 and r < per:
                            i = lax.broadcasted_iota(jnp.int32, (RUN, rows), 1) - r * RUN
                            j = lax.broadcasted_iota(jnp.int32, (RUN, rows), 0)
                            arg = jnp.where((i >= 0) & (i < j), -1e30, arg)
                        p = jnp.exp2(arg)
                        p_heads.append(p.astype(BF))
                        d_heads.append((p * (dpt[sl, hl] - delta[head : head + 1])).astype(BF))
                    p_rows.append(jnp.concatenate(p_heads, axis=1))
                    d_rows.append(jnp.concatenate(d_heads, axis=1))
                p = jnp.concatenate(p_rows, axis=0)
                d = jnp.concatenate(d_rows, axis=0)
                dv_n, dk_n, dq_n = dot(p, g), dot(d, q), dot(kt, d)
                dv = dv_n if dv is None else dv + dv_n
                dk = dk_n if dk is None else dk + dk_n
                old = dqt[b][n]
                dqt[b][n] = dq_n if old is None else old + dq_n
        for j, slot in enumerate(slots[c : c + 2]):
            dk_j, dv_j = dk[j * rows : (j + 1) * rows], dv[j * rows : (j + 1) * rows]
            if plan["acc"]:
                acc_ref, at = acc_refs[slot[2]], slot[3]
                dk_j += acc_ref[at, :rows, :]
                dv_j += acc_ref[at, rows:, :]
            dkv_ref[c + j, :rows, :] = dk_j.astype(dkv_ref.dtype)
            dkv_ref[c + j, rows:, :] = dv_j.astype(dkv_ref.dtype)
    for b, dq_ref in enumerate(dq_refs):
        for n in range(hr // COLS):
            cols = slice(n * COLS, (n + 1) * COLS)
            total = dqt[b][n] if dq_in is None else dqt[b][n] + dq_in[b, :, cols]
            dq_ref[:, cols] = total.astype(dq_ref.dtype)


def first_kernel(plan, rows, heads, scale, *refs):
    dq_ref = refs[-2]
    dq_refs = [dq_ref.at[b] for b in range(plan["queries"])]
    blocks_kernel(plan, rows, heads, scale, *refs[:-2], *dq_refs, refs[-1])


def blocks_call(xs, kvs, slots, rows, heads, scale, dkv_type, dq_types, acc=(), dq_in=None, diagonal=False):
    sds = jax.ShapeDtypeStruct
    width = xs[0].shape[1]
    hr = heads * rows
    plan = {
        "queries": len(xs),
        "kv": len(kvs),
        "acc": len(acc),
        "dq_in": dq_in is not None,
        "slots": slots,
        "diagonal": diagonal,
    }
    args = (*xs, *kvs, *acc) + (() if dq_in is None else (dq_in,))
    if dq_types is None:
        body = first_kernel
        outs = (sds((len(xs), width, hr), F32),)
    else:
        body = blocks_kernel
        outs = tuple(sds((width, hr), t) for t in dq_types)
    outs += (sds((len(slots), 2 * rows, width), dkv_type),)
    return pl.pallas_call(
        functools.partial(body, plan, rows, heads, scale),
        out_shape=outs,
        in_specs=[VMEM] * len(args),
        out_specs=(VMEM,) * len(outs),
        compiler_params=SMALL,
        cost_estimate=QUICK,
    )(*args)


def add_kernel(own_ref, got_ref, first_ref, *refs):
    first_ref[...] = own_ref[0] + got_ref[0].astype(F32)
    for n, ref in enumerate(refs):
        ref[...] = (own_ref[n + 1] + got_ref[n + 1].astype(F32)).astype(BF)


def final_kernel(rows, heads, scale, n_dq, dq_own, dkv_own, *refs):
    dq_refs, dkv_refs, (gq_ref, gk_ref, gv_ref) = refs[:n_dq], refs[n_dq:-3], refs[-3:]
    dq = dq_own[...]
    for r in dq_refs:
        dq = dq + r[...].astype(F32)
    for h in range(heads):
        part = dq[:, h * rows : (h + 1) * rows]
        gq_ref[:, h * 128 : (h + 1) * 128] = (scale * part).T.astype(BF)
    dkv = dkv_own[...]
    for r in dkv_refs:
        dkv = dkv + r[...].astype(F32)
    gk_ref[...] = (scale * dkv[:rows]).astype(BF)
    gv_ref[...] = dkv[rows:].astype(BF)


def crossed(block, t, other):
    pairs = []
    for i in range(lax.axis_size("inner")):
        chip, core = i // 2, i % 2
        pairs.append((i, 2 * (chip ^ (2 * t + (core if other else 1 - core))) + core))
    return lax.ppermute(block, "inner", pairs)


def on_device(query, key, value, out, grad_out, lse, positions):
    rows, width = key.shape
    heads = query.shape[1] // width
    hr = heads * rows
    scale = width ** (-0.5)
    nq = lax.axis_size("outer")
    nz = lax.axis_size("inner") // 2
    sds = jax.ShapeDtypeStruct
    inputs = (query, key, value, out, grad_out, lse, positions[None, :])
    x, kv = pl.pallas_call(
        pack_kernel,
        out_shape=(sds((2 * hr + 32, width), BF), sds((2 * rows + 16, width), BF)),
        in_specs=[pl.BlockSpec(memory_space=pltpu.HBM)] * 7,
        out_specs=(VMEM, VMEM),
        scratch_shapes=[
            pltpu.VMEM(out.shape, BF),
            pltpu.VMEM(lse.shape, F32),
            pltpu.VMEM((1, rows), jnp.int32),
            pltpu.SemaphoreType.DMA((5 + 2 * heads,)),
        ],
        compiler_params=SMALL,
        cost_estimate=QUICK,
    )(*[pltpu.with_memory_space_constraint(a, pltpu.HBM) for a in inputs])

    sib = swapped(kv, "inner", 1)
    near = swapped(kv, "inner", 2)
    pair = jnp.concatenate([kv, sib], axis=0)
    direct = [crossed(pair, t, False) for t in range(1, nz // 2)]
    xs = [x] + [swapped(x, "outer", s) for s in range(1, nq)]
    early = lax.optimization_barrier((near, *direct, *xs[1:-1]))
    near, direct, xs = early[0], early[1 : nz // 2], [x, *early[nz // 2 :], xs[-1]]
    traded = swapped(jnp.concatenate([near, *direct], axis=0), "inner", 1)

    size = kv.shape[0]
    group_a = [(0, 0), (1, 0)]
    group_b = [(0, 0), (1, 0)]
    for t in range(1, nz // 2):
        group_a += [(t + 1, 0), (t + 1, size)]
        group_b += [(1, (2 * t - 1) * size), (1, 2 * t * size)]
    common = (rows, heads, scale)
    dqs, acc_a = blocks_call(xs[:-1], [kv, sib, *direct], group_a, *common, F32, None, diagonal=True)
    *dqs, acc_b = blocks_call(
        xs[:-1], [near, traded], group_b, *common, F32, [F32] + [BF] * (nq - 2), dq_in=dqs
    )
    arrays = [kv, sib, *direct, near, traded]
    base = len(arrays) - 2
    in_a = [(n, start, 0, i) for i, (n, start) in enumerate(group_a)]
    in_b = [(base + n, start, 1, i) for i, (n, start) in enumerate(group_b)]
    theirs, ours = [in_a[1], in_b[1]], [in_a[0], in_b[0]]
    for t in range(1, nz // 2):
        theirs += [in_b[2 * t], in_a[2 * t + 1]]
        ours += [in_a[2 * t], in_b[2 * t + 1]]
    dq_last, dkv_sib = blocks_call([xs[-1]], arrays, theirs, *common, BF, None, acc=(acc_a, acc_b))
    dkv_got = swapped(dkv_sib, "inner", 1)
    dq_last, dkv_own = blocks_call(
        [xs[-1]], arrays, ours, *common, F32, [BF], acc=(acc_a, acc_b), dq_in=dq_last
    )
    got = [swapped(dq, "outer", s + 1) for s, dq in enumerate([*dqs[1:], dq_last])]
    dkv_own, *send = pl.pallas_call(
        add_kernel,
        out_shape=(sds((2 * rows, width), F32),) + (sds((2 * rows, width), BF),) * (nz - 1),
        in_specs=[VMEM] * 2,
        out_specs=(VMEM,) * nz,
        compiler_params=SMALL,
        cost_estimate=QUICK,
    )(dkv_own, dkv_got)
    dkv = [swapped(send[0], "inner", 2)]
    for t in range(1, nz // 2):
        dkv.append(crossed(send[2 * t - 1], t, False))
        dkv.append(crossed(send[2 * t], t, True))

    return pl.pallas_call(
        functools.partial(final_kernel, rows, heads, scale, len(got)),
        out_shape=(sds((rows, heads * width), BF), sds((rows, width), BF), sds((rows, width), BF)),
        in_specs=[VMEM] * (2 + len(got) + len(dkv)),
        out_specs=(VMEM,) * 3,
        compiler_params=SMALL,
        cost_estimate=QUICK,
    )(dqs[0], dkv_own, *got, *dkv)


def solution(mesh):
    tokens = P(("outer", "inner"), None)
    return jax.shard_map(
        on_device,
        mesh=mesh,
        in_specs=(tokens,) * 5 + (P(None, ("outer", "inner")), P(("outer", "inner"))),
        out_specs=(tokens,) * 3,
        check_vma=False,
    )
```

```python
import functools
import math

import jax
import jax.numpy as jnp
from jax import lax
from jax.experimental import pallas as pl
from jax.experimental.pallas import tpu as pltpu
from jax.sharding import PartitionSpec as P

BF = jnp.bfloat16
F32 = jnp.float32
RUN = 64
LOG2E = math.log2(math.e)
VMEM = pl.BlockSpec(memory_space=pltpu.VMEM)
SMALL = pltpu.CompilerParams(vmem_limit_bytes=16 * 1024 * 1024)
NN = (((1,), (0,)), ((), ()))
NT = (((1,), (1,)), ((), ()))
QUICK = pl.CostEstimate(flops=1000, bytes_accessed=1000, transcendentals=0)
COLS = 512


def swapped(block, axis, mask):
    pairs = [(i, i ^ mask) for i in range(lax.axis_size(axis))]
    return lax.ppermute(block, axis, pairs)


def three_parts(x):
    hi = x.astype(BF)
    rest = x - hi.astype(F32)
    mid = rest.astype(BF)
    low = (rest - mid.astype(F32)).astype(BF)
    return [hi, mid, low]


def dot(a, b, dims=NN):
    return lax.dot_general(a, b, dims, preferred_element_type=F32)


def pack_kernel(q_ref, k_ref, v_ref, o_ref, g_ref, lse_ref, pos_ref, x_ref, kv_ref, o_s, lse_s, pos_s, sems):
    rows, width = k_ref.shape
    heads = q_ref.shape[1] // width
    moves = [(lse_ref, lse_s), (pos_ref, pos_s), (o_ref, o_s)]
    for h in range(heads):
        cols = pl.ds(h * width, width)
        moves.append((g_ref.at[:, cols], x_ref.at[pl.ds((heads + h) * rows, rows), :]))
    for h in range(heads):
        cols = pl.ds(h * width, width)
        moves.append((q_ref.at[:, cols], x_ref.at[pl.ds(h * rows, rows), :]))
    moves.append((k_ref, kv_ref.at[pl.ds(0, rows), :]))
    moves.append((v_ref, kv_ref.at[pl.ds(rows, rows), :]))
    copies = [pltpu.make_async_copy(a, b, sems.at[n]) for n, (a, b) in enumerate(moves)]
    for copy in copies:
        copy.start()
    for copy in copies[: 3 + heads]:
        copy.wait()
    ones = jnp.ones((8, width), BF)
    deltas = []
    for h in range(heads):
        g = x_ref[(heads + h) * rows : (heads + h + 1) * rows, :]
        prod = g.astype(F32) * o_s[:, h * width : (h + 1) * width].astype(F32)
        hi = prod.astype(BF)
        low = (prod - hi.astype(F32)).astype(BF)
        deltas.append((dot(ones, hi, NT) + dot(ones, low, NT))[:1])
    run = (pos_s[...] // RUN).astype(F32)
    extra = (
        three_parts(lse_s[...] * LOG2E)
        + three_parts(jnp.concatenate(deltas, axis=0))
        + [run.astype(BF), jnp.zeros((32 - 6 * heads - 1, rows), BF)]
    )
    x_ref[2 * heads * rows :, :] = jnp.concatenate([e.astype(F32) for e in extra], axis=0).astype(BF)
    lane = lax.broadcasted_iota(jnp.int32, run.shape, 1)
    ids = [
        jnp.max(jnp.where(lane == r * RUN, run, 0.0), axis=1, keepdims=True)
        for r in range(rows // RUN)
    ]
    wide = [jnp.broadcast_to(i, (1, width)) for i in ids]
    wide.append(jnp.zeros((16 - len(ids), width), F32))
    kv_ref[2 * rows :, :] = jnp.concatenate(wide, axis=0).astype(BF)
    for copy in copies[3 + heads :]:
        copy.wait()


def blocks_kernel(plan, rows, heads, scale, *refs):
    x_refs = refs[: plan["queries"]]
    refs = refs[plan["queries"] :]
    kv_refs = refs[: plan["kv"]]
    refs = refs[plan["kv"] :]
    acc_refs = refs[: plan["acc"]]
    refs = refs[plan["acc"] :]
    dq_in = None
    if plan["dq_in"]:
        dq_in, refs = refs[0], refs[1:]
    dq_refs, dkv_ref = refs[:-1], refs[-1]
    width = x_refs[0].shape[1]
    hr = heads * rows
    per = rows // RUN
    step = COLS // rows
    slots = plan["slots"]
    rowed = []
    for x_ref in x_refs:
        e = x_ref[2 * hr :, :].astype(F32)
        lse = e[0:heads] + e[heads : 2 * heads] + e[2 * heads : 3 * heads]
        delta = e[3 * heads : 4 * heads] + e[4 * heads : 5 * heads] + e[5 * heads : 6 * heads]
        rowed.append((lse, delta, e[6 * heads : 6 * heads + 1]))
    dqt = [[None] * (hr // COLS) for _ in x_refs]
    for c in range(0, len(slots), 2):
        ks, vs, runs = [], [], []
        for n, start in (s[:2] for s in slots[c : c + 2]):
            ks.append(kv_refs[n][start : start + rows, :])
            vs.append(kv_refs[n][start + rows : start + 2 * rows, :])
            e = kv_refs[n][start + 2 * rows : start + 2 * rows + 16, :].astype(F32)
            runs += [e[r : r + 1] for r in range(per)]
        k = jnp.concatenate(ks, axis=0)
        v = jnp.concatenate(vs, axis=0)
        kt = jnp.concatenate([b.astype(F32).T.astype(BF) for b in ks], axis=1)
        dk = dv = None
        for b, x_ref in enumerate(x_refs):
            lse, delta, run = rowed[b]
            for n in range(hr // COLS):
                q = x_ref[n * COLS : (n + 1) * COLS, :]
                g = x_ref[hr + n * COLS : hr + (n + 1) * COLS, :]
                st = dot(k, q, NT)
                dpt = dot(v, g, NT)
                p_rows, d_rows = [], []
                for r in range(2 * per):
                    sl = slice(r * RUN, (r + 1) * RUN)
                    p_heads, d_heads = [], []
                    for h in range(step):
                        hl = slice(h * rows, (h + 1) * rows)
                        head = n * step + h
                        row = jnp.where(runs[r] <= run, lse[head : head + 1], 1e30)
                        arg = st[sl, hl] * (scale * LOG2E) - row
                        if plan["diagonal"] and b == 0 and c == 0 and r < per:
                            i = lax.broadcasted_iota(jnp.int32, (RUN, rows), 1) - r * RUN
                            j = lax.broadcasted_iota(jnp.int32, (RUN, rows), 0)
                            arg = jnp.where((i >= 0) & (i < j), -1e30, arg)
                        p = jnp.exp2(arg)
                        p_heads.append(p.astype(BF))
                        d_heads.append((p * (dpt[sl, hl] - delta[head : head + 1])).astype(BF))
                    p_rows.append(jnp.concatenate(p_heads, axis=1))
                    d_rows.append(jnp.concatenate(d_heads, axis=1))
                p = jnp.concatenate(p_rows, axis=0)
                d = jnp.concatenate(d_rows, axis=0)
                dv_n, dk_n, dq_n = dot(p, g), dot(d, q), dot(kt, d)
                dv = dv_n if dv is None else dv + dv_n
                dk = dk_n if dk is None else dk + dk_n
                old = dqt[b][n]
                dqt[b][n] = dq_n if old is None else old + dq_n
        for j, slot in enumerate(slots[c : c + 2]):
            dk_j, dv_j = dk[j * rows : (j + 1) * rows], dv[j * rows : (j + 1) * rows]
            if plan["acc"]:
                acc_ref, at = acc_refs[slot[2]], slot[3]
                dk_j += acc_ref[at, :rows, :]
                dv_j += acc_ref[at, rows:, :]
            dkv_ref[c + j, :rows, :] = dk_j.astype(dkv_ref.dtype)
            dkv_ref[c + j, rows:, :] = dv_j.astype(dkv_ref.dtype)
    for b, dq_ref in enumerate(dq_refs):
        for n in range(hr // COLS):
            cols = slice(n * COLS, (n + 1) * COLS)
            total = dqt[b][n] if dq_in is None else dqt[b][n] + dq_in[b, :, cols]
            dq_ref[:, cols] = total.astype(dq_ref.dtype)


def first_kernel(plan, rows, heads, scale, *refs):
    dq_ref = refs[-2]
    dq_refs = [dq_ref.at[b] for b in range(plan["queries"])]
    blocks_kernel(plan, rows, heads, scale, *refs[:-2], *dq_refs, refs[-1])


def blocks_call(xs, kvs, slots, rows, heads, scale, dkv_type, dq_types, acc=(), dq_in=None, diagonal=False):
    sds = jax.ShapeDtypeStruct
    width = xs[0].shape[1]
    hr = heads * rows
    plan = {
        "queries": len(xs),
        "kv": len(kvs),
        "acc": len(acc),
        "dq_in": dq_in is not None,
        "slots": slots,
        "diagonal": diagonal,
    }
    args = (*xs, *kvs, *acc) + (() if dq_in is None else (dq_in,))
    if dq_types is None:
        body = first_kernel
        outs = (sds((len(xs), width, hr), F32),)
    else:
        body = blocks_kernel
        outs = tuple(sds((width, hr), t) for t in dq_types)
    outs += (sds((len(slots), 2 * rows, width), dkv_type),)
    return pl.pallas_call(
        functools.partial(body, plan, rows, heads, scale),
        out_shape=outs,
        in_specs=[VMEM] * len(args),
        out_specs=(VMEM,) * len(outs),
        compiler_params=SMALL,
        cost_estimate=QUICK,
    )(*args)


def add_kernel(own_ref, got_ref, first_ref, *refs):
    first_ref[...] = own_ref[0] + got_ref[0].astype(F32)
    for n, ref in enumerate(refs):
        ref[...] = (own_ref[n + 1] + got_ref[n + 1].astype(F32)).astype(BF)


def final_kernel(rows, heads, scale, n_dq, dq_own, dkv_own, *refs):
    dq_refs, dkv_refs, (gq_ref, gk_ref, gv_ref) = refs[:n_dq], refs[n_dq:-3], refs[-3:]
    dq = dq_own[...]
    for r in dq_refs:
        dq = dq + r[...].astype(F32)
    for h in range(heads):
        part = dq[:, h * rows : (h + 1) * rows]
        gq_ref[:, h * 128 : (h + 1) * 128] = (scale * part).T.astype(BF)
    dkv = dkv_own[...]
    for r in dkv_refs:
        dkv = dkv + r[...].astype(F32)
    gk_ref[...] = (scale * dkv[:rows]).astype(BF)
    gv_ref[...] = dkv[rows:].astype(BF)


def crossed(block, t, other):
    pairs = []
    for i in range(lax.axis_size("inner")):
        chip, core = i // 2, i % 2
        pairs.append((i, 2 * (chip ^ (2 * t + (core if other else 1 - core))) + core))
    return lax.ppermute(block, "inner", pairs)


def on_device(query, key, value, out, grad_out, lse, positions):
    rows, width = key.shape
    heads = query.shape[1] // width
    hr = heads * rows
    scale = width ** (-0.5)
    nq = lax.axis_size("outer")
    nz = lax.axis_size("inner") // 2
    sds = jax.ShapeDtypeStruct
    inputs = (query, key, value, out, grad_out, lse, positions[None, :])
    x, kv = pl.pallas_call(
        pack_kernel,
        out_shape=(sds((2 * hr + 32, width), BF), sds((2 * rows + 16, width), BF)),
        in_specs=[pl.BlockSpec(memory_space=pltpu.HBM)] * 7,
        out_specs=(VMEM, VMEM),
        scratch_shapes=[
            pltpu.VMEM(out.shape, BF),
            pltpu.VMEM(lse.shape, F32),
            pltpu.VMEM((1, rows), jnp.int32),
            pltpu.SemaphoreType.DMA((5 + 2 * heads,)),
        ],
        compiler_params=SMALL,
        cost_estimate=QUICK,
    )(*[pltpu.with_memory_space_constraint(a, pltpu.HBM) for a in inputs])

    sib = swapped(kv, "inner", 1)
    near = swapped(kv, "inner", 2)
    pair = jnp.concatenate([kv, sib], axis=0)
    direct = [crossed(pair, t, False) for t in range(1, nz // 2)]
    xs = [x] + [swapped(x, "outer", s) for s in range(1, nq)]
    near, *direct = lax.optimization_barrier((near, *direct))
    traded = swapped(jnp.concatenate([near, *direct], axis=0), "inner", 1)

    size = kv.shape[0]
    group_a = [(0, 0), (1, 0)]
    group_b = [(0, 0), (1, 0)]
    for t in range(1, nz // 2):
        group_a += [(t + 1, 0), (t + 1, size)]
        group_b += [(1, (2 * t - 1) * size), (1, 2 * t * size)]
    common = (rows, heads, scale)
    dq_own, acc_a = blocks_call([x], [kv, sib, *direct], group_a, *common, F32, None, diagonal=True)
    dq_own, acc_b = blocks_call([x], [near, traded], group_b, *common, F32, [F32], dq_in=dq_own)
    arrays = [kv, sib, *direct, near, traded]
    base = len(arrays) - 2
    slots = [(n, start, 0, i) for i, (n, start) in enumerate(group_a)]
    slots += [(base + n, start, 1, i) for i, (n, start) in enumerate(group_b)]
    acc = (acc_a, acc_b)
    got = []
    for s in range(1, nq - 1):
        dq, acc = blocks_call([xs[s]], arrays, slots, *common, F32, [BF], acc=acc)
        got.append(swapped(dq, "outer", s))
        slots = [(n, start, 0, i) for i, (n, start, _, _) in enumerate(slots)]
        acc = (acc,)
    in_a, in_b = slots[:nz], slots[nz:]
    theirs, ours = [in_a[1], in_b[1]], [in_a[0], in_b[0]]
    for t in range(1, nz // 2):
        theirs += [in_b[2 * t], in_a[2 * t + 1]]
        ours += [in_a[2 * t], in_b[2 * t + 1]]
    dq_last, dkv_sib = blocks_call([xs[-1]], arrays, theirs, *common, BF, None, acc=acc)
    dkv_got = swapped(dkv_sib, "inner", 1)
    dq_last, dkv_own = blocks_call([xs[-1]], arrays, ours, *common, F32, [BF], acc=acc, dq_in=dq_last)
    got.append(swapped(dq_last, "outer", nq - 1))
    dkv_own, *send = pl.pallas_call(
        add_kernel,
        out_shape=(sds((2 * rows, width), F32),) + (sds((2 * rows, width), BF),) * (nz - 1),
        in_specs=[VMEM] * 2,
        out_specs=(VMEM,) * nz,
        compiler_params=SMALL,
        cost_estimate=QUICK,
    )(dkv_own, dkv_got)
    dkv = [swapped(send[0], "inner", 2)]
    for t in range(1, nz // 2):
        dkv.append(crossed(send[2 * t - 1], t, False))
        dkv.append(crossed(send[2 * t], t, True))

    return pl.pallas_call(
        functools.partial(final_kernel, rows, heads, scale, len(got)),
        out_shape=(sds((rows, heads * width), BF), sds((rows, width), BF), sds((rows, width), BF)),
        in_specs=[VMEM] * (2 + len(got) + len(dkv)),
        out_specs=(VMEM,) * 3,
        compiler_params=SMALL,
        cost_estimate=QUICK,
    )(dq_own, dkv_own, *got, *dkv)


def solution(mesh):
    tokens = P(("outer", "inner"), None)
    return jax.shard_map(
        on_device,
        mesh=mesh,
        in_specs=(tokens,) * 5 + (P(None, ("outer", "inner")), P(("outer", "inner"))),
        out_specs=(tokens,) * 3,
        check_vma=False,
    )
```

```python
import functools
import math

import jax
import jax.numpy as jnp
from jax import lax
from jax.experimental import pallas as pl
from jax.experimental.pallas import tpu as pltpu
from jax.sharding import PartitionSpec as P

BF = jnp.bfloat16
F32 = jnp.float32
RUN = 64
LOG2E = math.log2(math.e)
VMEM = pl.BlockSpec(memory_space=pltpu.VMEM)
SMALL = pltpu.CompilerParams(vmem_limit_bytes=16 * 1024 * 1024)
NN = (((1,), (0,)), ((), ()))
NT = (((1,), (1,)), ((), ()))
QUICK = pl.CostEstimate(flops=1000, bytes_accessed=1000, transcendentals=0)
COLS = 512


def swapped(block, axis, mask):
    pairs = [(i, i ^ mask) for i in range(lax.axis_size(axis))]
    return lax.ppermute(block, axis, pairs)


def three_parts(x):
    hi = x.astype(BF)
    rest = x - hi.astype(F32)
    mid = rest.astype(BF)
    low = (rest - mid.astype(F32)).astype(BF)
    return [hi, mid, low]


def dot(a, b, dims=NN):
    return lax.dot_general(a, b, dims, preferred_element_type=F32)


def pack_kernel(q_ref, k_ref, v_ref, o_ref, g_ref, lse_ref, pos_ref, x_ref, kv_ref, o_s, lse_s, pos_s, sems):
    rows, width = k_ref.shape
    heads = q_ref.shape[1] // width
    moves = [(lse_ref, lse_s), (pos_ref, pos_s), (o_ref, o_s)]
    for h in range(heads):
        cols = pl.ds(h * width, width)
        moves.append((g_ref.at[:, cols], x_ref.at[pl.ds((heads + h) * rows, rows), :]))
    for h in range(heads):
        cols = pl.ds(h * width, width)
        moves.append((q_ref.at[:, cols], x_ref.at[pl.ds(h * rows, rows), :]))
    moves.append((k_ref, kv_ref.at[pl.ds(0, rows), :]))
    moves.append((v_ref, kv_ref.at[pl.ds(rows, rows), :]))
    copies = [pltpu.make_async_copy(a, b, sems.at[n]) for n, (a, b) in enumerate(moves)]
    for copy in copies:
        copy.start()
    for copy in copies[: 3 + heads]:
        copy.wait()
    ones = jnp.ones((8, width), BF)
    deltas = []
    for h in range(heads):
        g = x_ref[(heads + h) * rows : (heads + h + 1) * rows, :]
        prod = g.astype(F32) * o_s[:, h * width : (h + 1) * width].astype(F32)
        hi = prod.astype(BF)
        low = (prod - hi.astype(F32)).astype(BF)
        deltas.append((dot(ones, hi, NT) + dot(ones, low, NT))[:1])
    run = (pos_s[...] // RUN).astype(F32)
    extra = (
        three_parts(lse_s[...] * LOG2E)
        + three_parts(jnp.concatenate(deltas, axis=0))
        + [run.astype(BF), jnp.zeros((32 - 6 * heads - 1, rows), BF)]
    )
    x_ref[2 * heads * rows :, :] = jnp.concatenate([e.astype(F32) for e in extra], axis=0).astype(BF)
    lane = lax.broadcasted_iota(jnp.int32, run.shape, 1)
    ids = [
        jnp.max(jnp.where(lane == r * RUN, run, 0.0), axis=1, keepdims=True)
        for r in range(rows // RUN)
    ]
    wide = [jnp.broadcast_to(i, (1, width)) for i in ids]
    wide.append(jnp.zeros((16 - len(ids), width), F32))
    kv_ref[2 * rows :, :] = jnp.concatenate(wide, axis=0).astype(BF)
    for copy in copies[3 + heads :]:
        copy.wait()


def blocks_kernel(plan, rows, heads, scale, *refs):
    if plan["halves"]:
        x_refs, refs = [refs[:2]], refs[2:]
    else:
        x_refs = [(x_ref, x_ref.at[heads * rows :, :]) for x_ref in refs[: plan["queries"]]]
        refs = refs[plan["queries"] :]
    kv_refs = refs[: plan["kv"]]
    refs = refs[plan["kv"] :]
    acc_refs = refs[: plan["acc"]]
    refs = refs[plan["acc"] :]
    dq_in = None
    if plan["dq_in"]:
        dq_in, refs = refs[0], refs[1:]
    dq_refs, dkv_ref = refs[:-1], refs[-1]
    width = x_refs[0][0].shape[1]
    hr = heads * rows
    per = rows // RUN
    step = COLS // rows
    slots = plan["slots"]
    rowed = []
    for _, g_ref in x_refs:
        e = g_ref[hr:, :].astype(F32)
        lse = e[0:heads] + e[heads : 2 * heads] + e[2 * heads : 3 * heads]
        delta = e[3 * heads : 4 * heads] + e[4 * heads : 5 * heads] + e[5 * heads : 6 * heads]
        rowed.append((lse, delta, e[6 * heads : 6 * heads + 1]))
    dqt = [[None] * (hr // COLS) for _ in x_refs]
    for c in range(0, len(slots), 2):
        ks, vs, runs = [], [], []
        for n, start in (s[:2] for s in slots[c : c + 2]):
            ks.append(kv_refs[n][start : start + rows, :])
            vs.append(kv_refs[n][start + rows : start + 2 * rows, :])
            e = kv_refs[n][start + 2 * rows : start + 2 * rows + 16, :].astype(F32)
            runs += [e[r : r + 1] for r in range(per)]
        k = jnp.concatenate(ks, axis=0)
        v = jnp.concatenate(vs, axis=0)
        kt = jnp.concatenate([b.astype(F32).T.astype(BF) for b in ks], axis=1)
        dk = dv = None
        for b, (q_ref, g_ref) in enumerate(x_refs):
            lse, delta, run = rowed[b]
            for n in range(hr // COLS):
                q = q_ref[n * COLS : (n + 1) * COLS, :]
                g = g_ref[n * COLS : (n + 1) * COLS, :]
                st = dot(k, q, NT)
                dpt = dot(v, g, NT)
                p_rows, d_rows = [], []
                for r in range(2 * per):
                    sl = slice(r * RUN, (r + 1) * RUN)
                    p_heads, d_heads = [], []
                    for h in range(step):
                        hl = slice(h * rows, (h + 1) * rows)
                        head = n * step + h
                        row = jnp.where(runs[r] <= run, lse[head : head + 1], 1e30)
                        arg = st[sl, hl] * (scale * LOG2E) - row
                        if plan["diagonal"] and b == 0 and c == 0 and r < per:
                            i = lax.broadcasted_iota(jnp.int32, (RUN, rows), 1) - r * RUN
                            j = lax.broadcasted_iota(jnp.int32, (RUN, rows), 0)
                            arg = jnp.where((i >= 0) & (i < j), -1e30, arg)
                        p = jnp.exp2(arg)
                        p_heads.append(p.astype(BF))
                        d_heads.append((p * (dpt[sl, hl] - delta[head : head + 1])).astype(BF))
                    p_rows.append(jnp.concatenate(p_heads, axis=1))
                    d_rows.append(jnp.concatenate(d_heads, axis=1))
                p = jnp.concatenate(p_rows, axis=0)
                d = jnp.concatenate(d_rows, axis=0)
                dv_n, dk_n, dq_n = dot(p, g), dot(d, q), dot(kt, d)
                dv = dv_n if dv is None else dv + dv_n
                dk = dk_n if dk is None else dk + dk_n
                old = dqt[b][n]
                dqt[b][n] = dq_n if old is None else old + dq_n
        for j, slot in enumerate(slots[c : c + 2]):
            dk_j, dv_j = dk[j * rows : (j + 1) * rows], dv[j * rows : (j + 1) * rows]
            if plan["acc"]:
                acc_ref, at = acc_refs[slot[2]], slot[3]
                dk_j += acc_ref[at, :rows, :]
                dv_j += acc_ref[at, rows:, :]
            dkv_ref[c + j, :rows, :] = dk_j.astype(dkv_ref.dtype)
            dkv_ref[c + j, rows:, :] = dv_j.astype(dkv_ref.dtype)
    for b, dq_ref in enumerate(dq_refs):
        for n in range(hr // COLS):
            cols = slice(n * COLS, (n + 1) * COLS)
            total = dqt[b][n] if dq_in is None else dqt[b][n] + dq_in[b, :, cols]
            dq_ref[:, cols] = total.astype(dq_ref.dtype)


def first_kernel(plan, rows, heads, scale, *refs):
    dq_ref = refs[-2]
    dq_refs = [dq_ref.at[b] for b in range(plan["queries"])]
    blocks_kernel(plan, rows, heads, scale, *refs[:-2], *dq_refs, refs[-1])


def blocks_call(
    xs, kvs, slots, rows, heads, scale, dkv_type, dq_types, acc=(), dq_in=None, diagonal=False, halves=False
):
    sds = jax.ShapeDtypeStruct
    width = xs[0].shape[1]
    hr = heads * rows
    queries = 1 if halves else len(xs)
    plan = {
        "halves": halves,
        "queries": queries,
        "kv": len(kvs),
        "acc": len(acc),
        "dq_in": dq_in is not None,
        "slots": slots,
        "diagonal": diagonal,
    }
    args = (*xs, *kvs, *acc) + (() if dq_in is None else (dq_in,))
    if dq_types is None:
        body = first_kernel
        outs = (sds((queries, width, hr), F32),)
    else:
        body = blocks_kernel
        outs = tuple(sds((width, hr), t) for t in dq_types)
    outs += (sds((len(slots), 2 * rows, width), dkv_type),)
    return pl.pallas_call(
        functools.partial(body, plan, rows, heads, scale),
        out_shape=outs,
        in_specs=[VMEM] * len(args),
        out_specs=(VMEM,) * len(outs),
        compiler_params=SMALL,
        cost_estimate=QUICK,
    )(*args)


def add_kernel(own_ref, got_ref, first_ref, *refs):
    first_ref[...] = own_ref[0] + got_ref[0].astype(F32)
    for n, ref in enumerate(refs):
        ref[...] = (own_ref[n + 1] + got_ref[n + 1].astype(F32)).astype(BF)


def final_kernel(rows, heads, scale, n_dq, dq_own, dkv_own, *refs):
    dq_refs, dkv_refs, (gq_ref, gk_ref, gv_ref) = refs[:n_dq], refs[n_dq:-3], refs[-3:]
    dq = dq_own[...]
    for r in dq_refs:
        dq = dq + r[...].astype(F32)
    for h in range(heads):
        part = dq[:, h * rows : (h + 1) * rows]
        gq_ref[:, h * 128 : (h + 1) * 128] = (scale * part).T.astype(BF)
    dkv = dkv_own[...]
    for r in dkv_refs:
        dkv = dkv + r[...].astype(F32)
    gk_ref[...] = (scale * dkv[:rows]).astype(BF)
    gv_ref[...] = dkv[rows:].astype(BF)


def crossed(block, t, other):
    pairs = []
    for i in range(lax.axis_size("inner")):
        chip, core = i // 2, i % 2
        pairs.append((i, 2 * (chip ^ (2 * t + (core if other else 1 - core))) + core))
    return lax.ppermute(block, "inner", pairs)


def on_device(query, key, value, out, grad_out, lse, positions):
    rows, width = key.shape
    heads = query.shape[1] // width
    hr = heads * rows
    scale = width ** (-0.5)
    nq = lax.axis_size("outer")
    nz = lax.axis_size("inner") // 2
    sds = jax.ShapeDtypeStruct
    inputs = (query, key, value, out, grad_out, lse, positions[None, :])
    x, kv = pl.pallas_call(
        pack_kernel,
        out_shape=(sds((2 * hr + 32, width), BF), sds((2 * rows + 16, width), BF)),
        in_specs=[pl.BlockSpec(memory_space=pltpu.HBM)] * 7,
        out_specs=(VMEM, VMEM),
        scratch_shapes=[
            pltpu.VMEM(out.shape, BF),
            pltpu.VMEM(lse.shape, F32),
            pltpu.VMEM((1, rows), jnp.int32),
            pltpu.SemaphoreType.DMA((5 + 2 * heads,)),
        ],
        compiler_params=SMALL,
        cost_estimate=QUICK,
    )(*[pltpu.with_memory_space_constraint(a, pltpu.HBM) for a in inputs])

    sib = swapped(kv, "inner", 1)
    near = swapped(kv, "inner", 2)
    pair = jnp.concatenate([kv, sib], axis=0)
    direct = [crossed(pair, t, False) for t in range(1, nz // 2)]
    xs = [swapped(x, "outer", s) for s in range(1, nq - 1)]
    near, *rest = lax.optimization_barrier((near, *direct, *xs))
    direct, xs = rest[: len(direct)], [x, *rest[len(direct) :]]
    one, two = xs[nq - 2], xs[(nq - 1) ^ (nq // 2)]
    corner = [swapped(one[:hr], "outer", 1), swapped(two[hr:], "outer", nq // 2)]
    traded = swapped(jnp.concatenate([near, *direct], axis=0), "inner", 1)

    size = kv.shape[0]
    group_a = [(0, 0), (1, 0)]
    group_b = [(0, 0), (1, 0)]
    for t in range(1, nz // 2):
        group_a += [(t + 1, 0), (t + 1, size)]
        group_b += [(1, (2 * t - 1) * size), (1, 2 * t * size)]
    common = (rows, heads, scale)
    dq_own, acc_a = blocks_call([x], [kv, sib, *direct], group_a, *common, F32, None, diagonal=True)
    dq_own, acc_b = blocks_call([x], [near, traded], group_b, *common, F32, [F32], dq_in=dq_own)
    arrays = [kv, sib, *direct, near, traded]
    base = len(arrays) - 2
    slots = [(n, start, 0, i) for i, (n, start) in enumerate(group_a)]
    slots += [(base + n, start, 1, i) for i, (n, start) in enumerate(group_b)]
    acc = (acc_a, acc_b)
    dqs = []
    for s in range(1, nq - 1):
        dq, acc = blocks_call([xs[s]], arrays, slots, *common, F32, [BF], acc=acc)
        dqs.append(dq)
        slots = [(n, start, 0, i) for i, (n, start, _, _) in enumerate(slots)]
        acc = (acc,)
    in_a, in_b = slots[:nz], slots[nz:]
    theirs, ours = [in_a[1], in_b[1]], [in_a[0], in_b[0]]
    for t in range(1, nz // 2):
        theirs += [in_b[2 * t], in_a[2 * t + 1]]
        ours += [in_a[2 * t], in_b[2 * t + 1]]
    dq_last, dkv_sib = blocks_call(
        corner, arrays, theirs, *common, BF, None, acc=acc, halves=True
    )
    dkv_got = swapped(dkv_sib, "inner", 1)
    dq_last, dkv_own = blocks_call(
        corner, arrays, ours, *common, F32, [BF], acc=acc, dq_in=dq_last, halves=True
    )
    dkv_own, *send = pl.pallas_call(
        add_kernel,
        out_shape=(sds((2 * rows, width), F32),) + (sds((2 * rows, width), BF),) * (nz - 1),
        in_specs=[VMEM] * 2,
        out_specs=(VMEM,) * nz,
        compiler_params=SMALL,
        cost_estimate=QUICK,
    )(dkv_own, dkv_got)
    got = []
    for s, dq in enumerate(dqs + [dq_last]):
        if s:
            dq = lax.optimization_barrier((dq, got[0], send[-1]))[0]
        got.append(swapped(dq, "outer", s + 1))
    dkv = [swapped(send[0], "inner", 2)]
    for t in range(1, nz // 2):
        dkv.append(crossed(send[2 * t - 1], t, False))
        dkv.append(crossed(send[2 * t], t, True))

    return pl.pallas_call(
        functools.partial(final_kernel, rows, heads, scale, len(got)),
        out_shape=(sds((rows, heads * width), BF), sds((rows, width), BF), sds((rows, width), BF)),
        in_specs=[VMEM] * (2 + len(got) + len(dkv)),
        out_specs=(VMEM,) * 3,
        compiler_params=SMALL,
        cost_estimate=QUICK,
    )(dq_own, dkv_own, *got, *dkv)


def solution(mesh):
    tokens = P(("outer", "inner"), None)
    return jax.shard_map(
        on_device,
        mesh=mesh,
        in_specs=(tokens,) * 5 + (P(None, ("outer", "inner")), P(("outer", "inner"))),
        out_specs=(tokens,) * 3,
        check_vma=False,
    )
```

```python
import functools
import math

import jax
import jax.numpy as jnp
from jax import lax
from jax.experimental import pallas as pl
from jax.experimental.pallas import tpu as pltpu
from jax.sharding import PartitionSpec as P

BF = jnp.bfloat16
F32 = jnp.float32
RUN = 64
LOG2E = math.log2(math.e)
VMEM = pl.BlockSpec(memory_space=pltpu.VMEM)
SMALL = pltpu.CompilerParams(vmem_limit_bytes=16 * 1024 * 1024)
NN = (((1,), (0,)), ((), ()))
NT = (((1,), (1,)), ((), ()))
QUICK = pl.CostEstimate(flops=1000, bytes_accessed=1000, transcendentals=0)
COLS = 512


def swapped(block, axis, mask):
    pairs = [(i, i ^ mask) for i in range(lax.axis_size(axis))]
    return lax.ppermute(block, axis, pairs)


def three_parts(x):
    hi = x.astype(BF)
    rest = x - hi.astype(F32)
    mid = rest.astype(BF)
    low = (rest - mid.astype(F32)).astype(BF)
    return [hi, mid, low]


def dot(a, b, dims=NN):
    return lax.dot_general(a, b, dims, preferred_element_type=F32)


def pack_kernel(q_ref, k_ref, v_ref, o_ref, g_ref, lse_ref, pos_ref, x_ref, kv_ref, o_s, lse_s, pos_s, sems):
    rows, width = k_ref.shape
    heads = q_ref.shape[1] // width
    moves = [(lse_ref, lse_s), (pos_ref, pos_s), (o_ref, o_s)]
    for h in range(heads):
        cols = pl.ds(h * width, width)
        moves.append((g_ref.at[:, cols], x_ref.at[pl.ds((heads + h) * rows, rows), :]))
    for h in range(heads):
        cols = pl.ds(h * width, width)
        moves.append((q_ref.at[:, cols], x_ref.at[pl.ds(h * rows, rows), :]))
    moves.append((k_ref, kv_ref.at[pl.ds(0, rows), :]))
    moves.append((v_ref, kv_ref.at[pl.ds(rows, rows), :]))
    copies = [pltpu.make_async_copy(a, b, sems.at[n]) for n, (a, b) in enumerate(moves)]
    for copy in copies:
        copy.start()
    for copy in copies[: 3 + heads]:
        copy.wait()
    ones = jnp.ones((8, width), BF)
    deltas = []
    for h in range(heads):
        g = x_ref[(heads + h) * rows : (heads + h + 1) * rows, :]
        prod = g.astype(F32) * o_s[:, h * width : (h + 1) * width].astype(F32)
        hi = prod.astype(BF)
        low = (prod - hi.astype(F32)).astype(BF)
        deltas.append((dot(ones, hi, NT) + dot(ones, low, NT))[:1])
    run = (pos_s[...] // RUN).astype(F32)
    extra = (
        three_parts(lse_s[...] * LOG2E)
        + three_parts(jnp.concatenate(deltas, axis=0))
        + [run.astype(BF), jnp.zeros((32 - 6 * heads - 1, rows), BF)]
    )
    x_ref[2 * heads * rows :, :] = jnp.concatenate([e.astype(F32) for e in extra], axis=0).astype(BF)
    lane = lax.broadcasted_iota(jnp.int32, run.shape, 1)
    ids = [
        jnp.max(jnp.where(lane == r * RUN, run, 0.0), axis=1, keepdims=True)
        for r in range(rows // RUN)
    ]
    wide = [jnp.broadcast_to(i, (1, width)) for i in ids]
    wide.append(jnp.zeros((16 - len(ids), width), F32))
    kv_ref[2 * rows :, :] = jnp.concatenate(wide, axis=0).astype(BF)
    for copy in copies[3 + heads :]:
        copy.wait()


def blocks_kernel(plan, rows, heads, scale, *refs):
    if plan["halves"]:
        x_refs, refs = [refs[:2]], refs[2:]
    else:
        x_refs = [(x_ref, x_ref.at[heads * rows :, :]) for x_ref in refs[: plan["queries"]]]
        refs = refs[plan["queries"] :]
    kv_refs = refs[: plan["kv"]]
    refs = refs[plan["kv"] :]
    acc_refs = refs[: plan["acc"]]
    refs = refs[plan["acc"] :]
    dq_in = None
    if plan["dq_in"]:
        dq_in, refs = refs[0], refs[1:]
    dq_refs, dkv_ref = refs[:-1], refs[-1]
    width = x_refs[0][0].shape[1]
    hr = heads * rows
    per = rows // RUN
    step = COLS // rows
    slots = plan["slots"]
    rowed = []
    for _, g_ref in x_refs:
        e = g_ref[hr:, :].astype(F32)
        lse = e[0:heads] + e[heads : 2 * heads] + e[2 * heads : 3 * heads]
        delta = e[3 * heads : 4 * heads] + e[4 * heads : 5 * heads] + e[5 * heads : 6 * heads]
        rowed.append((lse, delta, e[6 * heads : 6 * heads + 1]))
    dqt = [[None] * (hr // COLS) for _ in x_refs]
    for c in range(0, len(slots), 2):
        ks, vs, runs = [], [], []
        for n, start in (s[:2] for s in slots[c : c + 2]):
            ks.append(kv_refs[n][start : start + rows, :])
            vs.append(kv_refs[n][start + rows : start + 2 * rows, :])
            e = kv_refs[n][start + 2 * rows : start + 2 * rows + 16, :].astype(F32)
            runs += [e[r : r + 1] for r in range(per)]
        k = jnp.concatenate(ks, axis=0)
        v = jnp.concatenate(vs, axis=0)
        kt = jnp.concatenate([b.astype(F32).T.astype(BF) for b in ks], axis=1)
        dk = dv = None
        for b, (q_ref, g_ref) in enumerate(x_refs):
            lse, delta, run = rowed[b]
            for n in range(hr // COLS):
                q = q_ref[n * COLS : (n + 1) * COLS, :]
                g = g_ref[n * COLS : (n + 1) * COLS, :]
                st = dot(k, q, NT)
                dpt = dot(v, g, NT)
                p_rows, d_rows = [], []
                for r in range(2 * per):
                    sl = slice(r * RUN, (r + 1) * RUN)
                    p_heads, d_heads = [], []
                    for h in range(step):
                        hl = slice(h * rows, (h + 1) * rows)
                        head = n * step + h
                        row = jnp.where(runs[r] <= run, lse[head : head + 1], 1e30)
                        arg = st[sl, hl] * (scale * LOG2E) - row
                        if plan["diagonal"] and b == 0 and c == 0 and r < per:
                            i = lax.broadcasted_iota(jnp.int32, (RUN, rows), 1) - r * RUN
                            j = lax.broadcasted_iota(jnp.int32, (RUN, rows), 0)
                            arg = jnp.where((i >= 0) & (i < j), -1e30, arg)
                        p = jnp.exp2(arg)
                        p_heads.append(p.astype(BF))
                        d_heads.append((p * (dpt[sl, hl] - delta[head : head + 1])).astype(BF))
                    p_rows.append(jnp.concatenate(p_heads, axis=1))
                    d_rows.append(jnp.concatenate(d_heads, axis=1))
                p = jnp.concatenate(p_rows, axis=0)
                d = jnp.concatenate(d_rows, axis=0)
                dv_n, dk_n, dq_n = dot(p, g), dot(d, q), dot(kt, d)
                dv = dv_n if dv is None else dv + dv_n
                dk = dk_n if dk is None else dk + dk_n
                old = dqt[b][n]
                dqt[b][n] = dq_n if old is None else old + dq_n
        for j, slot in enumerate(slots[c : c + 2]):
            dk_j, dv_j = dk[j * rows : (j + 1) * rows], dv[j * rows : (j + 1) * rows]
            if plan["acc"]:
                acc_ref, at = acc_refs[slot[2]], slot[3]
                dk_j += acc_ref[at, :rows, :]
                dv_j += acc_ref[at, rows:, :]
            dkv_ref[c + j, :rows, :] = dk_j.astype(dkv_ref.dtype)
            dkv_ref[c + j, rows:, :] = dv_j.astype(dkv_ref.dtype)
    for b, dq_ref in enumerate(dq_refs):
        for n in range(hr // COLS):
            cols = slice(n * COLS, (n + 1) * COLS)
            total = dqt[b][n] if dq_in is None else dqt[b][n] + dq_in[b, :, cols]
            dq_ref[:, cols] = total.astype(dq_ref.dtype)


def first_kernel(plan, rows, heads, scale, *refs):
    dq_ref = refs[-2]
    dq_refs = [dq_ref.at[b] for b in range(plan["queries"])]
    blocks_kernel(plan, rows, heads, scale, *refs[:-2], *dq_refs, refs[-1])


def blocks_call(
    xs, kvs, slots, rows, heads, scale, dkv_type, dq_types, acc=(), dq_in=None, diagonal=False, halves=False
):
    sds = jax.ShapeDtypeStruct
    width = xs[0].shape[1]
    hr = heads * rows
    queries = 1 if halves else len(xs)
    plan = {
        "halves": halves,
        "queries": queries,
        "kv": len(kvs),
        "acc": len(acc),
        "dq_in": dq_in is not None,
        "slots": slots,
        "diagonal": diagonal,
    }
    args = (*xs, *kvs, *acc) + (() if dq_in is None else (dq_in,))
    if dq_types is None:
        body = first_kernel
        outs = (sds((queries, width, hr), F32),)
    else:
        body = blocks_kernel
        outs = tuple(sds((width, hr), t) for t in dq_types)
    outs += (sds((len(slots), 2 * rows, width), dkv_type),)
    return pl.pallas_call(
        functools.partial(body, plan, rows, heads, scale),
        out_shape=outs,
        in_specs=[VMEM] * len(args),
        out_specs=(VMEM,) * len(outs),
        compiler_params=SMALL,
        cost_estimate=QUICK,
    )(*args)


def add_kernel(own_ref, got_ref, first_ref, *refs):
    first_ref[...] = own_ref[0] + got_ref[0].astype(F32)
    for n, ref in enumerate(refs):
        ref[...] = (own_ref[n + 1] + got_ref[n + 1].astype(F32)).astype(BF)


def sum_kernel(own_ref, *refs):
    total = own_ref[...]
    for ref in refs[:-1]:
        total = total + ref[...].astype(F32)
    refs[-1][...] = total


def final_kernel(rows, heads, scale, dq_own, dkv_ref, *refs):
    dq_refs, (gq_ref, gk_ref, gv_ref) = refs[:-3], refs[-3:]
    dq = dq_own[...]
    for r in dq_refs:
        dq = dq + r[...].astype(F32)
    for h in range(heads):
        part = dq[:, h * rows : (h + 1) * rows]
        gq_ref[:, h * 128 : (h + 1) * 128] = (scale * part).T.astype(BF)
    gk_ref[...] = (scale * dkv_ref[:rows, :]).astype(BF)
    gv_ref[...] = dkv_ref[rows:, :].astype(BF)


def crossed(block, t, other):
    pairs = []
    for i in range(lax.axis_size("inner")):
        chip, core = i // 2, i % 2
        pairs.append((i, 2 * (chip ^ (2 * t + (core if other else 1 - core))) + core))
    return lax.ppermute(block, "inner", pairs)


def on_device(query, key, value, out, grad_out, lse, positions):
    rows, width = key.shape
    heads = query.shape[1] // width
    hr = heads * rows
    scale = width ** (-0.5)
    nq = lax.axis_size("outer")
    nz = lax.axis_size("inner") // 2
    sds = jax.ShapeDtypeStruct
    inputs = (query, key, value, out, grad_out, lse, positions[None, :])
    x, kv = pl.pallas_call(
        pack_kernel,
        out_shape=(sds((2 * hr + 32, width), BF), sds((2 * rows + 16, width), BF)),
        in_specs=[pl.BlockSpec(memory_space=pltpu.HBM)] * 7,
        out_specs=(VMEM, VMEM),
        scratch_shapes=[
            pltpu.VMEM(out.shape, BF),
            pltpu.VMEM(lse.shape, F32),
            pltpu.VMEM((1, rows), jnp.int32),
            pltpu.SemaphoreType.DMA((5 + 2 * heads,)),
        ],
        compiler_params=SMALL,
        cost_estimate=QUICK,
    )(*[pltpu.with_memory_space_constraint(a, pltpu.HBM) for a in inputs])

    sib = swapped(kv, "inner", 1)
    near = swapped(kv, "inner", 2)
    pair = jnp.concatenate([kv, sib], axis=0)
    direct = [crossed(pair, t, False) for t in range(1, nz // 2)]
    xs = [swapped(x, "outer", s) for s in range(1, nq - 1)]
    xs = [x, *lax.optimization_barrier(tuple(xs))]
    halves = [xs[nq - 2][:hr], xs[(nq - 1) ^ (nq // 2)][hr:]]
    corner = [swapped(halves[0], "outer", 1), swapped(halves[1], "outer", nq // 2)]
    near, *direct = lax.optimization_barrier((near, *direct, *halves))[: nz // 2]
    traded = swapped(jnp.concatenate([near, *direct], axis=0), "inner", 1)

    size = kv.shape[0]
    group_a = [(0, 0), (1, 0)]
    group_b = [(0, 0), (1, 0)]
    for t in range(1, nz // 2):
        group_a += [(t + 1, 0), (t + 1, size)]
        group_b += [(1, (2 * t - 1) * size), (1, 2 * t * size)]
    common = (rows, heads, scale)
    dqs, acc_a = blocks_call(xs, [kv, sib, *direct], group_a, *common, F32, None, diagonal=True)
    *dqs, acc_b = blocks_call(
        xs, [near, traded], group_b, *common, F32, [F32] + [BF] * (nq - 2), dq_in=dqs
    )
    arrays = [kv, sib, *direct, near, traded]
    base = len(arrays) - 2
    in_a = [(n, start, 0, i) for i, (n, start) in enumerate(group_a)]
    in_b = [(base + n, start, 1, i) for i, (n, start) in enumerate(group_b)]
    acc = (acc_a, acc_b)
    theirs, ours = [in_a[1], in_b[1]], [in_a[0], in_b[0]]
    for t in range(1, nz // 2):
        theirs += [in_b[2 * t], in_a[2 * t + 1]]
        ours += [in_a[2 * t], in_b[2 * t + 1]]
    dq_last, dkv_sib = blocks_call(
        corner, arrays, theirs, *common, BF, None, acc=acc, halves=True
    )
    dkv_got = swapped(dkv_sib, "inner", 1)
    dq_last, dkv_own = blocks_call(
        corner, arrays, ours, *common, F32, [BF], acc=acc, dq_in=dq_last, halves=True
    )
    dkv_own, *send = pl.pallas_call(
        add_kernel,
        out_shape=(sds((2 * rows, width), F32),) + (sds((2 * rows, width), BF),) * (nz - 1),
        in_specs=[VMEM] * 2,
        out_specs=(VMEM,) * nz,
        compiler_params=SMALL,
        cost_estimate=QUICK,
    )(dkv_own, dkv_got)
    dq_own, *dqs = dqs
    got = [swapped(dq, "outer", s + 1) for s, dq in enumerate(dqs)]
    dq_last, got[0] = lax.optimization_barrier((dq_last, got[0]))
    got.append(swapped(dq_last, "outer", nq - 1))
    dkv = [swapped(send[0], "inner", 2)]
    for t in range(1, nz // 2):
        dkv.append(crossed(send[2 * t - 1], t, False))
        dkv.append(crossed(send[2 * t], t, True))

    dkv_sum = pl.pallas_call(
        sum_kernel,
        out_shape=sds((2 * rows, width), F32),
        in_specs=[VMEM] * nz,
        out_specs=VMEM,
        compiler_params=SMALL,
        cost_estimate=pl.CostEstimate(flops=1_500_000_000, bytes_accessed=1000, transcendentals=0),
    )(dkv_own, *dkv)

    return pl.pallas_call(
        functools.partial(final_kernel, rows, heads, scale),
        out_shape=(sds((rows, heads * width), BF), sds((rows, width), BF), sds((rows, width), BF)),
        in_specs=[VMEM] * (2 + len(got)),
        out_specs=(VMEM,) * 3,
        compiler_params=SMALL,
        cost_estimate=QUICK,
    )(dq_own, dkv_sum, *got)


def solution(mesh):
    tokens = P(("outer", "inner"), None)
    return jax.shard_map(
        on_device,
        mesh=mesh,
        in_specs=(tokens,) * 5 + (P(None, ("outer", "inner")), P(("outer", "inner"))),
        out_specs=(tokens,) * 3,
        check_vma=False,
    )
```

```python
import functools
import math

import jax
import jax.numpy as jnp
from jax import lax
from jax.experimental import pallas as pl
from jax.experimental.pallas import tpu as pltpu
from jax.sharding import PartitionSpec as P

BF = jnp.bfloat16
F32 = jnp.float32
RUN = 64
LOG2E = math.log2(math.e)
VMEM = pl.BlockSpec(memory_space=pltpu.VMEM)
SMALL = pltpu.CompilerParams(vmem_limit_bytes=16 * 1024 * 1024)
NN = (((1,), (0,)), ((), ()))
NT = (((1,), (1,)), ((), ()))
QUICK = pl.CostEstimate(flops=1000, bytes_accessed=1000, transcendentals=0)
COLS = 512


def swapped(block, axis, mask):
    pairs = [(i, i ^ mask) for i in range(lax.axis_size(axis))]
    return lax.ppermute(block, axis, pairs)


def three_parts(x):
    hi = x.astype(BF)
    rest = x - hi.astype(F32)
    mid = rest.astype(BF)
    low = (rest - mid.astype(F32)).astype(BF)
    return [hi, mid, low]


def dot(a, b, dims=NN):
    return lax.dot_general(a, b, dims, preferred_element_type=F32)


def pack_kernel(q_ref, k_ref, v_ref, o_ref, g_ref, lse_ref, pos_ref, x_ref, kv_ref, o_s, lse_s, pos_s, sems):
    rows, width = k_ref.shape
    heads = q_ref.shape[1] // width
    moves = [(lse_ref, lse_s), (pos_ref, pos_s), (o_ref, o_s)]
    for h in range(heads):
        cols = pl.ds(h * width, width)
        moves.append((g_ref.at[:, cols], x_ref.at[pl.ds((heads + h) * rows, rows), :]))
    for h in range(heads):
        cols = pl.ds(h * width, width)
        moves.append((q_ref.at[:, cols], x_ref.at[pl.ds(h * rows, rows), :]))
    moves.append((k_ref, kv_ref.at[pl.ds(0, rows), :]))
    moves.append((v_ref, kv_ref.at[pl.ds(rows, rows), :]))
    copies = [pltpu.make_async_copy(a, b, sems.at[n]) for n, (a, b) in enumerate(moves)]
    for copy in copies:
        copy.start()
    for copy in copies[: 3 + heads]:
        copy.wait()
    ones = jnp.ones((8, width), BF)
    deltas = []
    for h in range(heads):
        g = x_ref[(heads + h) * rows : (heads + h + 1) * rows, :]
        prod = g.astype(F32) * o_s[:, h * width : (h + 1) * width].astype(F32)
        hi = prod.astype(BF)
        low = (prod - hi.astype(F32)).astype(BF)
        deltas.append((dot(ones, hi, NT) + dot(ones, low, NT))[:1])
    run = (pos_s[...] // RUN).astype(F32)
    extra = (
        three_parts(lse_s[...] * LOG2E)
        + three_parts(jnp.concatenate(deltas, axis=0))
        + [run.astype(BF), jnp.zeros((32 - 6 * heads - 1, rows), BF)]
    )
    x_ref[2 * heads * rows :, :] = jnp.concatenate([e.astype(F32) for e in extra], axis=0).astype(BF)
    lane = lax.broadcasted_iota(jnp.int32, run.shape, 1)
    ids = [
        jnp.max(jnp.where(lane == r * RUN, run, 0.0), axis=1, keepdims=True)
        for r in range(rows // RUN)
    ]
    wide = [jnp.broadcast_to(i, (1, width)) for i in ids]
    wide.append(jnp.zeros((16 - len(ids), width), F32))
    kv_ref[2 * rows :, :] = jnp.concatenate(wide, axis=0).astype(BF)
    for copy in copies[3 + heads :]:
        copy.wait()


def blocks_kernel(plan, rows, heads, scale, *refs):
    if plan["halves"]:
        x_refs, refs = [refs[:2]], refs[2:]
    else:
        x_refs = [(x_ref, x_ref.at[heads * rows :, :]) for x_ref in refs[: plan["queries"]]]
        refs = refs[plan["queries"] :]
    kv_refs = refs[: plan["kv"]]
    refs = refs[plan["kv"] :]
    acc_refs = refs[: plan["acc"]]
    refs = refs[plan["acc"] :]
    dq_in = None
    if plan["dq_in"]:
        dq_in, refs = refs[0], refs[1:]
    dq_refs, dkv_ref = refs[:-1], refs[-1]
    width = x_refs[0][0].shape[1]
    hr = heads * rows
    per = rows // RUN
    step = COLS // rows
    slots = plan["slots"]
    rowed = []
    for _, g_ref in x_refs:
        e = g_ref[hr:, :].astype(F32)
        lse = e[0:heads] + e[heads : 2 * heads] + e[2 * heads : 3 * heads]
        delta = e[3 * heads : 4 * heads] + e[4 * heads : 5 * heads] + e[5 * heads : 6 * heads]
        rowed.append((lse, delta, e[6 * heads : 6 * heads + 1]))
    dqt = [[None] * (hr // COLS) for _ in x_refs]
    for c in range(0, len(slots), 2):
        ks, vs, runs = [], [], []
        for n, start in (s[:2] for s in slots[c : c + 2]):
            ks.append(kv_refs[n][start : start + rows, :])
            vs.append(kv_refs[n][start + rows : start + 2 * rows, :])
            e = kv_refs[n][start + 2 * rows : start + 2 * rows + 16, :].astype(F32)
            runs += [e[r : r + 1] for r in range(per)]
        k = jnp.concatenate(ks, axis=0)
        v = jnp.concatenate(vs, axis=0)
        kt = jnp.concatenate([b.astype(F32).T.astype(BF) for b in ks], axis=1)
        dk = dv = None
        for b, (q_ref, g_ref) in enumerate(x_refs):
            lse, delta, run = rowed[b]
            for n in range(hr // COLS):
                q = q_ref[n * COLS : (n + 1) * COLS, :]
                g = g_ref[n * COLS : (n + 1) * COLS, :]
                st = dot(k, q, NT)
                dpt = dot(v, g, NT)
                p_rows, d_rows = [], []
                for r in range(2 * per):
                    sl = slice(r * RUN, (r + 1) * RUN)
                    p_heads, d_heads = [], []
                    for h in range(step):
                        hl = slice(h * rows, (h + 1) * rows)
                        head = n * step + h
                        row = jnp.where(runs[r] <= run, lse[head : head + 1], 1e30)
                        arg = st[sl, hl] * (scale * LOG2E) - row
                        if plan["diagonal"] and b == 0 and c == 0 and r < per:
                            i = lax.broadcasted_iota(jnp.int32, (RUN, rows), 1) - r * RUN
                            j = lax.broadcasted_iota(jnp.int32, (RUN, rows), 0)
                            arg = jnp.where((i >= 0) & (i < j), -1e30, arg)
                        p = jnp.exp2(arg)
                        p_heads.append(p.astype(BF))
                        d_heads.append((p * (dpt[sl, hl] - delta[head : head + 1])).astype(BF))
                    p_rows.append(jnp.concatenate(p_heads, axis=1))
                    d_rows.append(jnp.concatenate(d_heads, axis=1))
                p = jnp.concatenate(p_rows, axis=0)
                d = jnp.concatenate(d_rows, axis=0)
                dv_n, dk_n, dq_n = dot(p, g), dot(d, q), dot(kt, d)
                dv = dv_n if dv is None else dv + dv_n
                dk = dk_n if dk is None else dk + dk_n
                old = dqt[b][n]
                dqt[b][n] = dq_n if old is None else old + dq_n
        for j, slot in enumerate(slots[c : c + 2]):
            dk_j, dv_j = dk[j * rows : (j + 1) * rows], dv[j * rows : (j + 1) * rows]
            if plan["acc"]:
                acc_ref, at = acc_refs[slot[2]], slot[3]
                dk_j += acc_ref[at, :rows, :]
                dv_j += acc_ref[at, rows:, :]
            dkv_ref[c + j, :rows, :] = dk_j.astype(dkv_ref.dtype)
            dkv_ref[c + j, rows:, :] = dv_j.astype(dkv_ref.dtype)
    for b, dq_ref in enumerate(dq_refs):
        for n in range(hr // COLS):
            cols = slice(n * COLS, (n + 1) * COLS)
            total = dqt[b][n] if dq_in is None else dqt[b][n] + dq_in[b, :, cols]
            dq_ref[:, cols] = total.astype(dq_ref.dtype)


def first_kernel(plan, rows, heads, scale, *refs):
    dq_ref = refs[-2]
    dq_refs = [dq_ref.at[b] for b in range(plan["queries"])]
    blocks_kernel(plan, rows, heads, scale, *refs[:-2], *dq_refs, refs[-1])


def blocks_call(
    xs, kvs, slots, rows, heads, scale, dkv_type, dq_types, acc=(), dq_in=None, diagonal=False, halves=False
):
    sds = jax.ShapeDtypeStruct
    width = xs[0].shape[1]
    hr = heads * rows
    queries = 1 if halves else len(xs)
    plan = {
        "halves": halves,
        "queries": queries,
        "kv": len(kvs),
        "acc": len(acc),
        "dq_in": dq_in is not None,
        "slots": slots,
        "diagonal": diagonal,
    }
    args = (*xs, *kvs, *acc) + (() if dq_in is None else (dq_in,))
    if dq_types is None:
        body = first_kernel
        outs = (sds((queries, width, hr), F32),)
    else:
        body = blocks_kernel
        outs = tuple(sds((width, hr), t) for t in dq_types)
    outs += (sds((len(slots), 2 * rows, width), dkv_type),)
    return pl.pallas_call(
        functools.partial(body, plan, rows, heads, scale),
        out_shape=outs,
        in_specs=[VMEM] * len(args),
        out_specs=(VMEM,) * len(outs),
        compiler_params=SMALL,
        cost_estimate=QUICK,
    )(*args)


def add_kernel(own_ref, got_ref, first_ref, *refs):
    first_ref[...] = own_ref[0] + got_ref[0].astype(F32)
    for n, ref in enumerate(refs):
        ref[...] = (own_ref[n + 1] + got_ref[n + 1].astype(F32)).astype(BF)


def sum_kernel(own_ref, *refs):
    total = own_ref[...]
    for ref in refs[:-1]:
        total = total + ref[...].astype(F32)
    refs[-1][...] = total


def final_kernel(rows, heads, scale, dq_own, dkv_ref, *refs):
    dq_refs, (gq_ref, gk_ref, gv_ref) = refs[:-3], refs[-3:]
    dq = dq_own[...]
    for r in dq_refs:
        dq = dq + r[...].astype(F32)
    for h in range(heads):
        part = dq[:, h * rows : (h + 1) * rows]
        gq_ref[:, h * 128 : (h + 1) * 128] = (scale * part).T.astype(BF)
    gk_ref[...] = (scale * dkv_ref[:rows, :]).astype(BF)
    gv_ref[...] = dkv_ref[rows:, :].astype(BF)


def crossed(block, t, other):
    pairs = []
    for i in range(lax.axis_size("inner")):
        chip, core = i // 2, i % 2
        pairs.append((i, 2 * (chip ^ (2 * t + (core if other else 1 - core))) + core))
    return lax.ppermute(block, "inner", pairs)


def on_device(query, key, value, out, grad_out, lse, positions):
    rows, width = key.shape
    heads = query.shape[1] // width
    hr = heads * rows
    scale = width ** (-0.5)
    nq = lax.axis_size("outer")
    nz = lax.axis_size("inner") // 2
    sds = jax.ShapeDtypeStruct
    inputs = (query, key, value, out, grad_out, lse, positions[None, :])
    x, kv = pl.pallas_call(
        pack_kernel,
        out_shape=(sds((2 * hr + 32, width), BF), sds((2 * rows + 16, width), BF)),
        in_specs=[pl.BlockSpec(memory_space=pltpu.HBM)] * 7,
        out_specs=(VMEM, VMEM),
        scratch_shapes=[
            pltpu.VMEM(out.shape, BF),
            pltpu.VMEM(lse.shape, F32),
            pltpu.VMEM((1, rows), jnp.int32),
            pltpu.SemaphoreType.DMA((5 + 2 * heads,)),
        ],
        compiler_params=SMALL,
        cost_estimate=QUICK,
    )(*[pltpu.with_memory_space_constraint(a, pltpu.HBM) for a in inputs])

    sib = swapped(kv, "inner", 1)
    near = swapped(kv, "inner", 2)
    pair = jnp.concatenate([kv, sib], axis=0)
    direct = [crossed(pair, t, False) for t in range(1, nz // 2)]
    xs = [swapped(x, "outer", s) for s in range(1, nq - 1)]
    xs = [x, *lax.optimization_barrier(tuple(xs))]
    halves = [xs[nq - 2][:hr], xs[(nq - 1) ^ (nq // 2)][hr:]]
    corner = [swapped(halves[0], "outer", 1), swapped(halves[1], "outer", nq // 2)]
    near, *direct = lax.optimization_barrier((near, *direct, *halves))[: nz // 2]
    size = kv.shape[0]
    near_sib = swapped(near, "inner", 1)
    traded = [[swapped(p[n : n + size], "inner", 1) for n in (0, size)] for p in direct]

    group_a = [(0, 0), (1, 0)]
    group_b = [(0, 0), (1, 0)]
    for t in range(1, nz // 2):
        group_a += [(t + 1, 0), (t + 1, size)]
        group_b += [(2 * t, 0), (2 * t + 1, 0)]
    far = [near, near_sib, *sum(traded, [])]
    common = (rows, heads, scale)
    dqs, acc_a = blocks_call(xs, [kv, sib, *direct], group_a, *common, F32, None, diagonal=True)
    *dqs, acc_b = blocks_call(
        xs, far, group_b, *common, F32, [F32] + [BF] * (nq - 2), dq_in=dqs
    )
    arrays = [kv, sib, *direct, *far]
    base = 1 + nz // 2
    in_a = [(n, start, 0, i) for i, (n, start) in enumerate(group_a)]
    in_b = [(base + n, start, 1, i) for i, (n, start) in enumerate(group_b)]
    acc = (acc_a, acc_b)
    theirs, ours = [in_a[1], in_b[1]], [in_a[0], in_b[0]]
    for t in range(1, nz // 2):
        theirs += [in_b[2 * t], in_a[2 * t + 1]]
        ours += [in_a[2 * t], in_b[2 * t + 1]]
    dq_last, dkv_sib = blocks_call(
        corner, arrays, theirs, *common, BF, None, acc=acc, halves=True
    )
    dkv_got = swapped(dkv_sib, "inner", 1)
    dq_last, dkv_own = blocks_call(
        corner, arrays, ours, *common, F32, [BF], acc=acc, dq_in=dq_last, halves=True
    )
    dkv_own, *send = pl.pallas_call(
        add_kernel,
        out_shape=(sds((2 * rows, width), F32),) + (sds((2 * rows, width), BF),) * (nz - 1),
        in_specs=[VMEM] * 2,
        out_specs=(VMEM,) * nz,
        compiler_params=SMALL,
        cost_estimate=QUICK,
    )(dkv_own, dkv_got)
    dq_own, *dqs = dqs
    got = [swapped(dq, "outer", s + 1) for s, dq in enumerate(dqs)]
    dq_last, *got = lax.optimization_barrier((dq_last, *got))
    got.append(swapped(dq_last, "outer", nq - 1))
    dkv = []
    for t in range(1, nz // 2):
        dkv.append(crossed(send[2 * t - 1], t, False))
        dkv.append(crossed(send[2 * t], t, True))
    dkv.append(swapped(send[0], "inner", 2))

    dkv_sum = pl.pallas_call(
        sum_kernel,
        out_shape=sds((2 * rows, width), F32),
        in_specs=[VMEM] * nz,
        out_specs=VMEM,
        compiler_params=SMALL,
        cost_estimate=pl.CostEstimate(flops=1_500_000_000, bytes_accessed=1000, transcendentals=0),
    )(dkv_own, *dkv)

    return pl.pallas_call(
        functools.partial(final_kernel, rows, heads, scale),
        out_shape=(sds((rows, heads * width), BF), sds((rows, width), BF), sds((rows, width), BF)),
        in_specs=[VMEM] * (2 + len(got)),
        out_specs=(VMEM,) * 3,
        compiler_params=SMALL,
        cost_estimate=QUICK,
    )(dq_own, dkv_sum, *got)


def solution(mesh):
    tokens = P(("outer", "inner"), None)
    return jax.shard_map(
        on_device,
        mesh=mesh,
        in_specs=(tokens,) * 5 + (P(None, ("outer", "inner")), P(("outer", "inner"))),
        out_specs=(tokens,) * 3,
        check_vma=False,
    )
```

```python
import functools
import math

import jax
import jax.numpy as jnp
from jax import lax
from jax.experimental import pallas as pl
from jax.experimental.pallas import tpu as pltpu
from jax.sharding import PartitionSpec as P

BF = jnp.bfloat16
F32 = jnp.float32
RUN = 64
LOG2E = math.log2(math.e)
VMEM = pl.BlockSpec(memory_space=pltpu.VMEM)
SMALL = pltpu.CompilerParams(vmem_limit_bytes=16 * 1024 * 1024)
NN = (((1,), (0,)), ((), ()))
NT = (((1,), (1,)), ((), ()))
QUICK = pl.CostEstimate(flops=1000, bytes_accessed=1000, transcendentals=0)
COLS = 512


def swapped(block, axis, mask):
    pairs = [(i, i ^ mask) for i in range(lax.axis_size(axis))]
    return lax.ppermute(block, axis, pairs)


def three_parts(x):
    hi = x.astype(BF)
    rest = x - hi.astype(F32)
    mid = rest.astype(BF)
    low = (rest - mid.astype(F32)).astype(BF)
    return [hi, mid, low]


def dot(a, b, dims=NN):
    return lax.dot_general(a, b, dims, preferred_element_type=F32)


def pack_kernel(q_ref, k_ref, v_ref, o_ref, g_ref, lse_ref, pos_ref, x_ref, kv_ref, o_s, lse_s, pos_s, sems):
    rows, width = k_ref.shape
    heads = q_ref.shape[1] // width
    moves = [(lse_ref, lse_s), (pos_ref, pos_s), (o_ref, o_s)]
    for h in range(heads):
        cols = pl.ds(h * width, width)
        moves.append((g_ref.at[:, cols], x_ref.at[pl.ds((heads + h) * rows, rows), :]))
    for h in range(heads):
        cols = pl.ds(h * width, width)
        moves.append((q_ref.at[:, cols], x_ref.at[pl.ds(h * rows, rows), :]))
    moves.append((k_ref, kv_ref.at[pl.ds(0, rows), :]))
    moves.append((v_ref, kv_ref.at[pl.ds(rows, rows), :]))
    copies = [pltpu.make_async_copy(a, b, sems.at[n]) for n, (a, b) in enumerate(moves)]
    for copy in copies:
        copy.start()
    for copy in copies[: 3 + heads]:
        copy.wait()
    ones = jnp.ones((8, width), BF)
    deltas = []
    for h in range(heads):
        g = x_ref[(heads + h) * rows : (heads + h + 1) * rows, :]
        prod = g.astype(F32) * o_s[:, h * width : (h + 1) * width].astype(F32)
        hi = prod.astype(BF)
        low = (prod - hi.astype(F32)).astype(BF)
        deltas.append((dot(ones, hi, NT) + dot(ones, low, NT))[:1])
    run = (pos_s[...] // RUN).astype(F32)
    extra = (
        three_parts(lse_s[...] * LOG2E)
        + three_parts(jnp.concatenate(deltas, axis=0))
        + [run.astype(BF), jnp.zeros((32 - 6 * heads - 1, rows), BF)]
    )
    x_ref[2 * heads * rows :, :] = jnp.concatenate([e.astype(F32) for e in extra], axis=0).astype(BF)
    lane = lax.broadcasted_iota(jnp.int32, run.shape, 1)
    ids = [
        jnp.max(jnp.where(lane == r * RUN, run, 0.0), axis=1, keepdims=True)
        for r in range(rows // RUN)
    ]
    wide = [jnp.broadcast_to(i, (1, width)) for i in ids]
    wide.append(jnp.zeros((16 - len(ids), width), F32))
    kv_ref[2 * rows :, :] = jnp.concatenate(wide, axis=0).astype(BF)
    for copy in copies[3 + heads :]:
        copy.wait()


def blocks_kernel(plan, rows, heads, scale, *refs):
    refs = list(refs)
    x_refs = []
    for parts in plan["parts"]:
        whole = refs.pop(0)
        x_refs.append((whole, whole.at[heads * rows :, :] if parts == 1 else refs.pop(0)))
    kv_refs = [refs.pop(0) for _ in range(plan["kv"])]
    acc_refs = [refs.pop(0) for _ in range(plan["acc"])]
    dq_in = [refs.pop(0) for _ in range(plan["dq_in"])]
    dq_refs, dkv_ref = refs[:-1], refs[-1]
    width = x_refs[0][0].shape[1]
    hr = heads * rows
    per = rows // RUN
    step = COLS // rows
    slots = plan["slots"]
    rowed = []
    for _, g_ref in x_refs:
        e = g_ref[hr:, :].astype(F32)
        lse = e[0:heads] + e[heads : 2 * heads] + e[2 * heads : 3 * heads]
        delta = e[3 * heads : 4 * heads] + e[4 * heads : 5 * heads] + e[5 * heads : 6 * heads]
        rowed.append((lse, delta, e[6 * heads : 6 * heads + 1]))
    dqt = [[None] * (hr // COLS) for _ in x_refs]
    group = 3 if len(slots) == 3 else 2
    for c in range(0, len(slots), group):
        ks, vs, runs = [], [], []
        for n in slots[c : c + group]:
            ks.append(kv_refs[n][:rows, :])
            vs.append(kv_refs[n][rows : 2 * rows, :])
            e = kv_refs[n][2 * rows :, :].astype(F32)
            runs += [e[r : r + 1] for r in range(per)]
        k = jnp.concatenate(ks, axis=0)
        v = jnp.concatenate(vs, axis=0)
        kt = jnp.concatenate([b.astype(F32).T.astype(BF) for b in ks], axis=1)
        dk = dv = None
        for b, (q_ref, g_ref) in enumerate(x_refs):
            lse, delta, run = rowed[b]
            for n in range(hr // COLS):
                q = q_ref[n * COLS : (n + 1) * COLS, :]
                g = g_ref[n * COLS : (n + 1) * COLS, :]
                st = dot(k, q, NT)
                dpt = dot(v, g, NT)
                p_rows, d_rows = [], []
                for r in range(len(runs)):
                    sl = slice(r * RUN, (r + 1) * RUN)
                    p_heads, d_heads = [], []
                    for h in range(step):
                        hl = slice(h * rows, (h + 1) * rows)
                        head = n * step + h
                        row = jnp.where(runs[r] <= run, lse[head : head + 1], 1e30)
                        arg = st[sl, hl] * (scale * LOG2E) - row
                        if plan["diagonal"] and b == 0 and c == 0 and r < per:
                            i = lax.broadcasted_iota(jnp.int32, (RUN, rows), 1) - r * RUN
                            j = lax.broadcasted_iota(jnp.int32, (RUN, rows), 0)
                            arg = jnp.where((i >= 0) & (i < j), -1e30, arg)
                        p = jnp.exp2(arg)
                        p_heads.append(p.astype(BF))
                        d_heads.append((p * (dpt[sl, hl] - delta[head : head + 1])).astype(BF))
                    p_rows.append(jnp.concatenate(p_heads, axis=1))
                    d_rows.append(jnp.concatenate(d_heads, axis=1))
                p = jnp.concatenate(p_rows, axis=0)
                d = jnp.concatenate(d_rows, axis=0)
                dv_n, dk_n, dq_n = dot(p, g), dot(d, q), dot(kt, d)
                dv = dv_n if dv is None else dv + dv_n
                dk = dk_n if dk is None else dk + dk_n
                old = dqt[b][n]
                dqt[b][n] = dq_n if old is None else old + dq_n
        for j, n in enumerate(slots[c : c + group]):
            dk_j, dv_j = dk[j * rows : (j + 1) * rows], dv[j * rows : (j + 1) * rows]
            if plan["acc"]:
                acc_ref, at = acc_refs[plan["at"][n][0]], plan["at"][n][1]
                dk_j += acc_ref[at, :rows, :]
                dv_j += acc_ref[at, rows:, :]
            dkv_ref[c + j, :rows, :] = dk_j.astype(dkv_ref.dtype)
            dkv_ref[c + j, rows:, :] = dv_j.astype(dkv_ref.dtype)
    for b, dq_ref in enumerate(dq_refs):
        for n in range(hr // COLS):
            cols = slice(n * COLS, (n + 1) * COLS)
            total = dqt[b][n] + dq_in[b][:, cols] if dq_in else dqt[b][n]
            dq_ref[:, cols] = total.astype(dq_ref.dtype)


def blocks_call(xs, kvs, slots, rows, heads, scale, dkv_type, dq_type, acc=(), dq_in=(), diagonal=False):
    sds = jax.ShapeDtypeStruct
    width = kvs[0].shape[1]
    xs = [x if isinstance(x, list) else [x] for x in xs]
    slots = list(slots)
    totals = []
    for a, _ in acc:
        if all(a is not t for t in totals):
            totals.append(a)
    at = [([a is t for t in totals].index(True), n) for a, n in acc]
    plan = {
        "parts": [len(x) for x in xs],
        "kv": len(kvs),
        "acc": len(totals),
        "at": at,
        "dq_in": len(dq_in),
        "slots": slots,
        "diagonal": diagonal,
    }
    args = (*sum(xs, []), *kvs, *totals, *dq_in)
    types = dq_type if isinstance(dq_type, list) else [dq_type] * len(xs)
    outs = tuple(sds((width, heads * rows), t) for t in types)
    outs += (sds((len(slots), 2 * rows, width), dkv_type),)
    return pl.pallas_call(
        functools.partial(blocks_kernel, plan, rows, heads, scale),
        out_shape=outs,
        in_specs=[VMEM] * len(args),
        out_specs=(VMEM,) * len(outs),
        compiler_params=SMALL,
        cost_estimate=QUICK,
    )(*args)


def add_kernel(own_ref, got_ref, first_ref, *refs):
    first_ref[...] = own_ref[0] + got_ref[0].astype(F32)
    for n, ref in enumerate(refs):
        ref[...] = (own_ref[n + 1] + got_ref[n + 1].astype(F32)).astype(BF)


def sum_kernel(own_ref, *refs):
    total = own_ref[...]
    for ref in refs[:-1]:
        total = total + ref[...].astype(F32)
    refs[-1][...] = total


def final_kernel(rows, heads, scale, dq_own, dkv_ref, *refs):
    dq_refs, (gq_ref, gk_ref, gv_ref) = refs[:-3], refs[-3:]
    dq = dq_own[...]
    for r in dq_refs:
        dq = dq + r[...].astype(F32)
    for h in range(heads):
        part = dq[:, h * rows : (h + 1) * rows]
        gq_ref[:, h * 128 : (h + 1) * 128] = (scale * part).T.astype(BF)
    gk_ref[...] = (scale * dkv_ref[:rows, :]).astype(BF)
    gv_ref[...] = dkv_ref[rows:, :].astype(BF)


def crossed(block, t, other):
    pairs = []
    for i in range(lax.axis_size("inner")):
        chip, core = i // 2, i % 2
        pairs.append((i, 2 * (chip ^ (2 * t + (core if other else 1 - core))) + core))
    return lax.ppermute(block, "inner", pairs)


def on_device(query, key, value, out, grad_out, lse, positions):
    rows, width = key.shape
    heads = query.shape[1] // width
    hr = heads * rows
    scale = width ** (-0.5)
    nq = lax.axis_size("outer")
    nz = lax.axis_size("inner") // 2
    sds = jax.ShapeDtypeStruct
    inputs = (query, key, value, out, grad_out, lse, positions[None, :])
    x, kv = pl.pallas_call(
        pack_kernel,
        out_shape=(sds((2 * hr + 32, width), BF), sds((2 * rows + 16, width), BF)),
        in_specs=[pl.BlockSpec(memory_space=pltpu.HBM)] * 7,
        out_specs=(VMEM, VMEM),
        scratch_shapes=[
            pltpu.VMEM(out.shape, BF),
            pltpu.VMEM(lse.shape, F32),
            pltpu.VMEM((1, rows), jnp.int32),
            pltpu.SemaphoreType.DMA((5 + 2 * heads,)),
        ],
        compiler_params=SMALL,
        cost_estimate=QUICK,
    )(*[pltpu.with_memory_space_constraint(a, pltpu.HBM) for a in inputs])

    common = (rows, heads, scale)
    sib = swapped(kv, "inner", 1)
    near = swapped(kv, "inner", 2)
    direct = [crossed(block, t, False) for t in range(1, nz // 2) for block in (kv, sib)]
    early = [kv, sib, near]
    dq_own, acc = blocks_call([x], early, range(3), *common, F32, F32, diagonal=True)

    xs = [swapped(x, "outer", s) for s in range(1, nq - 1)]
    dq_own, acc, *xs = lax.optimization_barrier((dq_own, acc, *xs))
    halves = [xs[nq - 3][:hr], xs[((nq - 1) ^ (nq // 2)) - 1][hr:]]
    corner = [swapped(halves[0], "outer", 1), swapped(halves[1], "outer", nq // 2)]
    *dqs, acc = blocks_call(xs, early, range(3), *common, F32, F32, acc=[(acc, n) for n in range(3)])

    *direct, acc = lax.optimization_barrier((*direct, acc))
    traded = [swapped(block, "inner", 1) for block in (near, *direct)]
    xs = [x, *xs]
    n_d, n_t = len(direct), len(traded)
    *dqs, acc_d = blocks_call(xs, direct, range(n_d), *common, F32, F32, dq_in=(dq_own, *dqs))
    types = [F32] + [BF] * (nq - 2)
    dq_own, *dqs, acc_t = blocks_call(xs, traded, range(n_t), *common, F32, types, dq_in=dqs)

    arrays = [*early, *direct, *traded]
    accs = [(a, n) for a, count in ((acc, 3), (acc_d, n_d), (acc_t, n_t)) for n in range(count)]
    theirs, ours = [1, 3 + n_d], [0, 2]
    for t in range(0, n_d, 2):
        theirs += [4 + n_d + t, 3 + t + 1]
        ours += [3 + t, 4 + n_d + t + 1]
    dq_last, dkv_sib = blocks_call([corner], arrays, theirs, *common, BF, F32, acc=accs)
    dkv_got = swapped(dkv_sib, "inner", 1)
    dq_last, dkv_own = blocks_call([corner], arrays, ours, *common, F32, BF, acc=accs, dq_in=[dq_last])
    dkv_own, *send = pl.pallas_call(
        add_kernel,
        out_shape=(sds((2 * rows, width), F32),) + (sds((2 * rows, width), BF),) * (nz - 1),
        in_specs=[VMEM] * 2,
        out_specs=(VMEM,) * nz,
        compiler_params=SMALL,
        cost_estimate=QUICK,
    )(dkv_own, dkv_got)
    got = [swapped(dq, "outer", s + 1) for s, dq in enumerate(dqs)]
    dq_last, *got = lax.optimization_barrier((dq_last, *got))
    got.append(swapped(dq_last, "outer", nq - 1))
    dkv = []
    for t in range(1, nz // 2):
        dkv.append(crossed(send[2 * t - 1], t, False))
        dkv.append(crossed(send[2 * t], t, True))
    dkv.append(swapped(send[0], "inner", 2))

    dkv_sum = pl.pallas_call(
        sum_kernel,
        out_shape=sds((2 * rows, width), F32),
        in_specs=[VMEM] * nz,
        out_specs=VMEM,
        compiler_params=SMALL,
        cost_estimate=pl.CostEstimate(flops=1_500_000_000, bytes_accessed=1000, transcendentals=0),
    )(dkv_own, *dkv)

    return pl.pallas_call(
        functools.partial(final_kernel, rows, heads, scale),
        out_shape=(sds((rows, heads * width), BF), sds((rows, width), BF), sds((rows, width), BF)),
        in_specs=[VMEM] * (2 + len(got)),
        out_specs=(VMEM,) * 3,
        compiler_params=SMALL,
        cost_estimate=QUICK,
    )(dq_own, dkv_sum, *got)


def solution(mesh):
    tokens = P(("outer", "inner"), None)
    return jax.shard_map(
        on_device,
        mesh=mesh,
        in_specs=(tokens,) * 5 + (P(None, ("outer", "inner")), P(("outer", "inner"))),
        out_specs=(tokens,) * 3,
        check_vma=False,
    )
```

```python
import functools
import math

import jax
import jax.numpy as jnp
from jax import lax
from jax.experimental import pallas as pl
from jax.experimental.pallas import tpu as pltpu
from jax.sharding import PartitionSpec as P

BF = jnp.bfloat16
F32 = jnp.float32
RUN = 64
LOG2E = math.log2(math.e)
VMEM = pl.BlockSpec(memory_space=pltpu.VMEM)
SMALL = pltpu.CompilerParams(vmem_limit_bytes=16 * 1024 * 1024)
NN = (((1,), (0,)), ((), ()))
NT = (((1,), (1,)), ((), ()))
QUICK = pl.CostEstimate(flops=1000, bytes_accessed=1000, transcendentals=0)
COLS = 512


def swapped(block, axis, mask):
    pairs = [(i, i ^ mask) for i in range(lax.axis_size(axis))]
    return lax.ppermute(block, axis, pairs)


def three_parts(x):
    hi = x.astype(BF)
    rest = x - hi.astype(F32)
    mid = rest.astype(BF)
    low = (rest - mid.astype(F32)).astype(BF)
    return [hi, mid, low]


def dot(a, b, dims=NN):
    return lax.dot_general(a, b, dims, preferred_element_type=F32)


def pack_kernel(q_ref, k_ref, v_ref, o_ref, g_ref, lse_ref, pos_ref, x_ref, kv_ref, o_s, lse_s, pos_s, sems):
    rows, width = k_ref.shape
    heads = q_ref.shape[1] // width
    moves = [(lse_ref, lse_s), (pos_ref, pos_s), (o_ref, o_s)]
    for h in range(heads):
        cols = pl.ds(h * width, width)
        moves.append((g_ref.at[:, cols], x_ref.at[pl.ds((heads + h) * rows, rows), :]))
    for h in range(heads):
        cols = pl.ds(h * width, width)
        moves.append((q_ref.at[:, cols], x_ref.at[pl.ds(h * rows, rows), :]))
    moves.append((k_ref, kv_ref.at[pl.ds(0, rows), :]))
    moves.append((v_ref, kv_ref.at[pl.ds(rows, rows), :]))
    copies = [pltpu.make_async_copy(a, b, sems.at[n]) for n, (a, b) in enumerate(moves)]
    for copy in copies:
        copy.start()
    for copy in copies[: 3 + heads]:
        copy.wait()
    ones = jnp.ones((8, width), BF)
    deltas = []
    for h in range(heads):
        g = x_ref[(heads + h) * rows : (heads + h + 1) * rows, :]
        prod = g.astype(F32) * o_s[:, h * width : (h + 1) * width].astype(F32)
        hi = prod.astype(BF)
        low = (prod - hi.astype(F32)).astype(BF)
        deltas.append((dot(ones, hi, NT) + dot(ones, low, NT))[:1])
    run = (pos_s[...] // RUN).astype(F32)
    extra = (
        three_parts(lse_s[...] * LOG2E)
        + three_parts(jnp.concatenate(deltas, axis=0))
        + [run.astype(BF), jnp.zeros((32 - 6 * heads - 1, rows), BF)]
    )
    x_ref[2 * heads * rows :, :] = jnp.concatenate([e.astype(F32) for e in extra], axis=0).astype(BF)
    lane = lax.broadcasted_iota(jnp.int32, run.shape, 1)
    ids = [
        jnp.max(jnp.where(lane == r * RUN, run, 0.0), axis=1, keepdims=True)
        for r in range(rows // RUN)
    ]
    wide = [jnp.broadcast_to(i, (1, width)) for i in ids]
    wide.append(jnp.zeros((16 - len(ids), width), F32))
    kv_ref[2 * rows :, :] = jnp.concatenate(wide, axis=0).astype(BF)
    for copy in copies[3 + heads :]:
        copy.wait()


def blocks_kernel(plan, rows, heads, scale, *refs):
    refs = list(refs)
    x_refs = []
    for parts in plan["parts"]:
        whole = refs.pop(0)
        x_refs.append((whole, whole.at[heads * rows :, :] if parts == 1 else refs.pop(0)))
    kv_refs = [refs.pop(0) for _ in range(plan["kv"])]
    acc_refs = [refs.pop(0) for _ in range(plan["acc"])]
    dq_in = [refs.pop(0) for _ in range(plan["dq_in"])]
    dq_refs, dkv_ref = refs[:-1], refs[-1]
    width = x_refs[0][0].shape[1]
    hr = heads * rows
    per = rows // RUN
    step = COLS // rows
    slots = plan["slots"]
    rowed = []
    for _, g_ref in x_refs:
        e = g_ref[hr:, :].astype(F32)
        lse = e[0:heads] + e[heads : 2 * heads] + e[2 * heads : 3 * heads]
        delta = e[3 * heads : 4 * heads] + e[4 * heads : 5 * heads] + e[5 * heads : 6 * heads]
        rowed.append((lse, delta, e[6 * heads : 6 * heads + 1]))
    dqt = [[None] * (hr // COLS) for _ in x_refs]
    group = 3 if len(slots) == 3 else 2
    for c in range(0, len(slots), group):
        ks, vs, runs = [], [], []
        for n in slots[c : c + group]:
            ks.append(kv_refs[n][:rows, :])
            vs.append(kv_refs[n][rows : 2 * rows, :])
            e = kv_refs[n][2 * rows :, :].astype(F32)
            runs += [e[r : r + 1] for r in range(per)]
        k = jnp.concatenate(ks, axis=0)
        v = jnp.concatenate(vs, axis=0)
        kt = jnp.concatenate([b.astype(F32).T.astype(BF) for b in ks], axis=1)
        dk = dv = None
        for b, (q_ref, g_ref) in enumerate(x_refs):
            lse, delta, run = rowed[b]
            for n in range(hr // COLS):
                q = q_ref[n * COLS : (n + 1) * COLS, :]
                g = g_ref[n * COLS : (n + 1) * COLS, :]
                st = dot(k, q, NT)
                dpt = dot(v, g, NT)
                p_rows, d_rows = [], []
                for r in range(len(runs)):
                    sl = slice(r * RUN, (r + 1) * RUN)
                    p_heads, d_heads = [], []
                    for h in range(step):
                        hl = slice(h * rows, (h + 1) * rows)
                        head = n * step + h
                        row = jnp.where(runs[r] <= run, lse[head : head + 1], 1e30)
                        arg = st[sl, hl] * (scale * LOG2E) - row
                        if plan["diagonal"] and b == 0 and c == 0 and r < per:
                            i = lax.broadcasted_iota(jnp.int32, (RUN, rows), 1) - r * RUN
                            j = lax.broadcasted_iota(jnp.int32, (RUN, rows), 0)
                            arg = jnp.where((i >= 0) & (i < j), -1e30, arg)
                        p = jnp.exp2(arg)
                        p_heads.append(p.astype(BF))
                        d_heads.append((p * (dpt[sl, hl] - delta[head : head + 1])).astype(BF))
                    p_rows.append(jnp.concatenate(p_heads, axis=1))
                    d_rows.append(jnp.concatenate(d_heads, axis=1))
                p = jnp.concatenate(p_rows, axis=0)
                d = jnp.concatenate(d_rows, axis=0)
                dv_n, dk_n, dq_n = dot(p, g), dot(d, q), dot(kt, d)
                dv = dv_n if dv is None else dv + dv_n
                dk = dk_n if dk is None else dk + dk_n
                old = dqt[b][n]
                dqt[b][n] = dq_n if old is None else old + dq_n
        for j, n in enumerate(slots[c : c + group]):
            dk_j, dv_j = dk[j * rows : (j + 1) * rows], dv[j * rows : (j + 1) * rows]
            if plan["acc"]:
                acc_ref, at = acc_refs[plan["at"][n][0]], plan["at"][n][1]
                dk_j += acc_ref[at, :rows, :]
                dv_j += acc_ref[at, rows:, :]
            dkv_ref[c + j, :rows, :] = dk_j.astype(dkv_ref.dtype)
            dkv_ref[c + j, rows:, :] = dv_j.astype(dkv_ref.dtype)
    for b, dq_ref in enumerate(dq_refs):
        for n in range(hr // COLS):
            cols = slice(n * COLS, (n + 1) * COLS)
            total = dqt[b][n] + dq_in[b][:, cols] if dq_in else dqt[b][n]
            dq_ref[:, cols] = total.astype(dq_ref.dtype)


def blocks_call(xs, kvs, slots, rows, heads, scale, dkv_type, dq_type, acc=(), dq_in=(), diagonal=False):
    sds = jax.ShapeDtypeStruct
    width = kvs[0].shape[1]
    xs = [x if isinstance(x, list) else [x] for x in xs]
    slots = list(slots)
    totals = []
    for a, _ in acc:
        if all(a is not t for t in totals):
            totals.append(a)
    at = [([a is t for t in totals].index(True), n) for a, n in acc]
    plan = {
        "parts": [len(x) for x in xs],
        "kv": len(kvs),
        "acc": len(totals),
        "at": at,
        "dq_in": len(dq_in),
        "slots": slots,
        "diagonal": diagonal,
    }
    args = (*sum(xs, []), *kvs, *totals, *dq_in)
    types = dq_type if isinstance(dq_type, list) else [dq_type] * len(xs)
    outs = tuple(sds((width, heads * rows), t) for t in types)
    outs += (sds((len(slots), 2 * rows, width), dkv_type),)
    return pl.pallas_call(
        functools.partial(blocks_kernel, plan, rows, heads, scale),
        out_shape=outs,
        in_specs=[VMEM] * len(args),
        out_specs=(VMEM,) * len(outs),
        compiler_params=SMALL,
        cost_estimate=QUICK,
    )(*args)


def add_kernel(own_ref, got_ref, first_ref, *refs):
    first_ref[...] = own_ref[0] + got_ref[0].astype(F32)
    for n, ref in enumerate(refs):
        ref[...] = (own_ref[n + 1] + got_ref[n + 1].astype(F32)).astype(BF)


def sum_kernel(own_ref, *refs):
    total = own_ref[...]
    for ref in refs[:-1]:
        total = total + ref[...].astype(F32)
    refs[-1][...] = total


def final_kernel(rows, heads, scale, dq_own, dkv_ref, near_ref, *refs):
    dq_refs, (gq_ref, gk_ref, gv_ref) = refs[:-3], refs[-3:]
    dq = dq_own[...]
    for r in dq_refs:
        dq = dq + r[...].astype(F32)
    for h in range(heads):
        part = dq[:, h * rows : (h + 1) * rows]
        gq_ref[:, h * 128 : (h + 1) * 128] = (scale * part).T.astype(BF)
    dkv = dkv_ref[...] + near_ref[...].astype(F32)
    gk_ref[...] = (scale * dkv[:rows]).astype(BF)
    gv_ref[...] = dkv[rows:].astype(BF)


def crossed(block, t, other):
    pairs = []
    for i in range(lax.axis_size("inner")):
        chip, core = i // 2, i % 2
        pairs.append((i, 2 * (chip ^ (2 * t + (core if other else 1 - core))) + core))
    return lax.ppermute(block, "inner", pairs)


def on_device(query, key, value, out, grad_out, lse, positions):
    rows, width = key.shape
    heads = query.shape[1] // width
    hr = heads * rows
    scale = width ** (-0.5)
    nq = lax.axis_size("outer")
    nz = lax.axis_size("inner") // 2
    sds = jax.ShapeDtypeStruct
    inputs = (query, key, value, out, grad_out, lse, positions[None, :])
    x, kv = pl.pallas_call(
        pack_kernel,
        out_shape=(sds((2 * hr + 32, width), BF), sds((2 * rows + 16, width), BF)),
        in_specs=[pl.BlockSpec(memory_space=pltpu.HBM)] * 7,
        out_specs=(VMEM, VMEM),
        scratch_shapes=[
            pltpu.VMEM(out.shape, BF),
            pltpu.VMEM(lse.shape, F32),
            pltpu.VMEM((1, rows), jnp.int32),
            pltpu.SemaphoreType.DMA((5 + 2 * heads,)),
        ],
        compiler_params=SMALL,
        cost_estimate=QUICK,
    )(*[pltpu.with_memory_space_constraint(a, pltpu.HBM) for a in inputs])

    common = (rows, heads, scale)
    sib = swapped(kv, "inner", 1)
    near = swapped(kv, "inner", 2)
    direct = [crossed(block, t, False) for t in range(1, nz // 2) for block in (kv, sib)]
    early = [kv, sib, near]
    dq_own, acc = blocks_call([x], early, range(3), *common, F32, F32, diagonal=True)

    xs = [swapped(x, "outer", s) for s in range(1, nq - 1)]
    dq_own, acc, *xs = lax.optimization_barrier((dq_own, acc, *xs))
    halves = [xs[nq - 3][:hr], xs[((nq - 1) ^ (nq // 2)) - 1][hr:]]
    corner = [swapped(halves[0], "outer", 1), swapped(halves[1], "outer", nq // 2)]
    *dqs, acc = blocks_call(xs, early, range(3), *common, F32, F32, acc=[(acc, n) for n in range(3)])

    *fetched, acc = lax.optimization_barrier((near, *direct, acc))
    direct = fetched[1:]
    traded = [swapped(block, "inner", 1) for block in fetched]
    xs = [x, *xs]
    n_d, n_t = len(direct), len(traded)
    *dqs, acc_d = blocks_call(xs, direct, range(n_d), *common, F32, F32, dq_in=(dq_own, *dqs))
    types = [F32] + [BF] * (nq - 2)
    dq_own, *dqs, acc_t = blocks_call(xs, traded, range(n_t), *common, F32, types, dq_in=dqs)

    arrays = [*early, *direct, *traded]
    accs = [(a, n) for a, count in ((acc, 3), (acc_d, n_d), (acc_t, n_t)) for n in range(count)]
    theirs, ours = [1, 3 + n_d], [0, 2]
    for t in range(0, n_d, 2):
        theirs += [4 + n_d + t, 3 + t + 1]
        ours += [3 + t, 4 + n_d + t + 1]
    dq_last, dkv_sib = blocks_call([corner], arrays, theirs, *common, BF, F32, acc=accs)
    dkv_got = swapped(dkv_sib, "inner", 1)
    dq_last, dkv_own = blocks_call([corner], arrays, ours, *common, F32, BF, acc=accs, dq_in=[dq_last])
    dkv_own, *send = pl.pallas_call(
        add_kernel,
        out_shape=(sds((2 * rows, width), F32),) + (sds((2 * rows, width), BF),) * (nz - 1),
        in_specs=[VMEM] * 2,
        out_specs=(VMEM,) * nz,
        compiler_params=SMALL,
        cost_estimate=QUICK,
    )(dkv_own, dkv_got)
    got = [swapped(dq, "outer", s + 1) for s, dq in enumerate(dqs)]
    dq_last, *got = lax.optimization_barrier((dq_last, *got))
    got.append(swapped(dq_last, "outer", nq - 1))
    dkv = []
    for t in range(1, nz // 2):
        dkv.append(crossed(send[2 * t - 1], t, False))
        dkv.append(crossed(send[2 * t], t, True))
    dkv_near = swapped(send[0], "inner", 2)

    dkv_sum = pl.pallas_call(
        sum_kernel,
        out_shape=sds((2 * rows, width), F32),
        in_specs=[VMEM] * (nz - 1),
        out_specs=VMEM,
        compiler_params=SMALL,
        cost_estimate=pl.CostEstimate(flops=1_500_000_000, bytes_accessed=1000, transcendentals=0),
    )(dkv_own, *dkv)

    return pl.pallas_call(
        functools.partial(final_kernel, rows, heads, scale),
        out_shape=(sds((rows, heads * width), BF), sds((rows, width), BF), sds((rows, width), BF)),
        in_specs=[VMEM] * (3 + len(got)),
        out_specs=(VMEM,) * 3,
        compiler_params=SMALL,
        cost_estimate=QUICK,
    )(dq_own, dkv_sum, dkv_near, *got)


def solution(mesh):
    tokens = P(("outer", "inner"), None)
    return jax.shard_map(
        on_device,
        mesh=mesh,
        in_specs=(tokens,) * 5 + (P(None, ("outer", "inner")), P(("outer", "inner"))),
        out_specs=(tokens,) * 3,
        check_vma=False,
    )
```

```python
import functools
import math

import jax
import jax.numpy as jnp
from jax import lax
from jax.experimental import pallas as pl
from jax.experimental.pallas import tpu as pltpu
from jax.sharding import PartitionSpec as P

BF = jnp.bfloat16
F32 = jnp.float32
RUN = 64
LOG2E = math.log2(math.e)
VMEM = pl.BlockSpec(memory_space=pltpu.VMEM)
SMALL = pltpu.CompilerParams(vmem_limit_bytes=16 * 1024 * 1024)
NN = (((1,), (0,)), ((), ()))
NT = (((1,), (1,)), ((), ()))
QUICK = pl.CostEstimate(flops=1000, bytes_accessed=1000, transcendentals=0)
COLS = 512


def swapped(block, axis, mask):
    pairs = [(i, i ^ mask) for i in range(lax.axis_size(axis))]
    return lax.ppermute(block, axis, pairs)


def three_parts(x):
    hi = x.astype(BF)
    rest = x - hi.astype(F32)
    mid = rest.astype(BF)
    low = (rest - mid.astype(F32)).astype(BF)
    return [hi, mid, low]


def dot(a, b, dims=NN):
    return lax.dot_general(a, b, dims, preferred_element_type=F32)


def pack_kernel(q_ref, k_ref, v_ref, o_ref, g_ref, lse_ref, pos_ref, x_ref, kv_ref, o_s, lse_s, pos_s, sems):
    rows, width = k_ref.shape
    heads = q_ref.shape[1] // width
    moves = [(lse_ref, lse_s), (pos_ref, pos_s), (o_ref, o_s)]
    for h in range(heads):
        cols = pl.ds(h * width, width)
        moves.append((g_ref.at[:, cols], x_ref.at[pl.ds((heads + h) * rows, rows), :]))
    for h in range(heads):
        cols = pl.ds(h * width, width)
        moves.append((q_ref.at[:, cols], x_ref.at[pl.ds(h * rows, rows), :]))
    moves.append((k_ref, kv_ref.at[pl.ds(0, rows), :]))
    moves.append((v_ref, kv_ref.at[pl.ds(rows, rows), :]))
    copies = [pltpu.make_async_copy(a, b, sems.at[n]) for n, (a, b) in enumerate(moves)]
    for copy in copies:
        copy.start()
    for copy in copies[: 3 + heads]:
        copy.wait()
    ones = jnp.ones((8, width), BF)
    deltas = []
    for h in range(heads):
        g = x_ref[(heads + h) * rows : (heads + h + 1) * rows, :]
        prod = g.astype(F32) * o_s[:, h * width : (h + 1) * width].astype(F32)
        hi = prod.astype(BF)
        low = (prod - hi.astype(F32)).astype(BF)
        deltas.append((dot(ones, hi, NT) + dot(ones, low, NT))[:1])
    run = (pos_s[...] // RUN).astype(F32)
    extra = (
        three_parts(lse_s[...] * LOG2E)
        + three_parts(jnp.concatenate(deltas, axis=0))
        + [run.astype(BF), jnp.zeros((32 - 6 * heads - 1, rows), BF)]
    )
    x_ref[2 * heads * rows :, :] = jnp.concatenate([e.astype(F32) for e in extra], axis=0).astype(BF)
    lane = lax.broadcasted_iota(jnp.int32, run.shape, 1)
    ids = [
        jnp.max(jnp.where(lane == r * RUN, run, 0.0), axis=1, keepdims=True)
        for r in range(rows // RUN)
    ]
    wide = [jnp.broadcast_to(i, (1, width)) for i in ids]
    wide.append(jnp.zeros((16 - len(ids), width), F32))
    kv_ref[2 * rows :, :] = jnp.concatenate(wide, axis=0).astype(BF)
    for copy in copies[3 + heads :]:
        copy.wait()


def blocks_kernel(plan, rows, heads, scale, *refs):
    refs = list(refs)
    x_refs = []
    for parts in plan["parts"]:
        whole = refs.pop(0)
        x_refs.append((whole, whole.at[heads * rows :, :] if parts == 1 else refs.pop(0)))
    kv_refs = [refs.pop(0) for _ in range(plan["kv"])]
    acc_refs = [refs.pop(0) for _ in range(plan["acc"])]
    dq_in = [refs.pop(0) for _ in range(plan["dq_in"])]
    dq_refs, dkv_ref = refs[:-1], refs[-1]
    width = x_refs[0][0].shape[1]
    hr = heads * rows
    per = rows // RUN
    step = COLS // rows
    slots = plan["slots"]
    rowed = []
    for _, g_ref in x_refs:
        e = g_ref[hr:, :].astype(F32)
        lse = e[0:heads] + e[heads : 2 * heads] + e[2 * heads : 3 * heads]
        delta = e[3 * heads : 4 * heads] + e[4 * heads : 5 * heads] + e[5 * heads : 6 * heads]
        rowed.append((lse, delta, e[6 * heads : 6 * heads + 1]))
    dqt = [[None] * (hr // COLS) for _ in x_refs]
    group = 3 if len(slots) == 3 else 2
    for c in range(0, len(slots), group):
        ks, vs, runs = [], [], []
        for n in slots[c : c + group]:
            ks.append(kv_refs[n][:rows, :])
            vs.append(kv_refs[n][rows : 2 * rows, :])
            e = kv_refs[n][2 * rows :, :].astype(F32)
            runs += [e[r : r + 1] for r in range(per)]
        k = jnp.concatenate(ks, axis=0)
        v = jnp.concatenate(vs, axis=0)
        kt = jnp.concatenate([b.astype(F32).T.astype(BF) for b in ks], axis=1)
        dk = dv = None
        for b, (q_ref, g_ref) in enumerate(x_refs):
            lse, delta, run = rowed[b]
            for n in range(hr // COLS):
                q = q_ref[n * COLS : (n + 1) * COLS, :]
                g = g_ref[n * COLS : (n + 1) * COLS, :]
                st = dot(k, q, NT)
                dpt = dot(v, g, NT)
                p_rows, d_rows = [], []
                for r in range(len(runs)):
                    sl = slice(r * RUN, (r + 1) * RUN)
                    p_heads, d_heads = [], []
                    for h in range(step):
                        hl = slice(h * rows, (h + 1) * rows)
                        head = n * step + h
                        row = jnp.where(runs[r] <= run, lse[head : head + 1], 1e30)
                        arg = st[sl, hl] * (scale * LOG2E) - row
                        if plan["diagonal"] and b == 0 and c == 0 and r < per:
                            i = lax.broadcasted_iota(jnp.int32, (RUN, rows), 1) - r * RUN
                            j = lax.broadcasted_iota(jnp.int32, (RUN, rows), 0)
                            arg = jnp.where((i >= 0) & (i < j), -1e30, arg)
                        p = jnp.exp2(arg)
                        p_heads.append(p.astype(BF))
                        d_heads.append((p * (dpt[sl, hl] - delta[head : head + 1])).astype(BF))
                    p_rows.append(jnp.concatenate(p_heads, axis=1))
                    d_rows.append(jnp.concatenate(d_heads, axis=1))
                p = jnp.concatenate(p_rows, axis=0)
                d = jnp.concatenate(d_rows, axis=0)
                dv_n, dk_n, dq_n = dot(p, g), dot(d, q), dot(kt, d)
                dv = dv_n if dv is None else dv + dv_n
                dk = dk_n if dk is None else dk + dk_n
                old = dqt[b][n]
                dqt[b][n] = dq_n if old is None else old + dq_n
        for j, n in enumerate(slots[c : c + group]):
            dk_j, dv_j = dk[j * rows : (j + 1) * rows], dv[j * rows : (j + 1) * rows]
            if plan["acc"]:
                acc_ref, at = acc_refs[plan["at"][n][0]], plan["at"][n][1]
                dk_j += acc_ref[at, :rows, :]
                dv_j += acc_ref[at, rows:, :]
            dkv_ref[c + j, :rows, :] = dk_j.astype(dkv_ref.dtype)
            dkv_ref[c + j, rows:, :] = dv_j.astype(dkv_ref.dtype)
    for b, dq_ref in enumerate(dq_refs):
        for n in range(hr // COLS):
            cols = slice(n * COLS, (n + 1) * COLS)
            total = dqt[b][n] + dq_in[b][:, cols] if dq_in else dqt[b][n]
            dq_ref[:, cols] = total.astype(dq_ref.dtype)


def blocks_call(xs, kvs, slots, rows, heads, scale, dkv_type, dq_type, acc=(), dq_in=(), diagonal=False):
    sds = jax.ShapeDtypeStruct
    width = kvs[0].shape[1]
    xs = [x if isinstance(x, list) else [x] for x in xs]
    slots = list(slots)
    totals = []
    for a, _ in acc:
        if all(a is not t for t in totals):
            totals.append(a)
    at = [([a is t for t in totals].index(True), n) for a, n in acc]
    plan = {
        "parts": [len(x) for x in xs],
        "kv": len(kvs),
        "acc": len(totals),
        "at": at,
        "dq_in": len(dq_in),
        "slots": slots,
        "diagonal": diagonal,
    }
    args = (*sum(xs, []), *kvs, *totals, *dq_in)
    types = dq_type if isinstance(dq_type, list) else [dq_type] * len(xs)
    outs = tuple(sds((width, heads * rows), t) for t in types)
    outs += (sds((len(slots), 2 * rows, width), dkv_type),)
    return pl.pallas_call(
        functools.partial(blocks_kernel, plan, rows, heads, scale),
        out_shape=outs,
        in_specs=[VMEM] * len(args),
        out_specs=(VMEM,) * len(outs),
        compiler_params=SMALL,
        cost_estimate=QUICK,
    )(*args)


def add_kernel(start, own_ref, got_ref, *refs):
    for n, ref in enumerate(refs):
        ref[...] = (own_ref[n] + got_ref[start + n].astype(F32)).astype(ref.dtype)


def add_call(own, got, start, types):
    return pl.pallas_call(
        functools.partial(add_kernel, start),
        out_shape=tuple(jax.ShapeDtypeStruct(own.shape[1:], t) for t in types),
        in_specs=[VMEM] * 2,
        out_specs=(VMEM,) * len(types),
        compiler_params=SMALL,
        cost_estimate=QUICK,
    )(own, got)


def sum_kernel(own_ref, *refs):
    total = own_ref[...]
    for ref in refs[:-1]:
        total = total + ref[...].astype(F32)
    refs[-1][...] = total


def final_kernel(rows, heads, scale, dq_own, dkv_ref, near_ref, *refs):
    dq_refs, (gq_ref, gk_ref, gv_ref) = refs[:-3], refs[-3:]
    dq = dq_own[...]
    for r in dq_refs:
        dq = dq + r[...].astype(F32)
    for h in range(heads):
        part = dq[:, h * rows : (h + 1) * rows]
        gq_ref[:, h * 128 : (h + 1) * 128] = (scale * part).T.astype(BF)
    dkv = dkv_ref[...] + near_ref[...].astype(F32)
    gk_ref[...] = (scale * dkv[:rows]).astype(BF)
    gv_ref[...] = dkv[rows:].astype(BF)


def crossed(block, t, other):
    pairs = []
    for i in range(lax.axis_size("inner")):
        chip, core = i // 2, i % 2
        pairs.append((i, 2 * (chip ^ (2 * t + (core if other else 1 - core))) + core))
    return lax.ppermute(block, "inner", pairs)


def on_device(query, key, value, out, grad_out, lse, positions):
    rows, width = key.shape
    heads = query.shape[1] // width
    hr = heads * rows
    scale = width ** (-0.5)
    nq = lax.axis_size("outer")
    nz = lax.axis_size("inner") // 2
    sds = jax.ShapeDtypeStruct
    inputs = (query, key, value, out, grad_out, lse, positions[None, :])
    x, kv = pl.pallas_call(
        pack_kernel,
        out_shape=(sds((2 * hr + 32, width), BF), sds((2 * rows + 16, width), BF)),
        in_specs=[pl.BlockSpec(memory_space=pltpu.HBM)] * 7,
        out_specs=(VMEM, VMEM),
        scratch_shapes=[
            pltpu.VMEM(out.shape, BF),
            pltpu.VMEM(lse.shape, F32),
            pltpu.VMEM((1, rows), jnp.int32),
            pltpu.SemaphoreType.DMA((5 + 2 * heads,)),
        ],
        compiler_params=SMALL,
        cost_estimate=QUICK,
    )(*[pltpu.with_memory_space_constraint(a, pltpu.HBM) for a in inputs])

    common = (rows, heads, scale)
    sib = swapped(kv, "inner", 1)
    near = swapped(kv, "inner", 2)
    direct = [crossed(block, t, False) for t in range(1, nz // 2) for block in (kv, sib)]
    early = [kv, sib, near]
    dq_own, acc = blocks_call([x], early, range(3), *common, F32, F32, diagonal=True)

    xs = [swapped(x, "outer", s) for s in range(1, nq - 1)]
    dq_own, acc, *xs = lax.optimization_barrier((dq_own, acc, *xs))
    halves = [xs[nq - 3][:hr], xs[((nq - 1) ^ (nq // 2)) - 1][hr:]]
    corner = [swapped(halves[0], "outer", 1), swapped(halves[1], "outer", nq // 2)]
    *dqs, acc = blocks_call(xs, early, range(3), *common, F32, F32, acc=[(acc, n) for n in range(3)])

    *fetched, acc = lax.optimization_barrier((near, *direct, acc))
    direct = fetched[1:]
    traded = [swapped(block, "inner", 1) for block in fetched]
    xs = [x, *xs]
    n_d, n_t = len(direct), len(traded)
    *dqs, acc_d = blocks_call(xs, direct, range(n_d), *common, F32, F32, dq_in=(dq_own, *dqs))
    types = [F32] + [BF] * (nq - 2)
    dq_own, *dqs, acc_t = blocks_call(xs, traded, range(n_t), *common, F32, types, dq_in=dqs)

    arrays = [*early, *direct, *traded]
    accs = [(a, n) for a, count in ((acc, 3), (acc_d, n_d), (acc_t, n_t)) for n in range(count)]
    theirs, ours = [1, 3 + n_d], [0, 2]
    for t in range(0, n_d, 2):
        theirs += [4 + n_d + t, 3 + t + 1]
        ours += [3 + t, 4 + n_d + t + 1]
    dq_last, dkv_sib = blocks_call([corner], arrays, theirs, *common, BF, F32, acc=accs)
    dkv_got = swapped(dkv_sib, "inner", 1)
    dq_last, dkv_far = blocks_call([corner], arrays, ours[2:], *common, F32, F32, acc=accs, dq_in=[dq_last])
    dq_last, dkv_own = blocks_call([corner], arrays, ours[:2], *common, F32, BF, acc=accs, dq_in=[dq_last])
    far = add_call(dkv_far, dkv_got, 2, [BF] * (nz - 2))
    dkv_own, dkv_near = add_call(dkv_own, dkv_got, 0, [F32, BF])

    got = [swapped(dq, "outer", s + 1) for s, dq in enumerate(dqs)]
    dq_last, got[0] = lax.optimization_barrier((dq_last, got[0]))
    got.append(swapped(dq_last, "outer", nq - 1))
    dkv = []
    for t in range(1, nz // 2):
        dkv.append(crossed(far[2 * t - 2], t, False))
        dkv.append(crossed(far[2 * t - 1], t, True))
    dkv_near = swapped(dkv_near, "inner", 2)

    dkv_sum = pl.pallas_call(
        sum_kernel,
        out_shape=sds((2 * rows, width), F32),
        in_specs=[VMEM] * (nz - 1),
        out_specs=VMEM,
        compiler_params=SMALL,
        cost_estimate=pl.CostEstimate(flops=1_500_000_000, bytes_accessed=1000, transcendentals=0),
    )(dkv_own, *dkv)

    return pl.pallas_call(
        functools.partial(final_kernel, rows, heads, scale),
        out_shape=(sds((rows, heads * width), BF), sds((rows, width), BF), sds((rows, width), BF)),
        in_specs=[VMEM] * (3 + len(got)),
        out_specs=(VMEM,) * 3,
        compiler_params=SMALL,
        cost_estimate=QUICK,
    )(dq_own, dkv_sum, dkv_near, *got)


def solution(mesh):
    tokens = P(("outer", "inner"), None)
    return jax.shard_map(
        on_device,
        mesh=mesh,
        in_specs=(tokens,) * 5 + (P(None, ("outer", "inner")), P(("outer", "inner"))),
        out_specs=(tokens,) * 3,
        check_vma=False,
    )
```

```python
import functools
import math

import jax
import jax.numpy as jnp
from jax import lax
from jax.experimental import pallas as pl
from jax.experimental.pallas import tpu as pltpu
from jax.sharding import PartitionSpec as P

BF = jnp.bfloat16
F32 = jnp.float32
RUN = 64
LOG2E = math.log2(math.e)
VMEM = pl.BlockSpec(memory_space=pltpu.VMEM)
SMALL = pltpu.CompilerParams(vmem_limit_bytes=16 * 1024 * 1024)
NN = (((1,), (0,)), ((), ()))
NT = (((1,), (1,)), ((), ()))
QUICK = pl.CostEstimate(flops=1000, bytes_accessed=1000, transcendentals=0)
COLS = 512


def swapped(block, axis, mask):
    pairs = [(i, i ^ mask) for i in range(lax.axis_size(axis))]
    return lax.ppermute(block, axis, pairs)


def three_parts(x):
    hi = x.astype(BF)
    rest = x - hi.astype(F32)
    mid = rest.astype(BF)
    low = (rest - mid.astype(F32)).astype(BF)
    return [hi, mid, low]


def dot(a, b, dims=NN):
    return lax.dot_general(a, b, dims, preferred_element_type=F32)


def pack_kernel(q_ref, k_ref, v_ref, o_ref, g_ref, lse_ref, pos_ref, x_ref, kv_ref, o_s, lse_s, pos_s, sems):
    rows, width = k_ref.shape
    heads = q_ref.shape[1] // width
    moves = [(lse_ref, lse_s), (pos_ref, pos_s), (o_ref, o_s)]
    for h in range(heads):
        cols = pl.ds(h * width, width)
        moves.append((g_ref.at[:, cols], x_ref.at[pl.ds((heads + h) * rows, rows), :]))
    for h in range(heads):
        cols = pl.ds(h * width, width)
        moves.append((q_ref.at[:, cols], x_ref.at[pl.ds(h * rows, rows), :]))
    moves.append((k_ref, kv_ref.at[pl.ds(0, rows), :]))
    moves.append((v_ref, kv_ref.at[pl.ds(rows, rows), :]))
    copies = [pltpu.make_async_copy(a, b, sems.at[n]) for n, (a, b) in enumerate(moves)]
    for copy in copies:
        copy.start()
    for copy in copies[: 3 + heads]:
        copy.wait()
    ones = jnp.ones((8, width), BF)
    deltas = []
    for h in range(heads):
        g = x_ref[(heads + h) * rows : (heads + h + 1) * rows, :]
        prod = g.astype(F32) * o_s[:, h * width : (h + 1) * width].astype(F32)
        hi = prod.astype(BF)
        low = (prod - hi.astype(F32)).astype(BF)
        deltas.append((dot(ones, hi, NT) + dot(ones, low, NT))[:1])
    run = (pos_s[...] // RUN).astype(F32)
    extra = (
        three_parts(lse_s[...] * LOG2E)
        + three_parts(jnp.concatenate(deltas, axis=0))
        + [run.astype(BF), jnp.zeros((32 - 6 * heads - 1, rows), BF)]
    )
    x_ref[2 * heads * rows :, :] = jnp.concatenate([e.astype(F32) for e in extra], axis=0).astype(BF)
    lane = lax.broadcasted_iota(jnp.int32, run.shape, 1)
    ids = [
        jnp.max(jnp.where(lane == r * RUN, run, 0.0), axis=1, keepdims=True)
        for r in range(rows // RUN)
    ]
    wide = [jnp.broadcast_to(i, (1, width)) for i in ids]
    wide.append(jnp.zeros((16 - len(ids), width), F32))
    kv_ref[2 * rows :, :] = jnp.concatenate(wide, axis=0).astype(BF)
    for copy in copies[3 + heads :]:
        copy.wait()


def blocks_kernel(plan, rows, heads, scale, *refs):
    refs = list(refs)
    x_refs = []
    for parts in plan["parts"]:
        whole = refs.pop(0)
        x_refs.append((whole, whole.at[heads * rows :, :] if parts == 1 else refs.pop(0)))
    kv_refs = [refs.pop(0) for _ in range(plan["kv"])]
    acc_refs = [refs.pop(0) for _ in range(plan["acc"])]
    dq_in = [refs.pop(0) for _ in range(plan["dq_in"])]
    dq_refs, dkv_ref = refs[:-1], refs[-1]
    width = x_refs[0][0].shape[1]
    hr = heads * rows
    per = rows // RUN
    step = COLS // rows
    slots = plan["slots"]
    rowed = []
    for _, g_ref in x_refs:
        e = g_ref[hr:, :].astype(F32)
        lse = e[0:heads] + e[heads : 2 * heads] + e[2 * heads : 3 * heads]
        delta = e[3 * heads : 4 * heads] + e[4 * heads : 5 * heads] + e[5 * heads : 6 * heads]
        rowed.append((lse, delta, e[6 * heads : 6 * heads + 1]))
    dqt = [[None] * (hr // COLS) for _ in x_refs]
    group = 3 if len(slots) == 3 else 2
    for c in range(0, len(slots), group):
        ks, vs, runs = [], [], []
        for n in slots[c : c + group]:
            ks.append(kv_refs[n][:rows, :])
            vs.append(kv_refs[n][rows : 2 * rows, :])
            e = kv_refs[n][2 * rows :, :].astype(F32)
            runs += [e[r : r + 1] for r in range(per)]
        k = jnp.concatenate(ks, axis=0)
        v = jnp.concatenate(vs, axis=0)
        kt = jnp.concatenate([b.astype(F32).T.astype(BF) for b in ks], axis=1)
        dk = dv = None
        for b, (q_ref, g_ref) in enumerate(x_refs):
            lse, delta, run = rowed[b]
            for n in range(hr // COLS):
                q = q_ref[n * COLS : (n + 1) * COLS, :]
                g = g_ref[n * COLS : (n + 1) * COLS, :]
                st = dot(k, q, NT)
                dpt = dot(v, g, NT)
                p_rows, d_rows = [], []
                for r in range(len(runs)):
                    sl = slice(r * RUN, (r + 1) * RUN)
                    p_heads, d_heads = [], []
                    for h in range(step):
                        hl = slice(h * rows, (h + 1) * rows)
                        head = n * step + h
                        row = jnp.where(runs[r] <= run, lse[head : head + 1], 1e30)
                        arg = st[sl, hl] * (scale * LOG2E) - row
                        if plan["diagonal"] and b == 0 and c == 0 and r < per:
                            i = lax.broadcasted_iota(jnp.int32, (RUN, rows), 1) - r * RUN
                            j = lax.broadcasted_iota(jnp.int32, (RUN, rows), 0)
                            arg = jnp.where((i >= 0) & (i < j), -1e30, arg)
                        p = jnp.exp2(arg)
                        p_heads.append(p.astype(BF))
                        d_heads.append((p * (dpt[sl, hl] - delta[head : head + 1])).astype(BF))
                    p_rows.append(jnp.concatenate(p_heads, axis=1))
                    d_rows.append(jnp.concatenate(d_heads, axis=1))
                p = jnp.concatenate(p_rows, axis=0)
                d = jnp.concatenate(d_rows, axis=0)
                dv_n, dk_n, dq_n = dot(p, g), dot(d, q), dot(kt, d)
                dv = dv_n if dv is None else dv + dv_n
                dk = dk_n if dk is None else dk + dk_n
                old = dqt[b][n]
                dqt[b][n] = dq_n if old is None else old + dq_n
        for j, n in enumerate(slots[c : c + group]):
            dk_j, dv_j = dk[j * rows : (j + 1) * rows], dv[j * rows : (j + 1) * rows]
            if plan["acc"]:
                acc_ref, at = acc_refs[plan["at"][n][0]], plan["at"][n][1]
                dk_j += acc_ref[at, :rows, :]
                dv_j += acc_ref[at, rows:, :]
            dkv_ref[c + j, :rows, :] = dk_j.astype(dkv_ref.dtype)
            dkv_ref[c + j, rows:, :] = dv_j.astype(dkv_ref.dtype)
    for b, dq_ref in enumerate(dq_refs):
        for n in range(hr // COLS):
            cols = slice(n * COLS, (n + 1) * COLS)
            total = dqt[b][n] + dq_in[b][:, cols] if dq_in else dqt[b][n]
            dq_ref[:, cols] = total.astype(dq_ref.dtype)


def blocks_call(xs, kvs, slots, rows, heads, scale, dkv_type, dq_type, acc=(), dq_in=(), diagonal=False):
    sds = jax.ShapeDtypeStruct
    width = kvs[0].shape[1]
    xs = [x if isinstance(x, list) else [x] for x in xs]
    slots = list(slots)
    totals = []
    for a, _ in acc:
        if all(a is not t for t in totals):
            totals.append(a)
    at = [([a is t for t in totals].index(True), n) for a, n in acc]
    plan = {
        "parts": [len(x) for x in xs],
        "kv": len(kvs),
        "acc": len(totals),
        "at": at,
        "dq_in": len(dq_in),
        "slots": slots,
        "diagonal": diagonal,
    }
    args = (*sum(xs, []), *kvs, *totals, *dq_in)
    types = dq_type if isinstance(dq_type, list) else [dq_type] * len(xs)
    outs = tuple(sds((width, heads * rows), t) for t in types)
    outs += (sds((len(slots), 2 * rows, width), dkv_type),)
    return pl.pallas_call(
        functools.partial(blocks_kernel, plan, rows, heads, scale),
        out_shape=outs,
        in_specs=[VMEM] * len(args),
        out_specs=(VMEM,) * len(outs),
        compiler_params=SMALL,
        cost_estimate=QUICK,
    )(*args)


def add_kernel(start, own_ref, got_ref, *refs):
    for n, ref in enumerate(refs):
        ref[...] = (own_ref[n] + got_ref[start + n].astype(F32)).astype(ref.dtype)


def add_call(own, got, start, types):
    return pl.pallas_call(
        functools.partial(add_kernel, start),
        out_shape=tuple(jax.ShapeDtypeStruct(own.shape[1:], t) for t in types),
        in_specs=[VMEM] * 2,
        out_specs=(VMEM,) * len(types),
        compiler_params=SMALL,
        cost_estimate=QUICK,
    )(own, got)


def sum_kernel(own_ref, *refs):
    total = own_ref[...]
    for ref in refs[:-1]:
        total = total + ref[...].astype(F32)
    refs[-1][...] = total


def final_kernel(rows, heads, scale, dq_own, dkv_ref, near_ref, *refs):
    dq_refs, (gq_ref, gk_ref, gv_ref) = refs[:-3], refs[-3:]
    dq = dq_own[...]
    for r in dq_refs:
        dq = dq + r[...].astype(F32)
    for h in range(heads):
        part = dq[:, h * rows : (h + 1) * rows]
        gq_ref[:, h * 128 : (h + 1) * 128] = (scale * part).T.astype(BF)
    dkv = dkv_ref[...] + near_ref[...].astype(F32)
    gk_ref[...] = (scale * dkv[:rows]).astype(BF)
    gv_ref[...] = dkv[rows:].astype(BF)


def crossed(block, t, other):
    pairs = []
    for i in range(lax.axis_size("inner")):
        chip, core = i // 2, i % 2
        pairs.append((i, 2 * (chip ^ (2 * t + (core if other else 1 - core))) + core))
    return lax.ppermute(block, "inner", pairs)


def on_device(query, key, value, out, grad_out, lse, positions):
    rows, width = key.shape
    heads = query.shape[1] // width
    hr = heads * rows
    scale = width ** (-0.5)
    nq = lax.axis_size("outer")
    nz = lax.axis_size("inner") // 2
    sds = jax.ShapeDtypeStruct
    inputs = (query, key, value, out, grad_out, lse, positions[None, :])
    x, kv = pl.pallas_call(
        pack_kernel,
        out_shape=(sds((2 * hr + 32, width), BF), sds((2 * rows + 16, width), BF)),
        in_specs=[pl.BlockSpec(memory_space=pltpu.HBM)] * 7,
        out_specs=(VMEM, VMEM),
        scratch_shapes=[
            pltpu.VMEM(out.shape, BF),
            pltpu.VMEM(lse.shape, F32),
            pltpu.VMEM((1, rows), jnp.int32),
            pltpu.SemaphoreType.DMA((5 + 2 * heads,)),
        ],
        compiler_params=SMALL,
        cost_estimate=QUICK,
    )(*[pltpu.with_memory_space_constraint(a, pltpu.HBM) for a in inputs])

    common = (rows, heads, scale)
    sib = swapped(kv, "inner", 1)
    near = swapped(kv, "inner", 2)
    direct = [crossed(block, t, False) for t in range(1, nz // 2) for block in (kv, sib)]
    early = [kv, sib, near]
    dq_own, acc = blocks_call([x], early, range(3), *common, F32, F32, diagonal=True)

    xs = [swapped(x, "outer", s) for s in range(1, nq - 1)]
    dq_own, acc, *xs = lax.optimization_barrier((dq_own, acc, *xs))
    halves = [xs[nq - 3][:hr], xs[((nq - 1) ^ (nq // 2)) - 1][hr:]]
    corner = [swapped(halves[0], "outer", 1), swapped(halves[1], "outer", nq // 2)]
    *dqs, acc = blocks_call(xs, early, range(3), *common, F32, F32, acc=[(acc, n) for n in range(3)])

    *fetched, acc = lax.optimization_barrier((near, *direct, acc))
    direct = fetched[1:]
    traded = [swapped(block, "inner", 1) for block in fetched]
    xs = [x, *xs]
    n_d, n_t = len(direct), len(traded)
    *dqs, acc_d = blocks_call(xs, direct, range(n_d), *common, F32, F32, dq_in=(dq_own, *dqs))
    types = [F32] + [BF] * (nq - 2)
    dq_own, *dqs, acc_t = blocks_call(xs, traded, range(n_t), *common, F32, types, dq_in=dqs)

    arrays = [*early, *direct, *traded]
    accs = [(a, n) for a, count in ((acc, 3), (acc_d, n_d), (acc_t, n_t)) for n in range(count)]
    theirs, ours = [1, 3 + n_d], [0, 2]
    for t in range(0, n_d, 2):
        theirs += [4 + n_d + t, 3 + t + 1]
        ours += [3 + t, 4 + n_d + t + 1]
    dq_last, dkv_sib = blocks_call([corner], arrays, theirs, *common, BF, F32, acc=accs)
    dkv_got = swapped(dkv_sib, "inner", 1)
    dq_last, dkv_far = blocks_call([corner], arrays, ours[2:], *common, F32, F32, acc=accs, dq_in=[dq_last])
    dq_last, dkv_own = blocks_call([corner], arrays, ours[:2], *common, F32, BF, acc=accs, dq_in=[dq_last])
    far = add_call(dkv_far, dkv_got, 2, [BF] * (nz - 2))
    dkv_own, dkv_near = add_call(dkv_own, dkv_got, 0, [F32, BF])

    got = [swapped(dq, "outer", s + 1) for s, dq in enumerate(dqs)]
    dq_last, *got = lax.optimization_barrier((dq_last, *got))
    got.append(swapped(dq_last, "outer", nq - 1))
    dkv = []
    for t in range(1, nz // 2):
        dkv.append(crossed(far[2 * t - 2], t, False))
        dkv.append(crossed(far[2 * t - 1], t, True))
    dkv_near = swapped(dkv_near, "inner", 2)

    dkv_sum = pl.pallas_call(
        sum_kernel,
        out_shape=sds((2 * rows, width), F32),
        in_specs=[VMEM] * (nz - 1),
        out_specs=VMEM,
        compiler_params=SMALL,
        cost_estimate=pl.CostEstimate(flops=1_500_000_000, bytes_accessed=1000, transcendentals=0),
    )(dkv_own, *dkv)

    return pl.pallas_call(
        functools.partial(final_kernel, rows, heads, scale),
        out_shape=(sds((rows, heads * width), BF), sds((rows, width), BF), sds((rows, width), BF)),
        in_specs=[VMEM] * (3 + len(got)),
        out_specs=(VMEM,) * 3,
        compiler_params=SMALL,
        cost_estimate=QUICK,
    )(dq_own, dkv_sum, dkv_near, *got)


def solution(mesh):
    tokens = P(("outer", "inner"), None)
    return jax.shard_map(
        on_device,
        mesh=mesh,
        in_specs=(tokens,) * 5 + (P(None, ("outer", "inner")), P(("outer", "inner"))),
        out_specs=(tokens,) * 3,
        check_vma=False,
    )
```

```python
import functools
import math

import jax
import jax.numpy as jnp
from jax import lax
from jax.experimental import pallas as pl
from jax.experimental.pallas import tpu as pltpu
from jax.sharding import PartitionSpec as P

BF = jnp.bfloat16
F32 = jnp.float32
RUN = 64
LOG2E = math.log2(math.e)
VMEM = pl.BlockSpec(memory_space=pltpu.VMEM)
SMALL = pltpu.CompilerParams(vmem_limit_bytes=16 * 1024 * 1024)
NN = (((1,), (0,)), ((), ()))
NT = (((1,), (1,)), ((), ()))
QUICK = pl.CostEstimate(flops=1000, bytes_accessed=1000, transcendentals=0)
COLS = 512


def swapped(block, axis, mask):
    pairs = [(i, i ^ mask) for i in range(lax.axis_size(axis))]
    return lax.ppermute(block, axis, pairs)


def three_parts(x):
    hi = x.astype(BF)
    rest = x - hi.astype(F32)
    mid = rest.astype(BF)
    low = (rest - mid.astype(F32)).astype(BF)
    return [hi, mid, low]


def dot(a, b, dims=NN):
    return lax.dot_general(a, b, dims, preferred_element_type=F32)


def pack_kernel(q_ref, k_ref, v_ref, o_ref, g_ref, lse_ref, pos_ref, x_ref, kv_ref, o_s, lse_s, pos_s, sems):
    rows, width = k_ref.shape
    heads = q_ref.shape[1] // width
    moves = [(lse_ref, lse_s), (pos_ref, pos_s), (o_ref, o_s)]
    for h in range(heads):
        cols = pl.ds(h * width, width)
        moves.append((g_ref.at[:, cols], x_ref.at[pl.ds((heads + h) * rows, rows), :]))
    for h in range(heads):
        cols = pl.ds(h * width, width)
        moves.append((q_ref.at[:, cols], x_ref.at[pl.ds(h * rows, rows), :]))
    moves.append((k_ref, kv_ref.at[pl.ds(0, rows), :]))
    moves.append((v_ref, kv_ref.at[pl.ds(rows, rows), :]))
    copies = [pltpu.make_async_copy(a, b, sems.at[n]) for n, (a, b) in enumerate(moves)]
    for copy in copies:
        copy.start()
    for copy in copies[: 3 + heads]:
        copy.wait()
    ones = jnp.ones((8, width), BF)
    deltas = []
    for h in range(heads):
        g = x_ref[(heads + h) * rows : (heads + h + 1) * rows, :]
        prod = g.astype(F32) * o_s[:, h * width : (h + 1) * width].astype(F32)
        hi = prod.astype(BF)
        low = (prod - hi.astype(F32)).astype(BF)
        deltas.append((dot(ones, hi, NT) + dot(ones, low, NT))[:1])
    run = (pos_s[...] // RUN).astype(F32)
    extra = (
        three_parts(lse_s[...] * LOG2E)
        + three_parts(jnp.concatenate(deltas, axis=0))
        + [run.astype(BF), jnp.zeros((32 - 6 * heads - 1, rows), BF)]
    )
    x_ref[2 * heads * rows :, :] = jnp.concatenate([e.astype(F32) for e in extra], axis=0).astype(BF)
    lane = lax.broadcasted_iota(jnp.int32, run.shape, 1)
    ids = [
        jnp.max(jnp.where(lane == r * RUN, run, 0.0), axis=1, keepdims=True)
        for r in range(rows // RUN)
    ]
    wide = [jnp.broadcast_to(i, (1, width)) for i in ids]
    wide.append(jnp.zeros((16 - len(ids), width), F32))
    kv_ref[2 * rows :, :] = jnp.concatenate(wide, axis=0).astype(BF)
    for copy in copies[3 + heads :]:
        copy.wait()


def blocks_kernel(plan, rows, heads, scale, *refs):
    refs = list(refs)
    x_refs = []
    for parts in plan["parts"]:
        whole = refs.pop(0)
        x_refs.append((whole, whole.at[heads * rows :, :] if parts == 1 else refs.pop(0)))
    kv_refs = [refs.pop(0) for _ in range(plan["kv"])]
    acc_refs = [refs.pop(0) for _ in range(plan["acc"])]
    dq_in = [refs.pop(0) for _ in range(plan["dq_in"])]
    dq_refs, dkv_ref = refs[:-1], refs[-1]
    width = x_refs[0][0].shape[1]
    hr = heads * rows
    per = rows // RUN
    step = COLS // rows
    slots = plan["slots"]
    rowed = []
    for _, g_ref in x_refs:
        e = g_ref[hr:, :].astype(F32)
        lse = e[0:heads] + e[heads : 2 * heads] + e[2 * heads : 3 * heads]
        delta = e[3 * heads : 4 * heads] + e[4 * heads : 5 * heads] + e[5 * heads : 6 * heads]
        rowed.append((lse, delta, e[6 * heads : 6 * heads + 1]))
    dqt = [[None] * (hr // COLS) for _ in x_refs]
    group = 3 if len(slots) == 3 else 2
    for c in range(0, len(slots), group):
        ks, vs, runs = [], [], []
        for n in slots[c : c + group]:
            ks.append(kv_refs[n][:rows, :])
            vs.append(kv_refs[n][rows : 2 * rows, :])
            e = kv_refs[n][2 * rows :, :].astype(F32)
            runs += [e[r : r + 1] for r in range(per)]
        k = jnp.concatenate(ks, axis=0)
        v = jnp.concatenate(vs, axis=0)
        kt = jnp.concatenate([b.astype(F32).T.astype(BF) for b in ks], axis=1)
        dk = dv = None
        for b, (q_ref, g_ref) in enumerate(x_refs):
            lse, delta, run = rowed[b]
            for n in range(hr // COLS):
                q = q_ref[n * COLS : (n + 1) * COLS, :]
                g = g_ref[n * COLS : (n + 1) * COLS, :]
                st = dot(k, q, NT)
                dpt = dot(v, g, NT)
                p_rows, d_rows = [], []
                for r in range(len(runs)):
                    sl = slice(r * RUN, (r + 1) * RUN)
                    p_heads, d_heads = [], []
                    for h in range(step):
                        hl = slice(h * rows, (h + 1) * rows)
                        head = n * step + h
                        row = jnp.where(runs[r] <= run, lse[head : head + 1], 1e30)
                        arg = st[sl, hl] * (scale * LOG2E) - row
                        if plan["diagonal"] and b == 0 and c == 0 and r < per:
                            i = lax.broadcasted_iota(jnp.int32, (RUN, rows), 1) - r * RUN
                            j = lax.broadcasted_iota(jnp.int32, (RUN, rows), 0)
                            arg = jnp.where((i >= 0) & (i < j), -1e30, arg)
                        p = jnp.exp2(arg)
                        p_heads.append(p.astype(BF))
                        d_heads.append((p * (dpt[sl, hl] - delta[head : head + 1])).astype(BF))
                    p_rows.append(jnp.concatenate(p_heads, axis=1))
                    d_rows.append(jnp.concatenate(d_heads, axis=1))
                p = jnp.concatenate(p_rows, axis=0)
                d = jnp.concatenate(d_rows, axis=0)
                dv_n, dk_n, dq_n = dot(p, g), dot(d, q), dot(kt, d)
                dv = dv_n if dv is None else dv + dv_n
                dk = dk_n if dk is None else dk + dk_n
                old = dqt[b][n]
                dqt[b][n] = dq_n if old is None else old + dq_n
        for j, n in enumerate(slots[c : c + group]):
            dk_j, dv_j = dk[j * rows : (j + 1) * rows], dv[j * rows : (j + 1) * rows]
            if plan["acc"]:
                acc_ref, at = acc_refs[plan["at"][n][0]], plan["at"][n][1]
                dk_j += acc_ref[at, :rows, :]
                dv_j += acc_ref[at, rows:, :]
            dkv_ref[c + j, :rows, :] = dk_j.astype(dkv_ref.dtype)
            dkv_ref[c + j, rows:, :] = dv_j.astype(dkv_ref.dtype)
    for b, dq_ref in enumerate(dq_refs):
        for n in range(hr // COLS):
            cols = slice(n * COLS, (n + 1) * COLS)
            total = dqt[b][n] + dq_in[b][:, cols] if dq_in else dqt[b][n]
            dq_ref[:, cols] = total.astype(dq_ref.dtype)


def blocks_call(xs, kvs, slots, rows, heads, scale, dkv_type, dq_type, acc=(), dq_in=(), diagonal=False):
    sds = jax.ShapeDtypeStruct
    width = kvs[0].shape[1]
    xs = [x if isinstance(x, list) else [x] for x in xs]
    slots = list(slots)
    totals = []
    for a, _ in acc:
        if all(a is not t for t in totals):
            totals.append(a)
    at = [([a is t for t in totals].index(True), n) for a, n in acc]
    plan = {
        "parts": [len(x) for x in xs],
        "kv": len(kvs),
        "acc": len(totals),
        "at": at,
        "dq_in": len(dq_in),
        "slots": slots,
        "diagonal": diagonal,
    }
    args = (*sum(xs, []), *kvs, *totals, *dq_in)
    types = dq_type if isinstance(dq_type, list) else [dq_type] * len(xs)
    outs = tuple(sds((width, heads * rows), t) for t in types)
    outs += (sds((len(slots), 2 * rows, width), dkv_type),)
    return pl.pallas_call(
        functools.partial(blocks_kernel, plan, rows, heads, scale),
        out_shape=outs,
        in_specs=[VMEM] * len(args),
        out_specs=(VMEM,) * len(outs),
        compiler_params=SMALL,
        cost_estimate=QUICK,
    )(*args)


def add_kernel(start, own_ref, got_ref, *refs):
    for n, ref in enumerate(refs):
        ref[...] = (own_ref[n] + got_ref[start + n].astype(F32)).astype(ref.dtype)


def add_call(own, got, start, types):
    return pl.pallas_call(
        functools.partial(add_kernel, start),
        out_shape=tuple(jax.ShapeDtypeStruct(own.shape[1:], t) for t in types),
        in_specs=[VMEM] * 2,
        out_specs=(VMEM,) * len(types),
        compiler_params=SMALL,
        cost_estimate=QUICK,
    )(own, got)


def sum_kernel(own_ref, *refs):
    total = own_ref[...]
    for ref in refs[:-1]:
        total = total + ref[...].astype(F32)
    refs[-1][...] = total


def final_kernel(rows, heads, scale, dq_own, dkv_ref, near_ref, *refs):
    dq_refs, (gq_ref, gk_ref, gv_ref) = refs[:-3], refs[-3:]
    dq = dq_own[...]
    for r in dq_refs:
        dq = dq + r[...].astype(F32)
    for h in range(heads):
        part = dq[:, h * rows : (h + 1) * rows]
        gq_ref[:, h * 128 : (h + 1) * 128] = (scale * part).T.astype(BF)
    dkv = dkv_ref[...] + near_ref[...].astype(F32)
    gk_ref[...] = (scale * dkv[:rows]).astype(BF)
    gv_ref[...] = dkv[rows:].astype(BF)


def crossed(block, t, other):
    pairs = []
    for i in range(lax.axis_size("inner")):
        chip, core = i // 2, i % 2
        pairs.append((i, 2 * (chip ^ (2 * t + (core if other else 1 - core))) + core))
    return lax.ppermute(block, "inner", pairs)


def on_device(query, key, value, out, grad_out, lse, positions):
    rows, width = key.shape
    heads = query.shape[1] // width
    hr = heads * rows
    scale = width ** (-0.5)
    nq = lax.axis_size("outer")
    nz = lax.axis_size("inner") // 2
    sds = jax.ShapeDtypeStruct
    inputs = (query, key, value, out, grad_out, lse, positions[None, :])
    x, kv = pl.pallas_call(
        pack_kernel,
        out_shape=(sds((2 * hr + 32, width), BF), sds((2 * rows + 16, width), BF)),
        in_specs=[pl.BlockSpec(memory_space=pltpu.HBM)] * 7,
        out_specs=(VMEM, VMEM),
        scratch_shapes=[
            pltpu.VMEM(out.shape, BF),
            pltpu.VMEM(lse.shape, F32),
            pltpu.VMEM((1, rows), jnp.int32),
            pltpu.SemaphoreType.DMA((5 + 2 * heads,)),
        ],
        compiler_params=SMALL,
        cost_estimate=QUICK,
    )(*[pltpu.with_memory_space_constraint(a, pltpu.HBM) for a in inputs])

    common = (rows, heads, scale)
    sib = swapped(kv, "inner", 1)
    near = swapped(kv, "inner", 2)
    direct = [crossed(block, t, False) for t in range(1, nz // 2) for block in (kv, sib)]
    early = [kv, sib, near]
    dq_own, acc = blocks_call([x], early, range(3), *common, F32, F32, diagonal=True)

    near_sib = swapped(near, "inner", 1)
    xs = [swapped(x, "outer", s) for s in range(1, nq - 1)]
    dqs = [dq_own]
    for s in range(nq - 2):
        late = (near_sib,) if s == nq - 3 else ()
        xs[s], acc, *late = lax.optimization_barrier((xs[s], acc, *late))
        dq, acc = blocks_call([xs[s]], early, range(3), *common, F32, F32, acc=[(acc, n) for n in range(3)])
        dqs.append(dq)
    (near_sib,) = late
    halves = [xs[nq - 3][:hr], xs[((nq - 1) ^ (nq // 2)) - 1][hr:]]
    corner = [swapped(halves[0], "outer", 1), swapped(halves[1], "outer", nq // 2)]

    *direct, acc = lax.optimization_barrier((*direct, acc))
    traded = [swapped(block, "inner", 1) for block in direct]
    direct = [near_sib, *direct]
    xs = [x, *xs]
    n_d, n_t = len(direct), len(traded)
    *dqs, acc_d = blocks_call(xs, direct, range(n_d), *common, F32, F32, dq_in=dqs)
    types = [F32] + [BF] * (nq - 2)
    dq_own, *dqs, acc_t = blocks_call(xs, traded, range(n_t), *common, F32, types, dq_in=dqs)

    arrays = [*early, *direct, *traded]
    accs = [(a, n) for a, count in ((acc, 3), (acc_d, n_d), (acc_t, n_t)) for n in range(count)]
    theirs, ours = [1, 3], [0, 2]
    for t in range(0, n_t, 2):
        theirs += [3 + n_d + t, 4 + t + 1]
        ours += [4 + t, 3 + n_d + t + 1]
    dq_last, dkv_sib = blocks_call([corner], arrays, theirs, *common, BF, F32, acc=accs)
    dkv_got = swapped(dkv_sib, "inner", 1)
    dq_last, dkv_far = blocks_call([corner], arrays, ours[2:], *common, F32, F32, acc=accs, dq_in=[dq_last])
    dq_last, dkv_own = blocks_call([corner], arrays, ours[:2], *common, F32, BF, acc=accs, dq_in=[dq_last])
    far = add_call(dkv_far, dkv_got, 2, [BF] * (nz - 2))
    dkv_own, dkv_near = add_call(dkv_own, dkv_got, 0, [F32, BF])

    got = [swapped(dq, "outer", s + 1) for s, dq in enumerate(dqs)]
    dq_last, *got = lax.optimization_barrier((dq_last, *got))
    got.append(swapped(dq_last, "outer", nq - 1))
    dkv = []
    for t in range(1, nz // 2):
        dkv.append(crossed(far[2 * t - 2], t, False))
        dkv.append(crossed(far[2 * t - 1], t, True))
    dkv_near = swapped(dkv_near, "inner", 2)

    dkv_sum = pl.pallas_call(
        sum_kernel,
        out_shape=sds((2 * rows, width), F32),
        in_specs=[VMEM] * (nz - 1),
        out_specs=VMEM,
        compiler_params=SMALL,
        cost_estimate=pl.CostEstimate(flops=1_500_000_000, bytes_accessed=1000, transcendentals=0),
    )(dkv_own, *dkv)

    return pl.pallas_call(
        functools.partial(final_kernel, rows, heads, scale),
        out_shape=(sds((rows, heads * width), BF), sds((rows, width), BF), sds((rows, width), BF)),
        in_specs=[VMEM] * (3 + len(got)),
        out_specs=(VMEM,) * 3,
        compiler_params=SMALL,
        cost_estimate=QUICK,
    )(dq_own, dkv_sum, dkv_near, *got)


def solution(mesh):
    tokens = P(("outer", "inner"), None)
    return jax.shard_map(
        on_device,
        mesh=mesh,
        in_specs=(tokens,) * 5 + (P(None, ("outer", "inner")), P(("outer", "inner"))),
        out_specs=(tokens,) * 3,
        check_vma=False,
    )
```

```python
import functools
import math

import jax
import jax.numpy as jnp
from jax import lax
from jax.experimental import pallas as pl
from jax.experimental.pallas import tpu as pltpu
from jax.sharding import PartitionSpec as P

BF = jnp.bfloat16
F32 = jnp.float32
RUN = 64
LOG2E = math.log2(math.e)
VMEM = pl.BlockSpec(memory_space=pltpu.VMEM)
SMALL = pltpu.CompilerParams(vmem_limit_bytes=16 * 1024 * 1024)
NN = (((1,), (0,)), ((), ()))
NT = (((1,), (1,)), ((), ()))
QUICK = pl.CostEstimate(flops=1000, bytes_accessed=1000, transcendentals=0)
COLS = 512


def swapped(block, axis, mask):
    pairs = [(i, i ^ mask) for i in range(lax.axis_size(axis))]
    return lax.ppermute(block, axis, pairs)


def three_parts(x):
    hi = x.astype(BF)
    rest = x - hi.astype(F32)
    mid = rest.astype(BF)
    low = (rest - mid.astype(F32)).astype(BF)
    return [hi, mid, low]


def dot(a, b, dims=NN):
    return lax.dot_general(a, b, dims, preferred_element_type=F32)


def pack_kernel(q_ref, k_ref, v_ref, o_ref, g_ref, lse_ref, pos_ref, x_ref, kv_ref, o_s, lse_s, pos_s, sems):
    rows, width = k_ref.shape
    heads = q_ref.shape[1] // width
    moves = [(lse_ref, lse_s), (pos_ref, pos_s), (o_ref, o_s)]
    for h in range(heads):
        cols = pl.ds(h * width, width)
        moves.append((g_ref.at[:, cols], x_ref.at[pl.ds((heads + h) * rows, rows), :]))
    for h in range(heads):
        cols = pl.ds(h * width, width)
        moves.append((q_ref.at[:, cols], x_ref.at[pl.ds(h * rows, rows), :]))
    moves.append((k_ref, kv_ref.at[pl.ds(0, rows), :]))
    moves.append((v_ref, kv_ref.at[pl.ds(rows, rows), :]))
    copies = [pltpu.make_async_copy(a, b, sems.at[n]) for n, (a, b) in enumerate(moves)]
    for copy in copies:
        copy.start()
    for copy in copies[: 3 + heads]:
        copy.wait()
    ones = jnp.ones((8, width), BF)
    deltas = []
    for h in range(heads):
        g = x_ref[(heads + h) * rows : (heads + h + 1) * rows, :]
        prod = g.astype(F32) * o_s[:, h * width : (h + 1) * width].astype(F32)
        hi = prod.astype(BF)
        low = (prod - hi.astype(F32)).astype(BF)
        deltas.append((dot(ones, hi, NT) + dot(ones, low, NT))[:1])
    run = (pos_s[...] // RUN).astype(F32)
    extra = (
        three_parts(lse_s[...] * LOG2E)
        + three_parts(jnp.concatenate(deltas, axis=0))
        + [run.astype(BF), jnp.zeros((32 - 6 * heads - 1, rows), BF)]
    )
    x_ref[2 * heads * rows :, :] = jnp.concatenate([e.astype(F32) for e in extra], axis=0).astype(BF)
    lane = lax.broadcasted_iota(jnp.int32, run.shape, 1)
    ids = [
        jnp.max(jnp.where(lane == r * RUN, run, 0.0), axis=1, keepdims=True)
        for r in range(rows // RUN)
    ]
    wide = [jnp.broadcast_to(i, (1, width)) for i in ids]
    wide.append(jnp.zeros((16 - len(ids), width), F32))
    kv_ref[2 * rows :, :] = jnp.concatenate(wide, axis=0).astype(BF)
    for copy in copies[3 + heads :]:
        copy.wait()


def blocks_kernel(plan, rows, heads, scale, *refs):
    refs = list(refs)
    x_refs = []
    for parts in plan["parts"]:
        whole = refs.pop(0)
        x_refs.append((whole, whole.at[heads * rows :, :] if parts == 1 else refs.pop(0)))
    kv_refs = [refs.pop(0) for _ in range(plan["kv"])]
    acc_refs = [refs.pop(0) for _ in range(plan["acc"])]
    dq_in = [refs.pop(0) for _ in range(plan["dq_in"])]
    dq_refs, dkv_ref = refs[:-1], refs[-1]
    width = x_refs[0][0].shape[1]
    hr = heads * rows
    per = rows // RUN
    step = COLS // rows
    slots = plan["slots"]
    rowed = []
    for _, g_ref in x_refs:
        e = g_ref[hr:, :].astype(F32)
        lse = e[0:heads] + e[heads : 2 * heads] + e[2 * heads : 3 * heads]
        delta = e[3 * heads : 4 * heads] + e[4 * heads : 5 * heads] + e[5 * heads : 6 * heads]
        rowed.append((lse, delta, e[6 * heads : 6 * heads + 1]))
    dqt = [[None] * (hr // COLS) for _ in x_refs]
    group = 3 if len(slots) == 3 else 2
    for c in range(0, len(slots), group):
        ks, vs, runs = [], [], []
        for n in slots[c : c + group]:
            ks.append(kv_refs[n][:rows, :])
            vs.append(kv_refs[n][rows : 2 * rows, :])
            e = kv_refs[n][2 * rows :, :].astype(F32)
            runs += [e[r : r + 1] for r in range(per)]
        k = jnp.concatenate(ks, axis=0)
        v = jnp.concatenate(vs, axis=0)
        kt = jnp.concatenate([b.astype(F32).T.astype(BF) for b in ks], axis=1)
        dk = dv = None
        for b, (q_ref, g_ref) in enumerate(x_refs):
            lse, delta, run = rowed[b]
            for n in range(hr // COLS):
                q = q_ref[n * COLS : (n + 1) * COLS, :]
                g = g_ref[n * COLS : (n + 1) * COLS, :]
                st = dot(k, q, NT)
                dpt = dot(v, g, NT)
                p_rows, d_rows = [], []
                for r in range(len(runs)):
                    sl = slice(r * RUN, (r + 1) * RUN)
                    p_heads, d_heads = [], []
                    for h in range(step):
                        hl = slice(h * rows, (h + 1) * rows)
                        head = n * step + h
                        row = jnp.where(runs[r] <= run, lse[head : head + 1], 1e30)
                        arg = st[sl, hl] * (scale * LOG2E) - row
                        if plan["diagonal"] and b == 0 and c == 0 and r < per:
                            i = lax.broadcasted_iota(jnp.int32, (RUN, rows), 1) - r * RUN
                            j = lax.broadcasted_iota(jnp.int32, (RUN, rows), 0)
                            arg = jnp.where((i >= 0) & (i < j), -1e30, arg)
                        p = jnp.exp2(arg)
                        p_heads.append(p.astype(BF))
                        d_heads.append((p * (dpt[sl, hl] - delta[head : head + 1])).astype(BF))
                    p_rows.append(jnp.concatenate(p_heads, axis=1))
                    d_rows.append(jnp.concatenate(d_heads, axis=1))
                p = jnp.concatenate(p_rows, axis=0)
                d = jnp.concatenate(d_rows, axis=0)
                dv_n, dk_n, dq_n = dot(p, g), dot(d, q), dot(kt, d)
                dv = dv_n if dv is None else dv + dv_n
                dk = dk_n if dk is None else dk + dk_n
                old = dqt[b][n]
                dqt[b][n] = dq_n if old is None else old + dq_n
        for j, n in enumerate(slots[c : c + group]):
            dk_j, dv_j = dk[j * rows : (j + 1) * rows], dv[j * rows : (j + 1) * rows]
            if plan["acc"]:
                acc_ref, at = acc_refs[plan["at"][n][0]], plan["at"][n][1]
                dk_j += acc_ref[at, :rows, :]
                dv_j += acc_ref[at, rows:, :]
            dkv_ref[c + j, :rows, :] = dk_j.astype(dkv_ref.dtype)
            dkv_ref[c + j, rows:, :] = dv_j.astype(dkv_ref.dtype)
    for b, dq_ref in enumerate(dq_refs):
        for n in range(hr // COLS):
            cols = slice(n * COLS, (n + 1) * COLS)
            total = dqt[b][n] + dq_in[b][:, cols] if dq_in else dqt[b][n]
            dq_ref[:, cols] = total.astype(dq_ref.dtype)


def blocks_call(xs, kvs, slots, rows, heads, scale, dkv_type, dq_type, acc=(), dq_in=(), diagonal=False):
    sds = jax.ShapeDtypeStruct
    width = kvs[0].shape[1]
    xs = [x if isinstance(x, list) else [x] for x in xs]
    slots = list(slots)
    totals = []
    for a, _ in acc:
        if all(a is not t for t in totals):
            totals.append(a)
    at = [([a is t for t in totals].index(True), n) for a, n in acc]
    plan = {
        "parts": [len(x) for x in xs],
        "kv": len(kvs),
        "acc": len(totals),
        "at": at,
        "dq_in": len(dq_in),
        "slots": slots,
        "diagonal": diagonal,
    }
    args = (*sum(xs, []), *kvs, *totals, *dq_in)
    types = dq_type if isinstance(dq_type, list) else [dq_type] * len(xs)
    outs = tuple(sds((width, heads * rows), t) for t in types)
    outs += (sds((len(slots), 2 * rows, width), dkv_type),)
    return pl.pallas_call(
        functools.partial(blocks_kernel, plan, rows, heads, scale),
        out_shape=outs,
        in_specs=[VMEM] * len(args),
        out_specs=(VMEM,) * len(outs),
        compiler_params=SMALL,
        cost_estimate=QUICK,
    )(*args)


def add_kernel(start, own_ref, got_ref, *refs):
    for n, ref in enumerate(refs):
        ref[...] = (own_ref[n] + got_ref[start + n].astype(F32)).astype(ref.dtype)


def add_call(own, got, start, types):
    return pl.pallas_call(
        functools.partial(add_kernel, start),
        out_shape=tuple(jax.ShapeDtypeStruct(own.shape[1:], t) for t in types),
        in_specs=[VMEM] * 2,
        out_specs=(VMEM,) * len(types),
        compiler_params=SMALL,
        cost_estimate=QUICK,
    )(own, got)


def sum_kernel(own_ref, *refs):
    total = own_ref[...]
    for ref in refs[:-1]:
        total = total + ref[...].astype(F32)
    refs[-1][...] = total


def final_kernel(rows, heads, scale, dq_own, dkv_ref, near_ref, *refs):
    dq_refs, (gq_ref, gk_ref, gv_ref) = refs[:-3], refs[-3:]
    dq = dq_own[...]
    for r in dq_refs:
        dq = dq + r[...].astype(F32)
    for h in range(heads):
        part = dq[:, h * rows : (h + 1) * rows]
        gq_ref[:, h * 128 : (h + 1) * 128] = (scale * part).T.astype(BF)
    dkv = dkv_ref[...] + near_ref[...].astype(F32)
    gk_ref[...] = (scale * dkv[:rows]).astype(BF)
    gv_ref[...] = dkv[rows:].astype(BF)


def crossed(block, t, other):
    pairs = []
    for i in range(lax.axis_size("inner")):
        chip, core = i // 2, i % 2
        pairs.append((i, 2 * (chip ^ (2 * t + (core if other else 1 - core))) + core))
    return lax.ppermute(block, "inner", pairs)


def on_device(query, key, value, out, grad_out, lse, positions):
    rows, width = key.shape
    heads = query.shape[1] // width
    hr = heads * rows
    scale = width ** (-0.5)
    nq = lax.axis_size("outer")
    nz = lax.axis_size("inner") // 2
    sds = jax.ShapeDtypeStruct
    inputs = (query, key, value, out, grad_out, lse, positions[None, :])
    x, kv = pl.pallas_call(
        pack_kernel,
        out_shape=(sds((2 * hr + 32, width), BF), sds((2 * rows + 16, width), BF)),
        in_specs=[pl.BlockSpec(memory_space=pltpu.HBM)] * 7,
        out_specs=(VMEM, VMEM),
        scratch_shapes=[
            pltpu.VMEM(out.shape, BF),
            pltpu.VMEM(lse.shape, F32),
            pltpu.VMEM((1, rows), jnp.int32),
            pltpu.SemaphoreType.DMA((5 + 2 * heads,)),
        ],
        compiler_params=SMALL,
        cost_estimate=QUICK,
    )(*[pltpu.with_memory_space_constraint(a, pltpu.HBM) for a in inputs])

    common = (rows, heads, scale)
    sib = swapped(kv, "inner", 1)
    near = swapped(kv, "inner", 2)
    direct = [crossed(block, t, False) for t in range(1, nz // 2) for block in (kv, sib)]
    early = [kv, sib, near]
    dq_own, acc = blocks_call([x], early, range(3), *common, F32, F32, diagonal=True)

    xs = [swapped(x, "outer", s) for s in range(1, nq - 1)]
    dqs = [dq_own]
    for s in range(nq - 2):
        xs[s], acc = lax.optimization_barrier((xs[s], acc))
        dq, acc = blocks_call([xs[s]], early, range(3), *common, F32, F32, acc=[(acc, n) for n in range(3)])
        dqs.append(dq)
    halves = [xs[nq - 3][:hr], xs[((nq - 1) ^ (nq // 2)) - 1][hr:]]
    corner = [swapped(halves[0], "outer", 1), swapped(halves[1], "outer", nq // 2)]

    *fetched, acc = lax.optimization_barrier((near, *direct, acc))
    direct = fetched[1:]
    traded = [swapped(block, "inner", 1) for block in fetched]
    xs = [x, *xs]
    n_d, n_t = len(direct), len(traded)
    *dqs, acc_d = blocks_call(xs, direct, range(n_d), *common, F32, F32, dq_in=dqs)
    types = [F32] + [BF] * (nq - 2)
    dq_own, *dqs, acc_t = blocks_call(xs, traded, range(n_t), *common, F32, types, dq_in=dqs)

    arrays = [*early, *direct, *traded]
    accs = [(a, n) for a, count in ((acc, 3), (acc_d, n_d), (acc_t, n_t)) for n in range(count)]
    theirs, ours = [1, 3 + n_d], [0, 2]
    for t in range(0, n_d, 2):
        theirs += [4 + n_d + t, 3 + t + 1]
        ours += [3 + t, 4 + n_d + t + 1]
    dq_last, dkv_sib = blocks_call([corner], arrays, theirs, *common, BF, F32, acc=accs)
    dkv_got = swapped(dkv_sib, "inner", 1)
    dq_last, dkv_far = blocks_call([corner], arrays, ours[2:], *common, F32, F32, acc=accs, dq_in=[dq_last])
    dq_last, dkv_own = blocks_call([corner], arrays, ours[:2], *common, F32, BF, acc=accs, dq_in=[dq_last])
    far = add_call(dkv_far, dkv_got, 2, [BF] * (nz - 2))
    dkv_own, dkv_near = add_call(dkv_own, dkv_got, 0, [F32, BF])

    got = [swapped(dq, "outer", s + 1) for s, dq in enumerate(dqs)]
    dq_last, *got = lax.optimization_barrier((dq_last, *got))
    got.append(swapped(dq_last, "outer", nq - 1))
    dkv = []
    for t in range(1, nz // 2):
        dkv.append(crossed(far[2 * t - 2], t, False))
        dkv.append(crossed(far[2 * t - 1], t, True))
    dkv_near = swapped(dkv_near, "inner", 2)

    dkv_sum = pl.pallas_call(
        sum_kernel,
        out_shape=sds((2 * rows, width), F32),
        in_specs=[VMEM] * (nz - 1),
        out_specs=VMEM,
        compiler_params=SMALL,
        cost_estimate=pl.CostEstimate(flops=1_500_000_000, bytes_accessed=1000, transcendentals=0),
    )(dkv_own, *dkv)

    return pl.pallas_call(
        functools.partial(final_kernel, rows, heads, scale),
        out_shape=(sds((rows, heads * width), BF), sds((rows, width), BF), sds((rows, width), BF)),
        in_specs=[VMEM] * (3 + len(got)),
        out_specs=(VMEM,) * 3,
        compiler_params=SMALL,
        cost_estimate=QUICK,
    )(dq_own, dkv_sum, dkv_near, *got)


def solution(mesh):
    tokens = P(("outer", "inner"), None)
    return jax.shard_map(
        on_device,
        mesh=mesh,
        in_specs=(tokens,) * 5 + (P(None, ("outer", "inner")), P(("outer", "inner"))),
        out_specs=(tokens,) * 3,
        check_vma=False,
    )
```

```python
import functools
import math

import jax
import jax.numpy as jnp
from jax import lax
from jax.experimental import pallas as pl
from jax.experimental.pallas import tpu as pltpu
from jax.sharding import PartitionSpec as P

BF = jnp.bfloat16
F32 = jnp.float32
RUN = 64
LOG2E = math.log2(math.e)
VMEM = pl.BlockSpec(memory_space=pltpu.VMEM)
SMALL = pltpu.CompilerParams(vmem_limit_bytes=16 * 1024 * 1024)
NN = (((1,), (0,)), ((), ()))
NT = (((1,), (1,)), ((), ()))
QUICK = pl.CostEstimate(flops=1000, bytes_accessed=1000, transcendentals=0)
COLS = 512


def swapped(block, axis, mask):
    pairs = [(i, i ^ mask) for i in range(lax.axis_size(axis))]
    return lax.ppermute(block, axis, pairs)


def three_parts(x):
    hi = x.astype(BF)
    rest = x - hi.astype(F32)
    mid = rest.astype(BF)
    low = (rest - mid.astype(F32)).astype(BF)
    return [hi, mid, low]


def dot(a, b, dims=NN):
    return lax.dot_general(a, b, dims, preferred_element_type=F32)


def pack_kernel(q_ref, k_ref, v_ref, o_ref, g_ref, lse_ref, pos_ref, x_ref, kv_ref, o_s, lse_s, pos_s, sems):
    rows, width = k_ref.shape
    heads = q_ref.shape[1] // width
    moves = [(lse_ref, lse_s), (pos_ref, pos_s), (o_ref, o_s)]
    for h in range(heads):
        cols = pl.ds(h * width, width)
        moves.append((g_ref.at[:, cols], x_ref.at[pl.ds((heads + h) * rows, rows), :]))
    for h in range(heads):
        cols = pl.ds(h * width, width)
        moves.append((q_ref.at[:, cols], x_ref.at[pl.ds(h * rows, rows), :]))
    moves.append((k_ref, kv_ref.at[pl.ds(0, rows), :]))
    moves.append((v_ref, kv_ref.at[pl.ds(rows, rows), :]))
    copies = [pltpu.make_async_copy(a, b, sems.at[n]) for n, (a, b) in enumerate(moves)]
    for copy in copies:
        copy.start()
    for copy in copies[: 3 + heads]:
        copy.wait()
    ones = jnp.ones((8, width), BF)
    deltas = []
    for h in range(heads):
        g = x_ref[(heads + h) * rows : (heads + h + 1) * rows, :]
        prod = g.astype(F32) * o_s[:, h * width : (h + 1) * width].astype(F32)
        hi = prod.astype(BF)
        low = (prod - hi.astype(F32)).astype(BF)
        deltas.append((dot(ones, hi, NT) + dot(ones, low, NT))[:1])
    run = (pos_s[...] // RUN).astype(F32)
    extra = (
        three_parts(lse_s[...] * LOG2E)
        + three_parts(jnp.concatenate(deltas, axis=0))
        + [run.astype(BF), jnp.zeros((32 - 6 * heads - 1, rows), BF)]
    )
    x_ref[2 * heads * rows :, :] = jnp.concatenate([e.astype(F32) for e in extra], axis=0).astype(BF)
    lane = lax.broadcasted_iota(jnp.int32, run.shape, 1)
    ids = [
        jnp.max(jnp.where(lane == r * RUN, run, 0.0), axis=1, keepdims=True)
        for r in range(rows // RUN)
    ]
    wide = [jnp.broadcast_to(i, (1, width)) for i in ids]
    wide.append(jnp.zeros((16 - len(ids), width), F32))
    kv_ref[2 * rows :, :] = jnp.concatenate(wide, axis=0).astype(BF)
    for copy in copies[3 + heads :]:
        copy.wait()


def blocks_kernel(plan, rows, heads, scale, *refs):
    refs = list(refs)
    x_refs = []
    for parts in plan["parts"]:
        whole = refs.pop(0)
        x_refs.append((whole, whole.at[heads * rows :, :] if parts == 1 else refs.pop(0)))
    kv_refs = [refs.pop(0) for _ in range(plan["kv"])]
    acc_refs = [refs.pop(0) for _ in range(plan["acc"])]
    dq_in = [refs.pop(0) for _ in range(plan["dq_in"])]
    dq_refs, dkv_ref = refs[:-1], refs[-1]
    width = x_refs[0][0].shape[1]
    hr = heads * rows
    per = rows // RUN
    step = COLS // rows
    slots = plan["slots"]
    rowed = []
    for _, g_ref in x_refs:
        e = g_ref[hr:, :].astype(F32)
        lse = e[0:heads] + e[heads : 2 * heads] + e[2 * heads : 3 * heads]
        delta = e[3 * heads : 4 * heads] + e[4 * heads : 5 * heads] + e[5 * heads : 6 * heads]
        rowed.append((lse, delta, e[6 * heads : 6 * heads + 1]))
    group = 3 if len(slots) == 3 else 2
    loaded = {}

    def chunk(c):
        if c not in loaded:
            ks, vs, runs = [], [], []
            for n in slots[c : c + group]:
                ks.append(kv_refs[n][:rows, :])
                vs.append(kv_refs[n][rows : 2 * rows, :])
                e = kv_refs[n][2 * rows :, :].astype(F32)
                runs += [e[r : r + 1] for r in range(per)]
            kt = jnp.concatenate([b.astype(F32).T.astype(BF) for b in ks], axis=1)
            loaded[c] = (jnp.concatenate(ks, axis=0), jnp.concatenate(vs, axis=0), kt, runs)
        return loaded[c]

    def products(c, b, n):
        k, v, _, _ = chunk(c)
        q_ref, g_ref = x_refs[b]
        q = q_ref[n * COLS : (n + 1) * COLS, :]
        g = g_ref[n * COLS : (n + 1) * COLS, :]
        return q, g, dot(k, q, NT), dot(v, g, NT)

    def weights(c, b, n, st, dpt):
        lse, delta, run = rowed[b]
        p_rows, d_rows = [], []
        for r, krun in enumerate(chunk(c)[3]):
            sl = slice(r * RUN, (r + 1) * RUN)
            p_heads, d_heads = [], []
            for h in range(step):
                hl = slice(h * rows, (h + 1) * rows)
                head = n * step + h
                row = jnp.where(krun <= run, lse[head : head + 1], 1e30)
                arg = st[sl, hl] * (scale * LOG2E) - row
                if plan["diagonal"] and b == 0 and c == 0 and r < per:
                    i = lax.broadcasted_iota(jnp.int32, (RUN, rows), 1) - r * RUN
                    j = lax.broadcasted_iota(jnp.int32, (RUN, rows), 0)
                    arg = jnp.where((i >= 0) & (i < j), -1e30, arg)
                p = jnp.exp2(arg)
                p_heads.append(p.astype(BF))
                d_heads.append((p * (dpt[sl, hl] - delta[head : head + 1])).astype(BF))
            p_rows.append(jnp.concatenate(p_heads, axis=1))
            d_rows.append(jnp.concatenate(d_heads, axis=1))
        return jnp.concatenate(p_rows, axis=0), jnp.concatenate(d_rows, axis=0)

    def plus(total, part):
        return part if total is None else total + part

    dqt = [[None] * (hr // COLS) for _ in x_refs]
    units = [
        (c, b, n)
        for c in range(0, len(slots), group)
        for b in range(len(x_refs))
        for n in range(hr // COLS)
    ]
    dk = dv = None
    ahead = products(*units[0])
    for at, (c, b, n) in enumerate(units):
        q, g, st, dpt = ahead
        if at + 1 < len(units):
            ahead = products(*units[at + 1])
        p, d = weights(c, b, n, st, dpt)
        dv, dk = plus(dv, dot(p, g)), plus(dk, dot(d, q))
        dqt[b][n] = plus(dqt[b][n], dot(chunk(c)[2], d))
        if at + 1 < len(units) and units[at + 1][0] == c:
            continue
        for j, slot in enumerate(slots[c : c + group]):
            dk_j, dv_j = dk[j * rows : (j + 1) * rows], dv[j * rows : (j + 1) * rows]
            if plan["acc"]:
                acc_ref, place = acc_refs[plan["at"][slot][0]], plan["at"][slot][1]
                dk_j += acc_ref[place, :rows, :]
                dv_j += acc_ref[place, rows:, :]
            dkv_ref[c + j, :rows, :] = dk_j.astype(dkv_ref.dtype)
            dkv_ref[c + j, rows:, :] = dv_j.astype(dkv_ref.dtype)
        dk = dv = None
    for b, dq_ref in enumerate(dq_refs):
        for n in range(hr // COLS):
            cols = slice(n * COLS, (n + 1) * COLS)
            total = dqt[b][n] + dq_in[b][:, cols] if dq_in else dqt[b][n]
            dq_ref[:, cols] = total.astype(dq_ref.dtype)


def blocks_call(xs, kvs, slots, rows, heads, scale, dkv_type, dq_type, acc=(), dq_in=(), diagonal=False):
    sds = jax.ShapeDtypeStruct
    width = kvs[0].shape[1]
    xs = [x if isinstance(x, list) else [x] for x in xs]
    slots = list(slots)
    totals = []
    for a, _ in acc:
        if all(a is not t for t in totals):
            totals.append(a)
    at = [([a is t for t in totals].index(True), n) for a, n in acc]
    plan = {
        "parts": [len(x) for x in xs],
        "kv": len(kvs),
        "acc": len(totals),
        "at": at,
        "dq_in": len(dq_in),
        "slots": slots,
        "diagonal": diagonal,
    }
    args = (*sum(xs, []), *kvs, *totals, *dq_in)
    types = dq_type if isinstance(dq_type, list) else [dq_type] * len(xs)
    outs = tuple(sds((width, heads * rows), t) for t in types)
    outs += (sds((len(slots), 2 * rows, width), dkv_type),)
    return pl.pallas_call(
        functools.partial(blocks_kernel, plan, rows, heads, scale),
        out_shape=outs,
        in_specs=[VMEM] * len(args),
        out_specs=(VMEM,) * len(outs),
        compiler_params=SMALL,
        cost_estimate=QUICK,
    )(*args)


def add_kernel(start, own_ref, got_ref, *refs):
    for n, ref in enumerate(refs):
        ref[...] = (own_ref[n] + got_ref[start + n].astype(F32)).astype(ref.dtype)


def add_call(own, got, start, types):
    return pl.pallas_call(
        functools.partial(add_kernel, start),
        out_shape=tuple(jax.ShapeDtypeStruct(own.shape[1:], t) for t in types),
        in_specs=[VMEM] * 2,
        out_specs=(VMEM,) * len(types),
        compiler_params=SMALL,
        cost_estimate=QUICK,
    )(own, got)


def sum_kernel(own_ref, *refs):
    total = own_ref[...]
    for ref in refs[:-1]:
        total = total + ref[...].astype(F32)
    refs[-1][...] = total


def sum_call(own, got, flops):
    return pl.pallas_call(
        sum_kernel,
        out_shape=jax.ShapeDtypeStruct(own.shape, F32),
        in_specs=[VMEM] * (1 + len(got)),
        out_specs=VMEM,
        compiler_params=SMALL,
        cost_estimate=pl.CostEstimate(flops=flops, bytes_accessed=1000, transcendentals=0),
    )(own, *got)


def final_kernel(rows, heads, scale, dq_ref, dq_far, dkv_ref, dkv_near, gq_ref, gk_ref, gv_ref):
    dkv = dkv_ref[...] + dkv_near[...].astype(F32)
    gk_ref[...] = (scale * dkv[:rows]).astype(BF)
    gv_ref[...] = dkv[rows:].astype(BF)
    dq = dq_ref[...] + dq_far[...].astype(F32)
    for h in range(heads):
        part = dq[:, h * rows : (h + 1) * rows]
        gq_ref[:, h * 128 : (h + 1) * 128] = (scale * part).T.astype(BF)


def crossed(block, t, other):
    pairs = []
    for i in range(lax.axis_size("inner")):
        chip, core = i // 2, i % 2
        pairs.append((i, 2 * (chip ^ (2 * t + (core if other else 1 - core))) + core))
    return lax.ppermute(block, "inner", pairs)


def on_device(query, key, value, out, grad_out, lse, positions):
    rows, width = key.shape
    heads = query.shape[1] // width
    hr = heads * rows
    scale = width ** (-0.5)
    nq = lax.axis_size("outer")
    nz = lax.axis_size("inner") // 2
    sds = jax.ShapeDtypeStruct
    inputs = (query, key, value, out, grad_out, lse, positions[None, :])
    x, kv = pl.pallas_call(
        pack_kernel,
        out_shape=(sds((2 * hr + 32, width), BF), sds((2 * rows + 16, width), BF)),
        in_specs=[pl.BlockSpec(memory_space=pltpu.HBM)] * 7,
        out_specs=(VMEM, VMEM),
        scratch_shapes=[
            pltpu.VMEM(out.shape, BF),
            pltpu.VMEM(lse.shape, F32),
            pltpu.VMEM((1, rows), jnp.int32),
            pltpu.SemaphoreType.DMA((5 + 2 * heads,)),
        ],
        compiler_params=SMALL,
        cost_estimate=QUICK,
    )(*[pltpu.with_memory_space_constraint(a, pltpu.HBM) for a in inputs])

    common = (rows, heads, scale)
    sib = swapped(kv, "inner", 1)
    near = swapped(kv, "inner", 2)
    direct = [crossed(block, t, False) for t in range(1, nz // 2) for block in (kv, sib)]
    early = [kv, sib, near]
    dq_own, acc = blocks_call([x], early, range(3), *common, F32, F32, diagonal=True)

    xs = [swapped(x, "outer", s) for s in range(1, nq - 1)]
    dqs = [dq_own]
    for s in range(nq - 2):
        xs[s], acc = lax.optimization_barrier((xs[s], acc))
        dq, acc = blocks_call([xs[s]], early, range(3), *common, F32, F32, acc=[(acc, n) for n in range(3)])
        dqs.append(dq)
    halves = [xs[nq - 3][:hr], xs[((nq - 1) ^ (nq // 2)) - 1][hr:]]
    corner = [swapped(halves[0], "outer", 1), swapped(halves[1], "outer", nq // 2)]

    *direct, acc = lax.optimization_barrier((*direct, acc))
    traded = [swapped(block, "inner", 1) for block in direct]
    direct = [swapped(near, "inner", 1), *direct]
    xs = [x, *xs]
    n_d, n_t = len(direct), len(traded)
    *dqs, acc_d = blocks_call(xs, direct, range(n_d), *common, F32, F32, dq_in=dqs)
    types = [F32] + [BF] * (nq - 2)
    dq_own, *dqs, acc_t = blocks_call(xs, traded, range(n_t), *common, F32, types, dq_in=dqs)

    arrays = [*early, *direct, *traded]
    accs = [(a, n) for a, count in ((acc, 3), (acc_d, n_d), (acc_t, n_t)) for n in range(count)]
    theirs, ours = [1, 3], [0, 2]
    for t in range(0, n_t, 2):
        theirs += [3 + n_d + t, 4 + t + 1]
        ours += [4 + t, 3 + n_d + t + 1]
    dq_last, dkv_sib = blocks_call([corner], arrays, theirs, *common, BF, F32, acc=accs)
    dkv_got = swapped(dkv_sib, "inner", 1)
    dq_last, dkv_far = blocks_call([corner], arrays, ours[2:], *common, F32, F32, acc=accs, dq_in=[dq_last])
    dq_last, dkv_own = blocks_call([corner], arrays, ours[:2], *common, F32, BF, acc=accs, dq_in=[dq_last])
    far = add_call(dkv_far, dkv_got, 2, [BF] * (nz - 2))
    dkv_own, dkv_near = add_call(dkv_own, dkv_got, 0, [F32, BF])

    got = [swapped(dq, "outer", s + 1) for s, dq in enumerate(dqs)]
    dq_far = swapped(dq_last, "outer", nq - 1)
    dkv = []
    for t in range(1, nz // 2):
        dkv.append(crossed(far[2 * t - 2], t, False))
        dkv.append(crossed(far[2 * t - 1], t, True))
    dkv_near = swapped(dkv_near, "inner", 2)

    dkv_sum = sum_call(dkv_own, dkv, 1_500_000_000)
    dq_sum = sum_call(dq_own, got, 100_000_000)
    return pl.pallas_call(
        functools.partial(final_kernel, rows, heads, scale),
        out_shape=(sds((rows, heads * width), BF), sds((rows, width), BF), sds((rows, width), BF)),
        in_specs=[VMEM] * 4,
        out_specs=(VMEM,) * 3,
        compiler_params=SMALL,
        cost_estimate=QUICK,
    )(dq_sum, dq_far, dkv_sum, dkv_near)


def solution(mesh):
    tokens = P(("outer", "inner"), None)
    return jax.shard_map(
        on_device,
        mesh=mesh,
        in_specs=(tokens,) * 5 + (P(None, ("outer", "inner")), P(("outer", "inner"))),
        out_specs=(tokens,) * 3,
        check_vma=False,
    )
```

```python
import functools
import math

import jax
import jax.numpy as jnp
from jax import lax
from jax.experimental import pallas as pl
from jax.experimental.pallas import tpu as pltpu
from jax.sharding import PartitionSpec as P

BF = jnp.bfloat16
F32 = jnp.float32
RUN = 64
LOG2E = math.log2(math.e)
VMEM = pl.BlockSpec(memory_space=pltpu.VMEM)
SMALL = pltpu.CompilerParams(vmem_limit_bytes=16 * 1024 * 1024)
NN = (((1,), (0,)), ((), ()))
NT = (((1,), (1,)), ((), ()))
QUICK = pl.CostEstimate(flops=1000, bytes_accessed=1000, transcendentals=0)
COLS = 512


def swapped(block, axis, mask):
    pairs = [(i, i ^ mask) for i in range(lax.axis_size(axis))]
    return lax.ppermute(block, axis, pairs)


def three_parts(x):
    hi = x.astype(BF)
    rest = x - hi.astype(F32)
    mid = rest.astype(BF)
    low = (rest - mid.astype(F32)).astype(BF)
    return [hi, mid, low]


def dot(a, b, dims=NN):
    return lax.dot_general(a, b, dims, preferred_element_type=F32)


def pack_kernel(q_ref, k_ref, v_ref, o_ref, g_ref, lse_ref, pos_ref, x_ref, kv_ref, o_s, lse_s, pos_s, sems):
    rows, width = k_ref.shape
    heads = q_ref.shape[1] // width
    moves = [(lse_ref, lse_s), (pos_ref, pos_s), (o_ref, o_s)]
    for h in range(heads):
        cols = pl.ds(h * width, width)
        moves.append((g_ref.at[:, cols], x_ref.at[pl.ds((heads + h) * rows, rows), :]))
    for h in range(heads):
        cols = pl.ds(h * width, width)
        moves.append((q_ref.at[:, cols], x_ref.at[pl.ds(h * rows, rows), :]))
    moves.append((k_ref, kv_ref.at[pl.ds(0, rows), :]))
    moves.append((v_ref, kv_ref.at[pl.ds(rows, rows), :]))
    copies = [pltpu.make_async_copy(a, b, sems.at[n]) for n, (a, b) in enumerate(moves)]
    for copy in copies:
        copy.start()
    for copy in copies[: 3 + heads]:
        copy.wait()
    ones = jnp.ones((8, width), BF)
    deltas = []
    for h in range(heads):
        g = x_ref[(heads + h) * rows : (heads + h + 1) * rows, :]
        prod = g.astype(F32) * o_s[:, h * width : (h + 1) * width].astype(F32)
        hi = prod.astype(BF)
        low = (prod - hi.astype(F32)).astype(BF)
        deltas.append((dot(ones, hi, NT) + dot(ones, low, NT))[:1])
    run = (pos_s[...] // RUN).astype(F32)
    extra = (
        three_parts(lse_s[...] * LOG2E)
        + three_parts(jnp.concatenate(deltas, axis=0))
        + [run.astype(BF), jnp.zeros((32 - 6 * heads - 1, rows), BF)]
    )
    x_ref[2 * heads * rows :, :] = jnp.concatenate([e.astype(F32) for e in extra], axis=0).astype(BF)
    lane = lax.broadcasted_iota(jnp.int32, run.shape, 1)
    ids = [
        jnp.max(jnp.where(lane == r * RUN, run, 0.0), axis=1, keepdims=True)
        for r in range(rows // RUN)
    ]
    wide = [jnp.broadcast_to(i, (1, width)) for i in ids]
    wide.append(jnp.zeros((16 - len(ids), width), F32))
    kv_ref[2 * rows :, :] = jnp.concatenate(wide, axis=0).astype(BF)
    for copy in copies[3 + heads :]:
        copy.wait()


def blocks_kernel(plan, rows, heads, scale, *refs):
    refs = list(refs)
    x_refs = []
    for parts in plan["parts"]:
        whole = refs.pop(0)
        x_refs.append((whole, whole.at[heads * rows :, :] if parts == 1 else refs.pop(0)))
    kv_refs = [refs.pop(0) for _ in range(plan["kv"])]
    acc_refs = [refs.pop(0) for _ in range(plan["acc"])]
    dq_in = [refs.pop(0) for _ in range(plan["dq_in"])]
    dq_refs, dkv_ref = refs[:-1], refs[-1]
    width = x_refs[0][0].shape[1]
    hr = heads * rows
    per = rows // RUN
    step = COLS // rows
    slots = plan["slots"]
    rowed = []
    for _, g_ref in x_refs:
        e = g_ref[hr:, :].astype(F32)
        lse = e[0:heads] + e[heads : 2 * heads] + e[2 * heads : 3 * heads]
        delta = e[3 * heads : 4 * heads] + e[4 * heads : 5 * heads] + e[5 * heads : 6 * heads]
        rowed.append((lse, delta, e[6 * heads : 6 * heads + 1]))
    group = 3 if len(slots) == 3 else 2
    loaded = {}

    def chunk(c):
        if c not in loaded:
            ks, vs, runs = [], [], []
            for n in slots[c : c + group]:
                ks.append(kv_refs[n][:rows, :])
                vs.append(kv_refs[n][rows : 2 * rows, :])
                e = kv_refs[n][2 * rows :, :].astype(F32)
                runs += [e[r : r + 1] for r in range(per)]
            kt = jnp.concatenate([b.astype(F32).T.astype(BF) for b in ks], axis=1)
            loaded[c] = (jnp.concatenate(ks, axis=0), jnp.concatenate(vs, axis=0), kt, runs)
        return loaded[c]

    def products(c, b, n):
        k, v, _, _ = chunk(c)
        q_ref, g_ref = x_refs[b]
        q = q_ref[n * COLS : (n + 1) * COLS, :]
        g = g_ref[n * COLS : (n + 1) * COLS, :]
        return q, g, dot(k, q, NT), dot(v, g, NT)

    def weights(c, b, n, st, dpt):
        lse, delta, run = rowed[b]
        p_rows, d_rows = [], []
        for r, krun in enumerate(chunk(c)[3]):
            sl = slice(r * RUN, (r + 1) * RUN)
            p_heads, d_heads = [], []
            for h in range(step):
                hl = slice(h * rows, (h + 1) * rows)
                head = n * step + h
                row = jnp.where(krun <= run, lse[head : head + 1], 1e30)
                arg = st[sl, hl] * (scale * LOG2E) - row
                if plan["diagonal"] and b == 0 and c == 0 and r < per:
                    i = lax.broadcasted_iota(jnp.int32, (RUN, rows), 1) - r * RUN
                    j = lax.broadcasted_iota(jnp.int32, (RUN, rows), 0)
                    arg = jnp.where((i >= 0) & (i < j), -1e30, arg)
                p = jnp.exp2(arg)
                p_heads.append(p.astype(BF))
                d_heads.append((p * (dpt[sl, hl] - delta[head : head + 1])).astype(BF))
            p_rows.append(jnp.concatenate(p_heads, axis=1))
            d_rows.append(jnp.concatenate(d_heads, axis=1))
        return jnp.concatenate(p_rows, axis=0), jnp.concatenate(d_rows, axis=0)

    def plus(total, part):
        return part if total is None else total + part

    dqt = [[None] * (hr // COLS) for _ in x_refs]
    units = [
        (c, b, n)
        for c in range(0, len(slots), group)
        for b in range(len(x_refs))
        for n in range(hr // COLS)
    ]
    dk = dv = None
    ahead = products(*units[0])
    for at, (c, b, n) in enumerate(units):
        q, g, st, dpt = ahead
        if at + 1 < len(units):
            ahead = products(*units[at + 1])
        p, d = weights(c, b, n, st, dpt)
        dv, dk = plus(dv, dot(p, g)), plus(dk, dot(d, q))
        dqt[b][n] = plus(dqt[b][n], dot(chunk(c)[2], d))
        if at + 1 < len(units) and units[at + 1][0] == c:
            continue
        for j, slot in enumerate(slots[c : c + group]):
            dk_j, dv_j = dk[j * rows : (j + 1) * rows], dv[j * rows : (j + 1) * rows]
            if plan["acc"]:
                acc_ref, place = acc_refs[plan["at"][slot][0]], plan["at"][slot][1]
                dk_j += acc_ref[place, :rows, :]
                dv_j += acc_ref[place, rows:, :]
            dkv_ref[c + j, :rows, :] = dk_j.astype(dkv_ref.dtype)
            dkv_ref[c + j, rows:, :] = dv_j.astype(dkv_ref.dtype)
        dk = dv = None
    for b, dq_ref in enumerate(dq_refs):
        for n in range(hr // COLS):
            cols = slice(n * COLS, (n + 1) * COLS)
            total = dqt[b][n] + dq_in[b][:, cols] if dq_in else dqt[b][n]
            dq_ref[:, cols] = total.astype(dq_ref.dtype)


def blocks_call(xs, kvs, slots, rows, heads, scale, dkv_type, dq_type, acc=(), dq_in=(), diagonal=False):
    sds = jax.ShapeDtypeStruct
    width = kvs[0].shape[1]
    xs = [x if isinstance(x, list) else [x] for x in xs]
    slots = list(slots)
    totals = []
    for a, _ in acc:
        if all(a is not t for t in totals):
            totals.append(a)
    at = [([a is t for t in totals].index(True), n) for a, n in acc]
    plan = {
        "parts": [len(x) for x in xs],
        "kv": len(kvs),
        "acc": len(totals),
        "at": at,
        "dq_in": len(dq_in),
        "slots": slots,
        "diagonal": diagonal,
    }
    args = (*sum(xs, []), *kvs, *totals, *dq_in)
    types = dq_type if isinstance(dq_type, list) else [dq_type] * len(xs)
    outs = tuple(sds((width, heads * rows), t) for t in types)
    outs += (sds((len(slots), 2 * rows, width), dkv_type),)
    return pl.pallas_call(
        functools.partial(blocks_kernel, plan, rows, heads, scale),
        out_shape=outs,
        in_specs=[VMEM] * len(args),
        out_specs=(VMEM,) * len(outs),
        compiler_params=SMALL,
        cost_estimate=QUICK,
    )(*args)


def add_kernel(start, own_ref, got_ref, *refs):
    for n, ref in enumerate(refs):
        ref[...] = (own_ref[n] + got_ref[start + n].astype(F32)).astype(ref.dtype)


def add_call(own, got, start, types):
    return pl.pallas_call(
        functools.partial(add_kernel, start),
        out_shape=tuple(jax.ShapeDtypeStruct(own.shape[1:], t) for t in types),
        in_specs=[VMEM] * 2,
        out_specs=(VMEM,) * len(types),
        compiler_params=SMALL,
        cost_estimate=QUICK,
    )(own, got)


def sum_kernel(own_ref, *refs):
    total = own_ref[...]
    for ref in refs[:-1]:
        total = total + ref[...].astype(F32)
    refs[-1][...] = total


def sum_call(own, got, flops):
    return pl.pallas_call(
        sum_kernel,
        out_shape=jax.ShapeDtypeStruct(own.shape, F32),
        in_specs=[VMEM] * (1 + len(got)),
        out_specs=VMEM,
        compiler_params=SMALL,
        cost_estimate=pl.CostEstimate(flops=flops, bytes_accessed=1000, transcendentals=0),
    )(own, *got)


def final_kernel(rows, heads, scale, dq_ref, dq_far, dkv_ref, *refs):
    late, (gq_ref, gk_ref, gv_ref) = refs[:-3], refs[-3:]
    dkv = dkv_ref[...]
    for ref in late:
        dkv = dkv + ref[...].astype(F32)
    gk_ref[...] = (scale * dkv[:rows]).astype(BF)
    gv_ref[...] = dkv[rows:].astype(BF)
    dq = dq_ref[...] + dq_far[...].astype(F32)
    for h in range(heads):
        part = dq[:, h * rows : (h + 1) * rows]
        gq_ref[:, h * 128 : (h + 1) * 128] = (scale * part).T.astype(BF)


def crossed(block, t, other):
    pairs = []
    for i in range(lax.axis_size("inner")):
        chip, core = i // 2, i % 2
        pairs.append((i, 2 * (chip ^ (2 * t + (core if other else 1 - core))) + core))
    return lax.ppermute(block, "inner", pairs)


def on_device(query, key, value, out, grad_out, lse, positions):
    rows, width = key.shape
    heads = query.shape[1] // width
    hr = heads * rows
    scale = width ** (-0.5)
    nq = lax.axis_size("outer")
    nz = lax.axis_size("inner") // 2
    sds = jax.ShapeDtypeStruct
    inputs = (query, key, value, out, grad_out, lse, positions[None, :])
    x, kv = pl.pallas_call(
        pack_kernel,
        out_shape=(sds((2 * hr + 32, width), BF), sds((2 * rows + 16, width), BF)),
        in_specs=[pl.BlockSpec(memory_space=pltpu.HBM)] * 7,
        out_specs=(VMEM, VMEM),
        scratch_shapes=[
            pltpu.VMEM(out.shape, BF),
            pltpu.VMEM(lse.shape, F32),
            pltpu.VMEM((1, rows), jnp.int32),
            pltpu.SemaphoreType.DMA((5 + 2 * heads,)),
        ],
        compiler_params=SMALL,
        cost_estimate=QUICK,
    )(*[pltpu.with_memory_space_constraint(a, pltpu.HBM) for a in inputs])

    common = (rows, heads, scale)
    sib = swapped(kv, "inner", 1)
    near = swapped(kv, "inner", 2)
    direct = [crossed(block, t, False) for t in range(1, nz // 2) for block in (kv, sib)]
    early = [kv, sib, near]
    dq_own, acc = blocks_call([x], early, range(3), *common, F32, F32, diagonal=True)

    xs = [swapped(x, "outer", s) for s in range(1, nq - 1)]
    dqs = [dq_own]
    for s in range(nq - 2):
        xs[s], acc = lax.optimization_barrier((xs[s], acc))
        dq, acc = blocks_call([xs[s]], early, range(3), *common, F32, F32, acc=[(acc, n) for n in range(3)])
        dqs.append(dq)
    halves = [xs[nq - 3][:hr], xs[((nq - 1) ^ (nq // 2)) - 1][hr:]]
    corner = [swapped(halves[0], "outer", 1), swapped(halves[1], "outer", nq // 2)]

    *direct, acc = lax.optimization_barrier((*direct, acc))
    traded = [swapped(block, "inner", 1) for block in direct]
    direct = [swapped(near, "inner", 1), *direct]
    xs = [x, *xs]
    n_d, n_t = len(direct), len(traded)
    *dqs, acc_d = blocks_call(xs, direct, range(n_d), *common, F32, F32, dq_in=dqs)
    types = [F32] + [BF] * (nq - 2)
    dq_own, *dqs, acc_t = blocks_call(xs, traded, range(n_t), *common, F32, types, dq_in=dqs)

    arrays = [*early, *direct, *traded]
    accs = [(a, n) for a, count in ((acc, 3), (acc_d, n_d), (acc_t, n_t)) for n in range(count)]
    theirs, ours = [1, 3], [0, 2]
    for t in range(0, n_t, 2):
        theirs += [3 + n_d + t, 4 + t + 1]
        ours += [4 + t, 3 + n_d + t + 1]
    dq_last, dkv_sib = blocks_call([corner], arrays, theirs, *common, BF, F32, acc=accs)
    dkv_got = swapped(dkv_sib, "inner", 1)
    dq_last, dkv_far = blocks_call([corner], arrays, ours[2:], *common, F32, F32, acc=accs, dq_in=[dq_last])
    dq_last, dkv_own = blocks_call([corner], arrays, ours[:2], *common, F32, BF, acc=accs, dq_in=[dq_last])
    far = add_call(dkv_far, dkv_got, 2, [BF] * (nz - 2))
    dkv_own, dkv_near = add_call(dkv_own, dkv_got, 0, [F32, BF])

    got = [swapped(dq, "outer", s + 1) for s, dq in enumerate(dqs)]
    dq_far = swapped(dq_last, "outer", nq - 1)
    dkv = [crossed(far[2 * t - 2], t, False) for t in range(1, nz // 2)]
    late = [crossed(far[2 * t - 1], t, True) for t in range(1, nz // 2)]
    late.append(swapped(dkv_near, "inner", 2))

    dkv_sum = sum_call(dkv_own, dkv, 1_500_000_000)
    dq_sum = sum_call(dq_own, got, 100_000_000)
    return pl.pallas_call(
        functools.partial(final_kernel, rows, heads, scale),
        out_shape=(sds((rows, heads * width), BF), sds((rows, width), BF), sds((rows, width), BF)),
        in_specs=[VMEM] * (3 + len(late)),
        out_specs=(VMEM,) * 3,
        compiler_params=SMALL,
        cost_estimate=QUICK,
    )(dq_sum, dq_far, dkv_sum, *late)


def solution(mesh):
    tokens = P(("outer", "inner"), None)
    return jax.shard_map(
        on_device,
        mesh=mesh,
        in_specs=(tokens,) * 5 + (P(None, ("outer", "inner")), P(("outer", "inner"))),
        out_specs=(tokens,) * 3,
        check_vma=False,
    )
```

```python
import functools
import math

import jax
import jax.numpy as jnp
from jax import lax
from jax.experimental import pallas as pl
from jax.experimental.pallas import tpu as pltpu
from jax.sharding import PartitionSpec as P

BF = jnp.bfloat16
F32 = jnp.float32
RUN = 64
LOG2E = math.log2(math.e)
VMEM = pl.BlockSpec(memory_space=pltpu.VMEM)
SMALL = pltpu.CompilerParams(vmem_limit_bytes=16 * 1024 * 1024)
NN = (((1,), (0,)), ((), ()))
NT = (((1,), (1,)), ((), ()))
QUICK = pl.CostEstimate(flops=1000, bytes_accessed=1000, transcendentals=0)
COLS = 512


def swapped(block, axis, mask):
    pairs = [(i, i ^ mask) for i in range(lax.axis_size(axis))]
    return lax.ppermute(block, axis, pairs)


def three_parts(x):
    hi = x.astype(BF)
    rest = x - hi.astype(F32)
    mid = rest.astype(BF)
    low = (rest - mid.astype(F32)).astype(BF)
    return [hi, mid, low]


def dot(a, b, dims=NN):
    return lax.dot_general(a, b, dims, preferred_element_type=F32)


def pack_kernel(q_ref, k_ref, v_ref, o_ref, g_ref, lse_ref, pos_ref, x_ref, kv_ref, o_s, lse_s, pos_s, sems):
    rows, width = k_ref.shape
    heads = q_ref.shape[1] // width
    moves = [(lse_ref, lse_s), (pos_ref, pos_s), (o_ref, o_s)]
    for h in range(heads):
        cols = pl.ds(h * width, width)
        moves.append((g_ref.at[:, cols], x_ref.at[pl.ds((heads + h) * rows, rows), :]))
    for h in range(heads):
        cols = pl.ds(h * width, width)
        moves.append((q_ref.at[:, cols], x_ref.at[pl.ds(h * rows, rows), :]))
    moves.append((k_ref, kv_ref.at[pl.ds(0, rows), :]))
    moves.append((v_ref, kv_ref.at[pl.ds(rows, rows), :]))
    copies = [pltpu.make_async_copy(a, b, sems.at[n]) for n, (a, b) in enumerate(moves)]
    for copy in copies:
        copy.start()
    for copy in copies[: 3 + heads]:
        copy.wait()
    ones = jnp.ones((8, width), BF)
    deltas = []
    for h in range(heads):
        g = x_ref[(heads + h) * rows : (heads + h + 1) * rows, :]
        prod = g.astype(F32) * o_s[:, h * width : (h + 1) * width].astype(F32)
        hi = prod.astype(BF)
        low = (prod - hi.astype(F32)).astype(BF)
        deltas.append((dot(ones, hi, NT) + dot(ones, low, NT))[:1])
    run = (pos_s[...] // RUN).astype(F32)
    extra = (
        three_parts(lse_s[...] * LOG2E)
        + three_parts(jnp.concatenate(deltas, axis=0))
        + [run.astype(BF), jnp.zeros((32 - 6 * heads - 1, rows), BF)]
    )
    x_ref[2 * heads * rows :, :] = jnp.concatenate([e.astype(F32) for e in extra], axis=0).astype(BF)
    lane = lax.broadcasted_iota(jnp.int32, run.shape, 1)
    ids = [
        jnp.max(jnp.where(lane == r * RUN, run, 0.0), axis=1, keepdims=True)
        for r in range(rows // RUN)
    ]
    wide = [jnp.broadcast_to(i, (1, width)) for i in ids]
    wide.append(jnp.zeros((16 - len(ids), width), F32))
    kv_ref[2 * rows :, :] = jnp.concatenate(wide, axis=0).astype(BF)
    for copy in copies[3 + heads :]:
        copy.wait()


def blocks_kernel(plan, rows, heads, scale, *refs):
    refs = list(refs)
    x_refs = [[refs.pop(0) for _ in range(parts)] for parts in plan["parts"]]
    kv_refs = [refs.pop(0) for _ in range(plan["kv"])]
    acc_refs = [refs.pop(0) for _ in range(plan["acc"])]
    dq_in = [refs.pop(0) for _ in range(plan["dq_in"])]
    dq_refs, dkv_ref = refs[:-1], refs[-1]
    width = x_refs[0][0].shape[1]
    hr = heads * rows

    def taken(b, start, stop):
        first, cut = x_refs[b][0], x_refs[b][0].shape[0]
        if stop <= cut:
            return first[start:stop, :]
        rest = x_refs[b][1]
        if start >= cut:
            return rest[start - cut : stop - cut, :]
        return jnp.concatenate([first[start:, :], rest[: stop - cut, :]], axis=0)

    per = rows // RUN
    step = COLS // rows
    slots = plan["slots"]
    rowed = []
    for b in range(len(x_refs)):
        e = taken(b, 2 * hr, 2 * hr + 32).astype(F32)
        lse = e[0:heads] + e[heads : 2 * heads] + e[2 * heads : 3 * heads]
        delta = e[3 * heads : 4 * heads] + e[4 * heads : 5 * heads] + e[5 * heads : 6 * heads]
        rowed.append((lse, delta, e[6 * heads : 6 * heads + 1]))
    group = 3 if len(slots) == 3 else 2
    loaded = {}

    def chunk(c):
        if c not in loaded:
            ks, vs, runs = [], [], []
            for n in slots[c : c + group]:
                ks.append(kv_refs[n][:rows, :])
                vs.append(kv_refs[n][rows : 2 * rows, :])
                e = kv_refs[n][2 * rows :, :].astype(F32)
                runs += [e[r : r + 1] for r in range(per)]
            kt = jnp.concatenate([b.astype(F32).T.astype(BF) for b in ks], axis=1)
            loaded[c] = (jnp.concatenate(ks, axis=0), jnp.concatenate(vs, axis=0), kt, runs)
        return loaded[c]

    def products(c, b, n):
        k, v, _, _ = chunk(c)
        q = taken(b, n * COLS, (n + 1) * COLS)
        g = taken(b, hr + n * COLS, hr + (n + 1) * COLS)
        return q, g, dot(k, q, NT), dot(v, g, NT)

    def weights(c, b, n, st, dpt):
        lse, delta, run = rowed[b]
        p_rows, d_rows = [], []
        for r, krun in enumerate(chunk(c)[3]):
            sl = slice(r * RUN, (r + 1) * RUN)
            p_heads, d_heads = [], []
            for h in range(step):
                hl = slice(h * rows, (h + 1) * rows)
                head = n * step + h
                row = jnp.where(krun <= run, lse[head : head + 1], 1e30)
                arg = st[sl, hl] * (scale * LOG2E) - row
                if plan["diagonal"] and b == 0 and c == 0 and r < per:
                    i = lax.broadcasted_iota(jnp.int32, (RUN, rows), 1) - r * RUN
                    j = lax.broadcasted_iota(jnp.int32, (RUN, rows), 0)
                    arg = jnp.where((i >= 0) & (i < j), -1e30, arg)
                p = jnp.exp2(arg)
                p_heads.append(p.astype(BF))
                d_heads.append((p * (dpt[sl, hl] - delta[head : head + 1])).astype(BF))
            p_rows.append(jnp.concatenate(p_heads, axis=1))
            d_rows.append(jnp.concatenate(d_heads, axis=1))
        return jnp.concatenate(p_rows, axis=0), jnp.concatenate(d_rows, axis=0)

    def plus(total, part):
        return part if total is None else total + part

    dqt = [[None] * (hr // COLS) for _ in x_refs]
    units = [
        (c, b, n)
        for c in range(0, len(slots), group)
        for b in range(len(x_refs))
        for n in range(hr // COLS)
    ]
    dk = dv = None
    ahead = products(*units[0])
    for at, (c, b, n) in enumerate(units):
        q, g, st, dpt = ahead
        if at + 1 < len(units):
            ahead = products(*units[at + 1])
        p, d = weights(c, b, n, st, dpt)
        dv, dk = plus(dv, dot(p, g)), plus(dk, dot(d, q))
        dqt[b][n] = plus(dqt[b][n], dot(chunk(c)[2], d))
        if at + 1 < len(units) and units[at + 1][0] == c:
            continue
        for j, slot in enumerate(slots[c : c + group]):
            dk_j, dv_j = dk[j * rows : (j + 1) * rows], dv[j * rows : (j + 1) * rows]
            if plan["acc"]:
                acc_ref, place = acc_refs[plan["at"][slot][0]], plan["at"][slot][1]
                dk_j += acc_ref[place, :rows, :]
                dv_j += acc_ref[place, rows:, :]
            dkv_ref[c + j, :rows, :] = dk_j.astype(dkv_ref.dtype)
            dkv_ref[c + j, rows:, :] = dv_j.astype(dkv_ref.dtype)
        dk = dv = None
    for b, dq_ref in enumerate(dq_refs):
        for n in range(hr // COLS):
            cols = slice(n * COLS, (n + 1) * COLS)
            total = dqt[b][n] + dq_in[b][:, cols] if dq_in else dqt[b][n]
            dq_ref[:, cols] = total.astype(dq_ref.dtype)


def blocks_call(xs, kvs, slots, rows, heads, scale, dkv_type, dq_type, acc=(), dq_in=(), diagonal=False):
    sds = jax.ShapeDtypeStruct
    width = kvs[0].shape[1]
    xs = [x if isinstance(x, list) else [x] for x in xs]
    slots = list(slots)
    totals = []
    for a, _ in acc:
        if all(a is not t for t in totals):
            totals.append(a)
    at = [([a is t for t in totals].index(True), n) for a, n in acc]
    plan = {
        "parts": [len(x) for x in xs],
        "kv": len(kvs),
        "acc": len(totals),
        "at": at,
        "dq_in": len(dq_in),
        "slots": slots,
        "diagonal": diagonal,
    }
    args = (*sum(xs, []), *kvs, *totals, *dq_in)
    types = dq_type if isinstance(dq_type, list) else [dq_type] * len(xs)
    outs = tuple(sds((width, heads * rows), t) for t in types)
    outs += (sds((len(slots), 2 * rows, width), dkv_type),)
    return pl.pallas_call(
        functools.partial(blocks_kernel, plan, rows, heads, scale),
        out_shape=outs,
        in_specs=[VMEM] * len(args),
        out_specs=(VMEM,) * len(outs),
        compiler_params=SMALL,
        cost_estimate=QUICK,
    )(*args)


def add_kernel(start, own_ref, got_ref, *refs):
    for n, ref in enumerate(refs):
        ref[...] = (own_ref[n] + got_ref[start + n].astype(F32)).astype(ref.dtype)


def add_call(own, got, start, types):
    return pl.pallas_call(
        functools.partial(add_kernel, start),
        out_shape=tuple(jax.ShapeDtypeStruct(own.shape[1:], t) for t in types),
        in_specs=[VMEM] * 2,
        out_specs=(VMEM,) * len(types),
        compiler_params=SMALL,
        cost_estimate=QUICK,
    )(own, got)


def sum_kernel(own_ref, *refs):
    total = own_ref[...]
    for ref in refs[:-1]:
        total = total + ref[...].astype(F32)
    refs[-1][...] = total


def sum_call(own, got, flops):
    return pl.pallas_call(
        sum_kernel,
        out_shape=jax.ShapeDtypeStruct(own.shape, F32),
        in_specs=[VMEM] * (1 + len(got)),
        out_specs=VMEM,
        compiler_params=SMALL,
        cost_estimate=pl.CostEstimate(flops=flops, bytes_accessed=1000, transcendentals=0),
    )(own, *got)


def final_kernel(rows, heads, scale, dq_ref, dq_far, dkv_ref, dkv_near, gq_ref, gk_ref, gv_ref):
    dkv = dkv_ref[...] + dkv_near[...].astype(F32)
    gk_ref[...] = (scale * dkv[:rows]).astype(BF)
    gv_ref[...] = dkv[rows:].astype(BF)
    dq = dq_ref[...] + dq_far[...].astype(F32)
    for h in range(heads):
        part = dq[:, h * rows : (h + 1) * rows]
        gq_ref[:, h * 128 : (h + 1) * 128] = (scale * part).T.astype(BF)


def crossed(block, t, other):
    pairs = []
    for i in range(lax.axis_size("inner")):
        chip, core = i // 2, i % 2
        pairs.append((i, 2 * (chip ^ (2 * t + (core if other else 1 - core))) + core))
    return lax.ppermute(block, "inner", pairs)


def on_device(query, key, value, out, grad_out, lse, positions):
    rows, width = key.shape
    heads = query.shape[1] // width
    hr = heads * rows
    scale = width ** (-0.5)
    nq = lax.axis_size("outer")
    nz = lax.axis_size("inner") // 2
    sds = jax.ShapeDtypeStruct
    inputs = (query, key, value, out, grad_out, lse, positions[None, :])
    x, kv = pl.pallas_call(
        pack_kernel,
        out_shape=(sds((2 * hr + 32, width), BF), sds((2 * rows + 16, width), BF)),
        in_specs=[pl.BlockSpec(memory_space=pltpu.HBM)] * 7,
        out_specs=(VMEM, VMEM),
        scratch_shapes=[
            pltpu.VMEM(out.shape, BF),
            pltpu.VMEM(lse.shape, F32),
            pltpu.VMEM((1, rows), jnp.int32),
            pltpu.SemaphoreType.DMA((5 + 2 * heads,)),
        ],
        compiler_params=SMALL,
        cost_estimate=QUICK,
    )(*[pltpu.with_memory_space_constraint(a, pltpu.HBM) for a in inputs])

    common = (rows, heads, scale)
    sib = swapped(kv, "inner", 1)
    near = swapped(kv, "inner", 2)
    direct = [crossed(block, t, False) for t in range(1, nz // 2) for block in (kv, sib)]
    early = [kv, sib, near]
    dq_own, acc = blocks_call([x], early, range(3), *common, F32, F32, diagonal=True)

    cut = hr + 32
    top, acc = lax.optimization_barrier((x[:cut], acc))
    xs = [swapped(x, "outer", s) for s in range(1, nq - 1)]
    dqs = [dq_own]
    for s in range(nq - 2):
        xs[s], acc = lax.optimization_barrier((xs[s], acc))
        dq, acc = blocks_call([xs[s]], early, range(3), *common, F32, F32, acc=[(acc, n) for n in range(3)])
        dqs.append(dq)
    passed = xs[((nq - 1) ^ (nq // 2)) - 1][cut:]
    corner = [swapped(top, "outer", nq - 1), swapped(passed, "outer", nq // 2)]

    *direct, acc = lax.optimization_barrier((*direct, acc))
    traded = [swapped(block, "inner", 1) for block in direct]
    direct = [swapped(near, "inner", 1), *direct]
    xs = [x, *xs]
    n_d, n_t = len(direct), len(traded)
    *dqs, acc_d = blocks_call(xs, direct, range(n_d), *common, F32, F32, dq_in=dqs)
    types = [F32] + [BF] * (nq - 2)
    dq_own, *dqs, acc_t = blocks_call(xs, traded, range(n_t), *common, F32, types, dq_in=dqs)

    arrays = [*early, *direct, *traded]
    accs = [(a, n) for a, count in ((acc, 3), (acc_d, n_d), (acc_t, n_t)) for n in range(count)]
    theirs, ours = [1, 3], [0, 2]
    for t in range(0, n_t, 2):
        theirs += [3 + n_d + t, 4 + t + 1]
        ours += [4 + t, 3 + n_d + t + 1]
    dq_last, dkv_sib = blocks_call([corner], arrays, theirs, *common, BF, F32, acc=accs)
    dkv_got = swapped(dkv_sib, "inner", 1)
    dq_last, dkv_far = blocks_call([corner], arrays, ours[2:], *common, F32, F32, acc=accs, dq_in=[dq_last])
    dq_last, dkv_own = blocks_call([corner], arrays, ours[:2], *common, F32, BF, acc=accs, dq_in=[dq_last])
    far = add_call(dkv_far, dkv_got, 2, [BF] * (nz - 2))
    dkv_own, dkv_near = add_call(dkv_own, dkv_got, 0, [F32, BF])

    got = [swapped(dq, "outer", s + 1) for s, dq in enumerate(dqs)]
    dq_far = swapped(dq_last, "outer", nq - 1)
    dkv = []
    for t in range(1, nz // 2):
        dkv.append(crossed(far[2 * t - 2], t, False))
        dkv.append(crossed(far[2 * t - 1], t, True))
    dkv_near = swapped(dkv_near, "inner", 2)

    dkv_sum = sum_call(dkv_own, dkv, 1_500_000_000)
    dq_sum = sum_call(dq_own, got, 100_000_000)
    return pl.pallas_call(
        functools.partial(final_kernel, rows, heads, scale),
        out_shape=(sds((rows, heads * width), BF), sds((rows, width), BF), sds((rows, width), BF)),
        in_specs=[VMEM] * 4,
        out_specs=(VMEM,) * 3,
        compiler_params=SMALL,
        cost_estimate=QUICK,
    )(dq_sum, dq_far, dkv_sum, dkv_near)


def solution(mesh):
    tokens = P(("outer", "inner"), None)
    return jax.shard_map(
        on_device,
        mesh=mesh,
        in_specs=(tokens,) * 5 + (P(None, ("outer", "inner")), P(("outer", "inner"))),
        out_specs=(tokens,) * 3,
        check_vma=False,
    )
```

```python
import functools
import math

import jax
import jax.numpy as jnp
from jax import lax
from jax.experimental import pallas as pl
from jax.experimental.pallas import tpu as pltpu
from jax.sharding import PartitionSpec as P

BF = jnp.bfloat16
F32 = jnp.float32
RUN = 64
LOG2E = math.log2(math.e)
VMEM = pl.BlockSpec(memory_space=pltpu.VMEM)
SMALL = pltpu.CompilerParams(vmem_limit_bytes=16 * 1024 * 1024)
NN = (((1,), (0,)), ((), ()))
NT = (((1,), (1,)), ((), ()))
QUICK = pl.CostEstimate(flops=1000, bytes_accessed=1000, transcendentals=0)
COLS = 512


def swapped(block, axis, mask):
    pairs = [(i, i ^ mask) for i in range(lax.axis_size(axis))]
    return lax.ppermute(block, axis, pairs)


def three_parts(x):
    hi = x.astype(BF)
    rest = x - hi.astype(F32)
    mid = rest.astype(BF)
    low = (rest - mid.astype(F32)).astype(BF)
    return [hi, mid, low]


def dot(a, b, dims=NN):
    return lax.dot_general(a, b, dims, preferred_element_type=F32)


def pack_kernel(q_ref, k_ref, v_ref, o_ref, g_ref, lse_ref, pos_ref, x_ref, kv_ref, o_s, lse_s, pos_s, sems):
    rows, width = k_ref.shape
    heads = q_ref.shape[1] // width
    moves = [(lse_ref, lse_s), (pos_ref, pos_s), (o_ref, o_s)]
    for h in range(heads):
        cols = pl.ds(h * width, width)
        moves.append((g_ref.at[:, cols], x_ref.at[pl.ds((heads + h) * rows, rows), :]))
    for h in range(heads):
        cols = pl.ds(h * width, width)
        moves.append((q_ref.at[:, cols], x_ref.at[pl.ds(h * rows, rows), :]))
    moves.append((k_ref, kv_ref.at[pl.ds(0, rows), :]))
    moves.append((v_ref, kv_ref.at[pl.ds(rows, rows), :]))
    copies = [pltpu.make_async_copy(a, b, sems.at[n]) for n, (a, b) in enumerate(moves)]
    for copy in copies:
        copy.start()
    for copy in copies[: 3 + heads]:
        copy.wait()
    ones = jnp.ones((8, width), BF)
    deltas = []
    for h in range(heads):
        g = x_ref[(heads + h) * rows : (heads + h + 1) * rows, :]
        prod = g.astype(F32) * o_s[:, h * width : (h + 1) * width].astype(F32)
        hi = prod.astype(BF)
        low = (prod - hi.astype(F32)).astype(BF)
        deltas.append((dot(ones, hi, NT) + dot(ones, low, NT))[:1])
    run = (pos_s[...] // RUN).astype(F32)
    extra = (
        three_parts(lse_s[...] * LOG2E)
        + three_parts(jnp.concatenate(deltas, axis=0))
        + [run.astype(BF), jnp.zeros((32 - 6 * heads - 1, rows), BF)]
    )
    x_ref[2 * heads * rows :, :] = jnp.concatenate([e.astype(F32) for e in extra], axis=0).astype(BF)
    lane = lax.broadcasted_iota(jnp.int32, run.shape, 1)
    ids = [
        jnp.max(jnp.where(lane == r * RUN, run, 0.0), axis=1, keepdims=True)
        for r in range(rows // RUN)
    ]
    wide = [jnp.broadcast_to(i, (1, width)) for i in ids]
    wide.append(jnp.zeros((16 - len(ids), width), F32))
    kv_ref[2 * rows :, :] = jnp.concatenate(wide, axis=0).astype(BF)
    for copy in copies[3 + heads :]:
        copy.wait()


def blocks_kernel(plan, rows, heads, scale, *refs):
    refs = list(refs)
    x_refs = []
    for parts in plan["parts"]:
        whole = refs.pop(0)
        x_refs.append((whole, whole.at[heads * rows :, :] if parts == 1 else refs.pop(0)))
    kv_refs = [refs.pop(0) for _ in range(plan["kv"])]
    acc_refs = [refs.pop(0) for _ in range(plan["acc"])]
    dq_in = [refs.pop(0) for _ in range(plan["dq_in"])]
    dq_refs, dkv_ref = refs[:-1], refs[-1]
    width = x_refs[0][0].shape[1]
    hr = heads * rows
    per = rows // RUN
    step = COLS // rows
    slots = plan["slots"]
    rowed = []
    for _, g_ref in x_refs:
        e = g_ref[hr:, :].astype(F32)
        lse = e[0:heads] + e[heads : 2 * heads] + e[2 * heads : 3 * heads]
        delta = e[3 * heads : 4 * heads] + e[4 * heads : 5 * heads] + e[5 * heads : 6 * heads]
        rowed.append((lse, delta, e[6 * heads : 6 * heads + 1]))
    group = 3 if len(slots) == 3 else 2
    loaded = {}

    def chunk(c):
        if c not in loaded:
            ks, vs, runs = [], [], []
            for n in slots[c : c + group]:
                ks.append(kv_refs[n][:rows, :])
                vs.append(kv_refs[n][rows : 2 * rows, :])
                e = kv_refs[n][2 * rows :, :].astype(F32)
                runs += [e[r : r + 1] for r in range(per)]
            kt = jnp.concatenate([b.astype(F32).T.astype(BF) for b in ks], axis=1)
            loaded[c] = (jnp.concatenate(ks, axis=0), jnp.concatenate(vs, axis=0), kt, runs)
        return loaded[c]

    def products(c, b, n):
        k, v, _, _ = chunk(c)
        q_ref, g_ref = x_refs[b]
        q = q_ref[n * COLS : (n + 1) * COLS, :]
        g = g_ref[n * COLS : (n + 1) * COLS, :]
        return q, g, dot(k, q, NT), dot(v, g, NT)

    def weights(c, b, n, st, dpt):
        lse, delta, run = rowed[b]
        p_rows, d_rows = [], []
        for r, krun in enumerate(chunk(c)[3]):
            sl = slice(r * RUN, (r + 1) * RUN)
            p_heads, d_heads = [], []
            for h in range(step):
                hl = slice(h * rows, (h + 1) * rows)
                head = n * step + h
                row = jnp.where(krun <= run, lse[head : head + 1], 1e30)
                arg = st[sl, hl] * (scale * LOG2E) - row
                if plan["diagonal"] and b == 0 and c == 0 and r < per:
                    i = lax.broadcasted_iota(jnp.int32, (RUN, rows), 1) - r * RUN
                    j = lax.broadcasted_iota(jnp.int32, (RUN, rows), 0)
                    arg = jnp.where((i >= 0) & (i < j), -1e30, arg)
                p = jnp.exp2(arg)
                p_heads.append(p.astype(BF))
                d_heads.append((p * (dpt[sl, hl] - delta[head : head + 1])).astype(BF))
            p_rows.append(jnp.concatenate(p_heads, axis=1))
            d_rows.append(jnp.concatenate(d_heads, axis=1))
        return jnp.concatenate(p_rows, axis=0), jnp.concatenate(d_rows, axis=0)

    def plus(total, part):
        return part if total is None else total + part

    dqt = [[None] * (hr // COLS) for _ in x_refs]
    units = [
        (c, b, n)
        for c in range(0, len(slots), group)
        for b in range(len(x_refs))
        for n in range(hr // COLS)
    ]
    dk = dv = None
    ahead = products(*units[0])
    for at, (c, b, n) in enumerate(units):
        q, g, st, dpt = ahead
        if at + 1 < len(units):
            ahead = products(*units[at + 1])
        p, d = weights(c, b, n, st, dpt)
        dv, dk = plus(dv, dot(p, g)), plus(dk, dot(d, q))
        dqt[b][n] = plus(dqt[b][n], dot(chunk(c)[2], d))
        if at + 1 < len(units) and units[at + 1][0] == c:
            continue
        for j, slot in enumerate(slots[c : c + group]):
            dk_j, dv_j = dk[j * rows : (j + 1) * rows], dv[j * rows : (j + 1) * rows]
            if plan["acc"]:
                acc_ref, place = acc_refs[plan["at"][slot][0]], plan["at"][slot][1]
                dk_j += acc_ref[place, :rows, :]
                dv_j += acc_ref[place, rows:, :]
            dkv_ref[c + j, :rows, :] = dk_j.astype(dkv_ref.dtype)
            dkv_ref[c + j, rows:, :] = dv_j.astype(dkv_ref.dtype)
        dk = dv = None
    for b, dq_ref in enumerate(dq_refs):
        for n in range(hr // COLS):
            cols = slice(n * COLS, (n + 1) * COLS)
            total = dqt[b][n] + dq_in[b][:, cols] if dq_in else dqt[b][n]
            dq_ref[:, cols] = total.astype(dq_ref.dtype)


def blocks_call(xs, kvs, slots, rows, heads, scale, dkv_type, dq_type, acc=(), dq_in=(), diagonal=False):
    sds = jax.ShapeDtypeStruct
    width = kvs[0].shape[1]
    xs = [x if isinstance(x, list) else [x] for x in xs]
    slots = list(slots)
    totals = []
    for a, _ in acc:
        if all(a is not t for t in totals):
            totals.append(a)
    at = [([a is t for t in totals].index(True), n) for a, n in acc]
    plan = {
        "parts": [len(x) for x in xs],
        "kv": len(kvs),
        "acc": len(totals),
        "at": at,
        "dq_in": len(dq_in),
        "slots": slots,
        "diagonal": diagonal,
    }
    args = (*sum(xs, []), *kvs, *totals, *dq_in)
    types = dq_type if isinstance(dq_type, list) else [dq_type] * len(xs)
    outs = tuple(sds((width, heads * rows), t) for t in types)
    outs += (sds((len(slots), 2 * rows, width), dkv_type),)
    return pl.pallas_call(
        functools.partial(blocks_kernel, plan, rows, heads, scale),
        out_shape=outs,
        in_specs=[VMEM] * len(args),
        out_specs=(VMEM,) * len(outs),
        compiler_params=SMALL,
        cost_estimate=QUICK,
    )(*args)


def add_kernel(own_ref, got_ref, *refs):
    for n, ref in enumerate(refs):
        ref[...] = (own_ref[n] + got_ref[n].astype(F32)).astype(ref.dtype)


def add_call(own, got, types):
    return pl.pallas_call(
        add_kernel,
        out_shape=tuple(jax.ShapeDtypeStruct(own.shape[1:], t) for t in types),
        in_specs=[VMEM] * 2,
        out_specs=(VMEM,) * len(types),
        compiler_params=SMALL,
        cost_estimate=QUICK,
    )(own, got)


def sum_kernel(own_ref, *refs):
    total = own_ref[...]
    for ref in refs[:-1]:
        total = total + ref[...].astype(F32)
    refs[-1][...] = total


def sum_call(own, got, flops):
    return pl.pallas_call(
        sum_kernel,
        out_shape=jax.ShapeDtypeStruct(own.shape, F32),
        in_specs=[VMEM] * (1 + len(got)),
        out_specs=VMEM,
        compiler_params=SMALL,
        cost_estimate=pl.CostEstimate(flops=flops, bytes_accessed=1000, transcendentals=0),
    )(own, *got)


def final_kernel(rows, heads, scale, dq_ref, dkv_ref, dkv_near, *refs):
    got, (gq_ref, gk_ref, gv_ref) = refs[:-3], refs[-3:]
    dkv = dkv_ref[...] + dkv_near[...].astype(F32)
    gk_ref[...] = (scale * dkv[:rows]).astype(BF)
    gv_ref[...] = dkv[rows:].astype(BF)
    dq = dq_ref[...]
    for ref in got:
        dq = dq + ref[...].astype(F32)
    for h in range(heads):
        part = dq[:, h * rows : (h + 1) * rows]
        gq_ref[:, h * 128 : (h + 1) * 128] = (scale * part).T.astype(BF)


def crossed(block, t, other):
    pairs = []
    for i in range(lax.axis_size("inner")):
        chip, core = i // 2, i % 2
        pairs.append((i, 2 * (chip ^ (2 * t + (core if other else 1 - core))) + core))
    return lax.ppermute(block, "inner", pairs)


def on_device(query, key, value, out, grad_out, lse, positions):
    rows, width = key.shape
    heads = query.shape[1] // width
    hr = heads * rows
    scale = width ** (-0.5)
    nq = lax.axis_size("outer")
    nz = lax.axis_size("inner") // 2
    sds = jax.ShapeDtypeStruct
    inputs = (query, key, value, out, grad_out, lse, positions[None, :])
    x, kv = pl.pallas_call(
        pack_kernel,
        out_shape=(sds((2 * hr + 32, width), BF), sds((2 * rows + 16, width), BF)),
        in_specs=[pl.BlockSpec(memory_space=pltpu.HBM)] * 7,
        out_specs=(VMEM, VMEM),
        scratch_shapes=[
            pltpu.VMEM(out.shape, BF),
            pltpu.VMEM(lse.shape, F32),
            pltpu.VMEM((1, rows), jnp.int32),
            pltpu.SemaphoreType.DMA((5 + 2 * heads,)),
        ],
        compiler_params=SMALL,
        cost_estimate=QUICK,
    )(*[pltpu.with_memory_space_constraint(a, pltpu.HBM) for a in inputs])

    common = (rows, heads, scale)
    sib = swapped(kv, "inner", 1)
    near = swapped(kv, "inner", 2)
    direct = [crossed(block, t, False) for t in range(1, nz // 2) for block in (kv, sib)]
    early = [kv, sib, near]
    dq_own, acc = blocks_call([x], early, range(3), *common, F32, F32, diagonal=True)

    xs = [swapped(x, "outer", s) for s in range(1, nq - 1)]
    dqs = [dq_own]
    for s in range(nq - 2):
        xs[s], acc = lax.optimization_barrier((xs[s], acc))
        dq, acc = blocks_call([xs[s]], early, range(3), *common, F32, F32, acc=[(acc, n) for n in range(3)])
        dqs.append(dq)
    halves = [xs[nq - 3][:hr], xs[((nq - 1) ^ (nq // 2)) - 1][hr:]]
    corner = [swapped(halves[0], "outer", 1), swapped(halves[1], "outer", nq // 2)]

    *direct, acc = lax.optimization_barrier((*direct, acc))
    traded = [swapped(block, "inner", 1) for block in direct]
    direct = [swapped(near, "inner", 1), *direct]
    xs = [x, *xs]
    n_d, n_t = len(direct), len(traded)
    *dqs, acc_d = blocks_call(xs, direct, range(n_d), *common, F32, F32, dq_in=dqs)
    types = [F32] + [BF] * (nq - 2)
    dq_own, *dqs, acc_t = blocks_call(xs, traded, range(n_t), *common, F32, types, dq_in=dqs)

    arrays = [*early, *direct, *traded]
    accs = [(a, n) for a, count in ((acc, 3), (acc_d, n_d), (acc_t, n_t)) for n in range(count)]
    theirs, ours = [1, 3], [0, 2]
    for t in range(0, n_t, 2):
        theirs += [3 + n_d + t, 4 + t + 1]
        ours += [4 + t, 3 + n_d + t + 1]
    dq_last, dkv_sib = blocks_call([corner], arrays, theirs, *common, BF, F32, acc=accs)
    dkv_got = swapped(dkv_sib, "inner", 1)
    dq_last, dkv_own = blocks_call([corner], arrays, ours, *common, F32, BF, acc=accs, dq_in=[dq_last])
    dq_far = swapped(dq_last, "outer", nq - 1)
    dkv_own, dkv_near, *far = add_call(dkv_own, dkv_got, [F32] + [BF] * (nz - 1))
    got = [swapped(dq, "outer", s + 1) for s, dq in enumerate(dqs)]
    dkv = []
    for t in range(1, nz // 2):
        dkv.append(crossed(far[2 * t - 2], t, False))
        dkv.append(crossed(far[2 * t - 1], t, True))
    dkv_near = swapped(dkv_near, "inner", 2)

    dkv_sum = sum_call(dkv_own, dkv, 1_500_000_000)
    dq_sum = sum_call(dq_own, [dq_far], 100_000_000)
    return pl.pallas_call(
        functools.partial(final_kernel, rows, heads, scale),
        out_shape=(sds((rows, heads * width), BF), sds((rows, width), BF), sds((rows, width), BF)),
        in_specs=[VMEM] * (3 + len(got)),
        out_specs=(VMEM,) * 3,
        compiler_params=SMALL,
        cost_estimate=QUICK,
    )(dq_sum, dkv_sum, dkv_near, *got)


def solution(mesh):
    tokens = P(("outer", "inner"), None)
    return jax.shard_map(
        on_device,
        mesh=mesh,
        in_specs=(tokens,) * 5 + (P(None, ("outer", "inner")), P(("outer", "inner"))),
        out_specs=(tokens,) * 3,
        check_vma=False,
    )
```

```python
import functools
import math

import jax
import jax.numpy as jnp
from jax import lax
from jax.experimental import pallas as pl
from jax.experimental.pallas import tpu as pltpu
from jax.sharding import PartitionSpec as P

BF = jnp.bfloat16
F32 = jnp.float32
RUN = 64
LOG2E = math.log2(math.e)
VMEM = pl.BlockSpec(memory_space=pltpu.VMEM)
SMALL = pltpu.CompilerParams(vmem_limit_bytes=16 * 1024 * 1024)
NN = (((1,), (0,)), ((), ()))
NT = (((1,), (1,)), ((), ()))
QUICK = pl.CostEstimate(flops=1000, bytes_accessed=1000, transcendentals=0)
COLS = 512


def swapped(block, axis, mask):
    pairs = [(i, i ^ mask) for i in range(lax.axis_size(axis))]
    return lax.ppermute(block, axis, pairs)


def three_parts(x):
    hi = x.astype(BF)
    rest = x - hi.astype(F32)
    mid = rest.astype(BF)
    low = (rest - mid.astype(F32)).astype(BF)
    return [hi, mid, low]


def dot(a, b, dims=NN):
    return lax.dot_general(a, b, dims, preferred_element_type=F32)


def pack_kernel(q_ref, k_ref, v_ref, o_ref, g_ref, lse_ref, pos_ref, x_ref, kv_ref, o_s, lse_s, pos_s, sems):
    rows, width = k_ref.shape
    heads = q_ref.shape[1] // width
    moves = [(lse_ref, lse_s), (pos_ref, pos_s), (o_ref, o_s)]
    for h in range(heads):
        cols = pl.ds(h * width, width)
        moves.append((g_ref.at[:, cols], x_ref.at[pl.ds((heads + h) * rows, rows), :]))
    for h in range(heads):
        cols = pl.ds(h * width, width)
        moves.append((q_ref.at[:, cols], x_ref.at[pl.ds(h * rows, rows), :]))
    moves.append((k_ref, kv_ref.at[pl.ds(0, rows), :]))
    moves.append((v_ref, kv_ref.at[pl.ds(rows, rows), :]))
    copies = [pltpu.make_async_copy(a, b, sems.at[n]) for n, (a, b) in enumerate(moves)]
    for copy in copies:
        copy.start()
    for copy in copies[: 3 + heads]:
        copy.wait()
    ones = jnp.ones((8, width), BF)
    deltas = []
    for h in range(heads):
        g = x_ref[(heads + h) * rows : (heads + h + 1) * rows, :]
        prod = g.astype(F32) * o_s[:, h * width : (h + 1) * width].astype(F32)
        hi = prod.astype(BF)
        low = (prod - hi.astype(F32)).astype(BF)
        deltas.append((dot(ones, hi, NT) + dot(ones, low, NT))[:1])
    run = (pos_s[...] // RUN).astype(F32)
    extra = (
        three_parts(lse_s[...] * LOG2E)
        + three_parts(jnp.concatenate(deltas, axis=0))
        + [run.astype(BF), jnp.zeros((32 - 6 * heads - 1, rows), BF)]
    )
    x_ref[2 * heads * rows :, :] = jnp.concatenate([e.astype(F32) for e in extra], axis=0).astype(BF)
    lane = lax.broadcasted_iota(jnp.int32, run.shape, 1)
    ids = [
        jnp.max(jnp.where(lane == r * RUN, run, 0.0), axis=1, keepdims=True)
        for r in range(rows // RUN)
    ]
    wide = [jnp.broadcast_to(i, (1, width)) for i in ids]
    wide.append(jnp.zeros((16 - len(ids), width), F32))
    kv_ref[2 * rows :, :] = jnp.concatenate(wide, axis=0).astype(BF)
    for copy in copies[3 + heads :]:
        copy.wait()


def blocks_kernel(plan, rows, heads, scale, *refs):
    refs = list(refs)
    x_refs = []
    for parts in plan["parts"]:
        whole = refs.pop(0)
        x_refs.append((whole, whole.at[heads * rows :, :] if parts == 1 else refs.pop(0)))
    kv_refs = [refs.pop(0) for _ in range(plan["kv"])]
    acc_refs = [refs.pop(0) for _ in range(plan["acc"])]
    dq_in = [refs.pop(0) for _ in range(plan["dq_in"])]
    dq_refs, dkv_ref = refs[:-1], refs[-1]
    width = x_refs[0][0].shape[1]
    hr = heads * rows
    per = rows // RUN
    step = COLS // rows
    slots = plan["slots"]
    rowed = []
    for _, g_ref in x_refs:
        e = g_ref[hr:, :].astype(F32)
        lse = e[0:heads] + e[heads : 2 * heads] + e[2 * heads : 3 * heads]
        delta = e[3 * heads : 4 * heads] + e[4 * heads : 5 * heads] + e[5 * heads : 6 * heads]
        rowed.append((lse, delta, e[6 * heads : 6 * heads + 1]))
    group = 3 if len(slots) == 3 else 2
    loaded = {}

    def chunk(c):
        if c not in loaded:
            ks, vs, runs = [], [], []
            for n in slots[c : c + group]:
                ks.append(kv_refs[n][:rows, :])
                vs.append(kv_refs[n][rows : 2 * rows, :])
                e = kv_refs[n][2 * rows :, :].astype(F32)
                runs += [e[r : r + 1] for r in range(per)]
            kt = jnp.concatenate([b.astype(F32).T.astype(BF) for b in ks], axis=1)
            loaded[c] = (jnp.concatenate(ks, axis=0), jnp.concatenate(vs, axis=0), kt, runs)
        return loaded[c]

    def products(c, b, n):
        k, v, _, _ = chunk(c)
        q_ref, g_ref = x_refs[b]
        q = q_ref[n * COLS : (n + 1) * COLS, :]
        g = g_ref[n * COLS : (n + 1) * COLS, :]
        return q, g, dot(k, q, NT), dot(v, g, NT)

    def weights(c, b, n, st, dpt):
        lse, delta, run = rowed[b]
        p_rows, d_rows = [], []
        for r, krun in enumerate(chunk(c)[3]):
            sl = slice(r * RUN, (r + 1) * RUN)
            p_heads, d_heads = [], []
            for h in range(step):
                hl = slice(h * rows, (h + 1) * rows)
                head = n * step + h
                row = jnp.where(krun <= run, lse[head : head + 1], 1e30)
                arg = st[sl, hl] * (scale * LOG2E) - row
                if plan["diagonal"] and b == 0 and c == 0 and r < per:
                    i = lax.broadcasted_iota(jnp.int32, (RUN, rows), 1) - r * RUN
                    j = lax.broadcasted_iota(jnp.int32, (RUN, rows), 0)
                    arg = jnp.where((i >= 0) & (i < j), -1e30, arg)
                p = jnp.exp2(arg)
                p_heads.append(p.astype(BF))
                d_heads.append((p * (dpt[sl, hl] - delta[head : head + 1])).astype(BF))
            p_rows.append(jnp.concatenate(p_heads, axis=1))
            d_rows.append(jnp.concatenate(d_heads, axis=1))
        return jnp.concatenate(p_rows, axis=0), jnp.concatenate(d_rows, axis=0)

    def plus(total, part):
        return part if total is None else total + part

    dqt = [[None] * (hr // COLS) for _ in x_refs]
    units = [
        (c, b, n)
        for c in range(0, len(slots), group)
        for b in range(len(x_refs))
        for n in range(hr // COLS)
    ]
    dk = dv = None
    ahead = products(*units[0])
    for at, (c, b, n) in enumerate(units):
        q, g, st, dpt = ahead
        if at + 1 < len(units):
            ahead = products(*units[at + 1])
        p, d = weights(c, b, n, st, dpt)
        dv, dk = plus(dv, dot(p, g)), plus(dk, dot(d, q))
        dqt[b][n] = plus(dqt[b][n], dot(chunk(c)[2], d))
        if at + 1 < len(units) and units[at + 1][0] == c:
            continue
        for j, slot in enumerate(slots[c : c + group]):
            dk_j, dv_j = dk[j * rows : (j + 1) * rows], dv[j * rows : (j + 1) * rows]
            if plan["acc"]:
                acc_ref, place = acc_refs[plan["at"][slot][0]], plan["at"][slot][1]
                dk_j += acc_ref[place, :rows, :]
                dv_j += acc_ref[place, rows:, :]
            dkv_ref[c + j, :rows, :] = dk_j.astype(dkv_ref.dtype)
            dkv_ref[c + j, rows:, :] = dv_j.astype(dkv_ref.dtype)
        dk = dv = None
    for b, dq_ref in enumerate(dq_refs):
        for n in range(hr // COLS):
            cols = slice(n * COLS, (n + 1) * COLS)
            total = dqt[b][n] + dq_in[b][:, cols] if dq_in else dqt[b][n]
            dq_ref[:, cols] = total.astype(dq_ref.dtype)


def blocks_call(xs, kvs, slots, rows, heads, scale, dkv_type, dq_type, acc=(), dq_in=(), diagonal=False):
    sds = jax.ShapeDtypeStruct
    width = kvs[0].shape[1]
    xs = [x if isinstance(x, list) else [x] for x in xs]
    slots = list(slots)
    totals = []
    for a, _ in acc:
        if all(a is not t for t in totals):
            totals.append(a)
    at = [([a is t for t in totals].index(True), n) for a, n in acc]
    plan = {
        "parts": [len(x) for x in xs],
        "kv": len(kvs),
        "acc": len(totals),
        "at": at,
        "dq_in": len(dq_in),
        "slots": slots,
        "diagonal": diagonal,
    }
    args = (*sum(xs, []), *kvs, *totals, *dq_in)
    types = dq_type if isinstance(dq_type, list) else [dq_type] * len(xs)
    outs = tuple(sds((width, heads * rows), t) for t in types)
    outs += (sds((len(slots), 2 * rows, width), dkv_type),)
    return pl.pallas_call(
        functools.partial(blocks_kernel, plan, rows, heads, scale),
        out_shape=outs,
        in_specs=[VMEM] * len(args),
        out_specs=(VMEM,) * len(outs),
        compiler_params=SMALL,
        cost_estimate=QUICK,
    )(*args)


def add_kernel(own_ref, got_ref, *refs):
    for n, ref in enumerate(refs):
        ref[...] = (own_ref[n] + got_ref[n].astype(F32)).astype(ref.dtype)


def add_call(own, got, types):
    return pl.pallas_call(
        add_kernel,
        out_shape=tuple(jax.ShapeDtypeStruct(own.shape[1:], t) for t in types),
        in_specs=[VMEM] * 2,
        out_specs=(VMEM,) * len(types),
        compiler_params=SMALL,
        cost_estimate=QUICK,
    )(own, got)


def sum_kernel(own_ref, *refs):
    total = own_ref[...]
    for ref in refs[:-1]:
        total = total + ref[...].astype(F32)
    refs[-1][...] = total


def sum_call(own, got, flops):
    return pl.pallas_call(
        sum_kernel,
        out_shape=jax.ShapeDtypeStruct(own.shape, F32),
        in_specs=[VMEM] * (1 + len(got)),
        out_specs=VMEM,
        compiler_params=SMALL,
        cost_estimate=pl.CostEstimate(flops=flops, bytes_accessed=1000, transcendentals=0),
    )(own, *got)


def query_kernel(rows, heads, scale, dq_ref, *refs):
    dq = dq_ref[...]
    for ref in refs[:-1]:
        dq = dq + ref[...].astype(F32)
    for h in range(heads):
        part = dq[:, h * rows : (h + 1) * rows]
        refs[-1][:, h * 128 : (h + 1) * 128] = (scale * part).T.astype(BF)


def key_kernel(rows, scale, dkv_ref, near_ref, gk_ref, gv_ref):
    gk_ref[...] = (scale * (dkv_ref[:rows, :] + near_ref[:rows, :].astype(F32))).astype(BF)
    gv_ref[...] = (dkv_ref[rows:, :] + near_ref[rows:, :].astype(F32)).astype(BF)


def crossed(block, t, other):
    pairs = []
    for i in range(lax.axis_size("inner")):
        chip, core = i // 2, i % 2
        pairs.append((i, 2 * (chip ^ (2 * t + (core if other else 1 - core))) + core))
    return lax.ppermute(block, "inner", pairs)


def on_device(query, key, value, out, grad_out, lse, positions):
    rows, width = key.shape
    heads = query.shape[1] // width
    hr = heads * rows
    scale = width ** (-0.5)
    nq = lax.axis_size("outer")
    nz = lax.axis_size("inner") // 2
    sds = jax.ShapeDtypeStruct
    inputs = (query, key, value, out, grad_out, lse, positions[None, :])
    x, kv = pl.pallas_call(
        pack_kernel,
        out_shape=(sds((2 * hr + 32, width), BF), sds((2 * rows + 16, width), BF)),
        in_specs=[pl.BlockSpec(memory_space=pltpu.HBM)] * 7,
        out_specs=(VMEM, VMEM),
        scratch_shapes=[
            pltpu.VMEM(out.shape, BF),
            pltpu.VMEM(lse.shape, F32),
            pltpu.VMEM((1, rows), jnp.int32),
            pltpu.SemaphoreType.DMA((5 + 2 * heads,)),
        ],
        compiler_params=SMALL,
        cost_estimate=QUICK,
    )(*[pltpu.with_memory_space_constraint(a, pltpu.HBM) for a in inputs])

    common = (rows, heads, scale)
    sib = swapped(kv, "inner", 1)
    near = swapped(kv, "inner", 2)
    direct = [crossed(block, t, False) for t in range(1, nz // 2) for block in (kv, sib)]
    early = [kv, sib, near]
    dq_own, acc = blocks_call([x], early, range(3), *common, F32, F32, diagonal=True)

    xs = [swapped(x, "outer", s) for s in range(1, nq - 1)]
    dqs = [dq_own]
    for s in range(nq - 2):
        xs[s], acc = lax.optimization_barrier((xs[s], acc))
        dq, acc = blocks_call([xs[s]], early, range(3), *common, F32, F32, acc=[(acc, n) for n in range(3)])
        dqs.append(dq)
    halves = [xs[nq - 3][:hr], xs[((nq - 1) ^ (nq // 2)) - 1][hr:]]
    corner = [swapped(halves[0], "outer", 1), swapped(halves[1], "outer", nq // 2)]

    *direct, acc = lax.optimization_barrier((*direct, acc))
    traded = [swapped(block, "inner", 1) for block in direct]
    direct = [swapped(near, "inner", 1), *direct]
    xs = [x, *xs]
    n_d, n_t = len(direct), len(traded)
    *dqs, acc_d = blocks_call(xs, direct, range(n_d), *common, F32, F32, dq_in=dqs)
    types = [F32] + [BF] * (nq - 2)
    dq_own, *dqs, acc_t = blocks_call(xs, traded, range(n_t), *common, F32, types, dq_in=dqs)

    arrays = [*early, *direct, *traded]
    accs = [(a, n) for a, count in ((acc, 3), (acc_d, n_d), (acc_t, n_t)) for n in range(count)]
    theirs, ours = [1, 3], [0, 2]
    for t in range(0, n_t, 2):
        theirs += [3 + n_d + t, 4 + t + 1]
        ours += [4 + t, 3 + n_d + t + 1]
    dq_last, dkv_sib = blocks_call([corner], arrays, theirs, *common, BF, F32, acc=accs)
    dkv_got = swapped(dkv_sib, "inner", 1)
    dq_last, dkv_own = blocks_call([corner], arrays, ours, *common, F32, BF, acc=accs, dq_in=[dq_last])
    dq_far = swapped(dq_last, "outer", nq - 1)
    dkv_own, dkv_near, *far = add_call(dkv_own, dkv_got, [F32] + [BF] * (nz - 1))
    got = [swapped(dq, "outer", s + 1) for s, dq in enumerate(dqs)]
    dkv = []
    for t in range(1, nz // 2):
        dkv.append(crossed(far[2 * t - 2], t, False))
        dkv.append(crossed(far[2 * t - 1], t, True))
    dkv_near = swapped(dkv_near, "inner", 2)

    dkv_sum = sum_call(dkv_own, dkv, 1_500_000_000)
    dq_sum = sum_call(dq_own, [dq_far], 100_000_000)
    dq_sum, dkv_sum = lax.optimization_barrier((dq_sum, dkv_sum))
    grad_query = pl.pallas_call(
        functools.partial(query_kernel, rows, heads, scale),
        out_shape=sds((rows, heads * width), BF),
        in_specs=[VMEM] * (1 + len(got)),
        out_specs=VMEM,
        compiler_params=SMALL,
        cost_estimate=QUICK,
    )(dq_sum, *got)
    dkv_near, grad_query = lax.optimization_barrier((dkv_near, grad_query))
    grad_key, grad_value = pl.pallas_call(
        functools.partial(key_kernel, rows, scale),
        out_shape=(sds((rows, width), BF),) * 2,
        in_specs=[VMEM] * 2,
        out_specs=(VMEM,) * 2,
        compiler_params=SMALL,
        cost_estimate=QUICK,
    )(dkv_sum, dkv_near)
    return grad_query, grad_key, grad_value


def solution(mesh):
    tokens = P(("outer", "inner"), None)
    return jax.shard_map(
        on_device,
        mesh=mesh,
        in_specs=(tokens,) * 5 + (P(None, ("outer", "inner")), P(("outer", "inner"))),
        out_specs=(tokens,) * 3,
        check_vma=False,
    )
```

```python
import functools
import math

import jax
import jax.numpy as jnp
from jax import lax
from jax.experimental import pallas as pl
from jax.experimental.pallas import tpu as pltpu
from jax.sharding import PartitionSpec as P

BF = jnp.bfloat16
F32 = jnp.float32
RUN = 64
LOG2E = math.log2(math.e)
VMEM = pl.BlockSpec(memory_space=pltpu.VMEM)
SMALL = pltpu.CompilerParams(vmem_limit_bytes=16 * 1024 * 1024)
NN = (((1,), (0,)), ((), ()))
NT = (((1,), (1,)), ((), ()))
QUICK = pl.CostEstimate(flops=1000, bytes_accessed=1000, transcendentals=0)
COLS = 512


def swapped(block, axis, mask):
    pairs = [(i, i ^ mask) for i in range(lax.axis_size(axis))]
    return lax.ppermute(block, axis, pairs)


def three_parts(x):
    hi = x.astype(BF)
    rest = x - hi.astype(F32)
    mid = rest.astype(BF)
    low = (rest - mid.astype(F32)).astype(BF)
    return [hi, mid, low]


def dot(a, b, dims=NN):
    return lax.dot_general(a, b, dims, preferred_element_type=F32)


def pack_kernel(q_ref, k_ref, v_ref, o_ref, g_ref, lse_ref, pos_ref, x_ref, kv_ref, o_s, lse_s, pos_s, sems):
    rows, width = k_ref.shape
    heads = q_ref.shape[1] // width
    moves = [(lse_ref, lse_s), (pos_ref, pos_s), (o_ref, o_s)]
    for h in range(heads):
        cols = pl.ds(h * width, width)
        moves.append((g_ref.at[:, cols], x_ref.at[pl.ds((heads + h) * rows, rows), :]))
    for h in range(heads):
        cols = pl.ds(h * width, width)
        moves.append((q_ref.at[:, cols], x_ref.at[pl.ds(h * rows, rows), :]))
    moves.append((k_ref, kv_ref.at[pl.ds(0, rows), :]))
    moves.append((v_ref, kv_ref.at[pl.ds(rows, rows), :]))
    copies = [pltpu.make_async_copy(a, b, sems.at[n]) for n, (a, b) in enumerate(moves)]
    for copy in copies:
        copy.start()
    for copy in copies[: 3 + heads]:
        copy.wait()
    ones = jnp.ones((8, width), BF)
    deltas = []
    for h in range(heads):
        g = x_ref[(heads + h) * rows : (heads + h + 1) * rows, :]
        prod = g.astype(F32) * o_s[:, h * width : (h + 1) * width].astype(F32)
        hi = prod.astype(BF)
        low = (prod - hi.astype(F32)).astype(BF)
        deltas.append((dot(ones, hi, NT) + dot(ones, low, NT))[:1])
    run = (pos_s[...] // RUN).astype(F32)
    extra = (
        three_parts(lse_s[...] * LOG2E)
        + three_parts(jnp.concatenate(deltas, axis=0))
        + [run.astype(BF), jnp.zeros((32 - 6 * heads - 1, rows), BF)]
    )
    x_ref[2 * heads * rows :, :] = jnp.concatenate([e.astype(F32) for e in extra], axis=0).astype(BF)
    lane = lax.broadcasted_iota(jnp.int32, run.shape, 1)
    ids = [
        jnp.max(jnp.where(lane == r * RUN, run, 0.0), axis=1, keepdims=True)
        for r in range(rows // RUN)
    ]
    wide = [jnp.broadcast_to(i, (1, width)) for i in ids]
    wide.append(jnp.zeros((16 - len(ids), width), F32))
    kv_ref[2 * rows :, :] = jnp.concatenate(wide, axis=0).astype(BF)
    for copy in copies[3 + heads :]:
        copy.wait()


def blocks_kernel(plan, rows, heads, scale, *refs):
    refs = list(refs)
    x_refs = []
    for parts in plan["parts"]:
        whole = refs.pop(0)
        x_refs.append((whole, whole.at[heads * rows :, :] if parts == 1 else refs.pop(0)))
    kv_refs = [refs.pop(0) for _ in range(plan["kv"])]
    acc_refs = [refs.pop(0) for _ in range(plan["acc"])]
    dq_in = [refs.pop(0) for _ in range(plan["dq_in"])]
    dq_refs, dkv_ref = refs[:-1], refs[-1]
    width = x_refs[0][0].shape[1]
    hr = heads * rows
    per = rows // RUN
    step = COLS // rows
    slots = plan["slots"]
    rowed = []
    for _, g_ref in x_refs:
        e = g_ref[hr:, :].astype(F32)
        lse = e[0:heads] + e[heads : 2 * heads] + e[2 * heads : 3 * heads]
        delta = e[3 * heads : 4 * heads] + e[4 * heads : 5 * heads] + e[5 * heads : 6 * heads]
        rowed.append((lse, delta, e[6 * heads : 6 * heads + 1]))
    group = 3 if len(slots) == 3 else 2
    loaded = {}

    def chunk(c):
        if c not in loaded:
            ks, vs, runs = [], [], []
            for n in slots[c : c + group]:
                ks.append(kv_refs[n][:rows, :])
                vs.append(kv_refs[n][rows : 2 * rows, :])
                e = kv_refs[n][2 * rows :, :].astype(F32)
                runs += [e[r : r + 1] for r in range(per)]
            kt = jnp.concatenate([b.astype(F32).T.astype(BF) for b in ks], axis=1)
            loaded[c] = (jnp.concatenate(ks, axis=0), jnp.concatenate(vs, axis=0), kt, runs)
        return loaded[c]

    def products(c, b, n):
        k, v, _, _ = chunk(c)
        q_ref, g_ref = x_refs[b]
        q = q_ref[n * COLS : (n + 1) * COLS, :]
        g = g_ref[n * COLS : (n + 1) * COLS, :]
        return q, g, dot(k, q, NT), dot(v, g, NT)

    def weights(c, b, n, st, dpt):
        lse, delta, run = rowed[b]
        p_rows, d_rows = [], []
        for r, krun in enumerate(chunk(c)[3]):
            sl = slice(r * RUN, (r + 1) * RUN)
            p_heads, d_heads = [], []
            for h in range(step):
                hl = slice(h * rows, (h + 1) * rows)
                head = n * step + h
                row = jnp.where(krun <= run, lse[head : head + 1], 1e30)
                arg = st[sl, hl] * (scale * LOG2E) - row
                if plan["diagonal"] and b == 0 and c == 0 and r < per:
                    i = lax.broadcasted_iota(jnp.int32, (RUN, rows), 1) - r * RUN
                    j = lax.broadcasted_iota(jnp.int32, (RUN, rows), 0)
                    arg = jnp.where((i >= 0) & (i < j), -1e30, arg)
                p = jnp.exp2(arg)
                p_heads.append(p.astype(BF))
                d_heads.append((p * (dpt[sl, hl] - delta[head : head + 1])).astype(BF))
            p_rows.append(jnp.concatenate(p_heads, axis=1))
            d_rows.append(jnp.concatenate(d_heads, axis=1))
        return jnp.concatenate(p_rows, axis=0), jnp.concatenate(d_rows, axis=0)

    def plus(total, part):
        return part if total is None else total + part

    dqt = [[None] * (hr // COLS) for _ in x_refs]
    units = [
        (c, b, n)
        for c in range(0, len(slots), group)
        for b in range(len(x_refs))
        for n in range(hr // COLS)
    ]
    dk = dv = None
    ahead = products(*units[0])
    for at, (c, b, n) in enumerate(units):
        q, g, st, dpt = ahead
        if at + 1 < len(units):
            ahead = products(*units[at + 1])
        p, d = weights(c, b, n, st, dpt)
        dv, dk = plus(dv, dot(p, g)), plus(dk, dot(d, q))
        dqt[b][n] = plus(dqt[b][n], dot(chunk(c)[2], d))
        if at + 1 < len(units) and units[at + 1][0] == c:
            continue
        for j, slot in enumerate(slots[c : c + group]):
            dk_j, dv_j = dk[j * rows : (j + 1) * rows], dv[j * rows : (j + 1) * rows]
            if plan["acc"]:
                acc_ref, place = acc_refs[plan["at"][slot][0]], plan["at"][slot][1]
                dk_j += acc_ref[place, :rows, :]
                dv_j += acc_ref[place, rows:, :]
            dkv_ref[c + j, :rows, :] = dk_j.astype(dkv_ref.dtype)
            dkv_ref[c + j, rows:, :] = dv_j.astype(dkv_ref.dtype)
        dk = dv = None
    for b, dq_ref in enumerate(dq_refs):
        for n in range(hr // COLS):
            cols = slice(n * COLS, (n + 1) * COLS)
            total = dqt[b][n] + dq_in[b][:, cols] if dq_in else dqt[b][n]
            dq_ref[:, cols] = total.astype(dq_ref.dtype)


def blocks_call(xs, kvs, slots, rows, heads, scale, dkv_type, dq_type, acc=(), dq_in=(), diagonal=False):
    sds = jax.ShapeDtypeStruct
    width = kvs[0].shape[1]
    xs = [x if isinstance(x, list) else [x] for x in xs]
    slots = list(slots)
    totals = []
    for a, _ in acc:
        if all(a is not t for t in totals):
            totals.append(a)
    at = [([a is t for t in totals].index(True), n) for a, n in acc]
    plan = {
        "parts": [len(x) for x in xs],
        "kv": len(kvs),
        "acc": len(totals),
        "at": at,
        "dq_in": len(dq_in),
        "slots": slots,
        "diagonal": diagonal,
    }
    args = (*sum(xs, []), *kvs, *totals, *dq_in)
    types = dq_type if isinstance(dq_type, list) else [dq_type] * len(xs)
    outs = tuple(sds((width, heads * rows), t) for t in types)
    outs += (sds((len(slots), 2 * rows, width), dkv_type),)
    return pl.pallas_call(
        functools.partial(blocks_kernel, plan, rows, heads, scale),
        out_shape=outs,
        in_specs=[VMEM] * len(args),
        out_specs=(VMEM,) * len(outs),
        compiler_params=SMALL,
        cost_estimate=QUICK,
    )(*args)


def add_kernel(own_ref, got_ref, *refs):
    for n, ref in enumerate(refs):
        ref[...] = (own_ref[n] + got_ref[n].astype(F32)).astype(ref.dtype)


def add_call(own, got, types):
    return pl.pallas_call(
        add_kernel,
        out_shape=tuple(jax.ShapeDtypeStruct(own.shape[1:], t) for t in types),
        in_specs=[VMEM] * 2,
        out_specs=(VMEM,) * len(types),
        compiler_params=SMALL,
        cost_estimate=QUICK,
    )(own, got)


def sum_kernel(own_ref, *refs):
    total = own_ref[...]
    for ref in refs[:-1]:
        total = total + ref[...].astype(F32)
    refs[-1][...] = total


def sum_call(own, got, flops):
    return pl.pallas_call(
        sum_kernel,
        out_shape=jax.ShapeDtypeStruct(own.shape, F32),
        in_specs=[VMEM] * (1 + len(got)),
        out_specs=VMEM,
        compiler_params=SMALL,
        cost_estimate=pl.CostEstimate(flops=flops, bytes_accessed=1000, transcendentals=0),
    )(own, *got)


def query_kernel(rows, heads, scale, dq_ref, *refs):
    dq = dq_ref[...]
    for ref in refs[:-1]:
        dq = dq + ref[...].astype(F32)
    for h in range(heads):
        part = dq[:, h * rows : (h + 1) * rows]
        refs[-1][:, h * 128 : (h + 1) * 128] = (scale * part).T.astype(BF)


def key_kernel(rows, scale, dkv_ref, near_ref, gk_ref, gv_ref):
    gk_ref[...] = (scale * (dkv_ref[:rows, :] + near_ref[:rows, :].astype(F32))).astype(BF)
    gv_ref[...] = (dkv_ref[rows:, :] + near_ref[rows:, :].astype(F32)).astype(BF)


def crossed(block, t, other):
    pairs = []
    for i in range(lax.axis_size("inner")):
        chip, core = i // 2, i % 2
        pairs.append((i, 2 * (chip ^ (2 * t + (core if other else 1 - core))) + core))
    return lax.ppermute(block, "inner", pairs)


def on_device(query, key, value, out, grad_out, lse, positions):
    rows, width = key.shape
    heads = query.shape[1] // width
    hr = heads * rows
    scale = width ** (-0.5)
    nq = lax.axis_size("outer")
    nz = lax.axis_size("inner") // 2
    sds = jax.ShapeDtypeStruct
    inputs = (query, key, value, out, grad_out, lse, positions[None, :])
    x, kv = pl.pallas_call(
        pack_kernel,
        out_shape=(sds((2 * hr + 32, width), BF), sds((2 * rows + 16, width), BF)),
        in_specs=[pl.BlockSpec(memory_space=pltpu.HBM)] * 7,
        out_specs=(VMEM, VMEM),
        scratch_shapes=[
            pltpu.VMEM(out.shape, BF),
            pltpu.VMEM(lse.shape, F32),
            pltpu.VMEM((1, rows), jnp.int32),
            pltpu.SemaphoreType.DMA((5 + 2 * heads,)),
        ],
        compiler_params=SMALL,
        cost_estimate=QUICK,
    )(*[pltpu.with_memory_space_constraint(a, pltpu.HBM) for a in inputs])

    common = (rows, heads, scale)
    sib = swapped(kv, "inner", 1)
    near = swapped(kv, "inner", 2)
    direct = [crossed(block, t, False) for t in range(1, nz // 2) for block in (kv, sib)]
    early = [kv, sib, near]
    dq_own, acc = blocks_call([x], early, range(3), *common, F32, F32, diagonal=True)

    xs = [swapped(x, "outer", s) for s in range(1, nq - 1)]
    *xs, acc = lax.optimization_barrier((*xs, acc))
    halves = [xs[nq - 3][:hr], xs[((nq - 1) ^ (nq // 2)) - 1][hr:]]
    corner = [swapped(halves[0], "outer", 1), swapped(halves[1], "outer", nq // 2)]
    *dqs, acc = blocks_call(xs, early, range(3), *common, F32, F32, acc=[(acc, n) for n in range(3)])
    dqs = [dq_own, *dqs]

    *direct, acc = lax.optimization_barrier((*direct, acc))
    traded = [swapped(block, "inner", 1) for block in direct]
    direct = [swapped(near, "inner", 1), *direct]
    xs = [x, *xs]
    n_d, n_t = len(direct), len(traded)
    *dqs, acc_d = blocks_call(xs, direct, range(n_d), *common, F32, F32, dq_in=dqs)
    types = [F32] + [BF] * (nq - 2)
    dq_own, *dqs, acc_t = blocks_call(xs, traded, range(n_t), *common, F32, types, dq_in=dqs)

    arrays = [*early, *direct, *traded]
    accs = [(a, n) for a, count in ((acc, 3), (acc_d, n_d), (acc_t, n_t)) for n in range(count)]
    theirs, ours = [1, 3], [0, 2]
    for t in range(0, n_t, 2):
        theirs += [3 + n_d + t, 4 + t + 1]
        ours += [4 + t, 3 + n_d + t + 1]
    dq_last, dkv_sib = blocks_call([corner], arrays, theirs, *common, BF, F32, acc=accs)
    dkv_got = swapped(dkv_sib, "inner", 1)
    dq_last, dkv_own = blocks_call([corner], arrays, ours, *common, F32, BF, acc=accs, dq_in=[dq_last])
    dq_far = swapped(dq_last, "outer", nq - 1)
    dkv_own, dkv_near, *far = add_call(dkv_own, dkv_got, [F32] + [BF] * (nz - 1))
    got = [swapped(dq, "outer", s + 1) for s, dq in enumerate(dqs)]
    dkv = []
    for t in range(1, nz // 2):
        dkv.append(crossed(far[2 * t - 2], t, False))
        dkv.append(crossed(far[2 * t - 1], t, True))
    dkv_near = swapped(dkv_near, "inner", 2)

    dkv_sum = sum_call(dkv_own, dkv, 1_500_000_000)
    dq_sum = sum_call(dq_own, [dq_far], 100_000_000)
    dq_sum, dkv_sum = lax.optimization_barrier((dq_sum, dkv_sum))
    grad_query = pl.pallas_call(
        functools.partial(query_kernel, rows, heads, scale),
        out_shape=sds((rows, heads * width), BF),
        in_specs=[VMEM] * (1 + len(got)),
        out_specs=VMEM,
        compiler_params=SMALL,
        cost_estimate=QUICK,
    )(dq_sum, *got)
    dkv_near, grad_query = lax.optimization_barrier((dkv_near, grad_query))
    grad_key, grad_value = pl.pallas_call(
        functools.partial(key_kernel, rows, scale),
        out_shape=(sds((rows, width), BF),) * 2,
        in_specs=[VMEM] * 2,
        out_specs=(VMEM,) * 2,
        compiler_params=SMALL,
        cost_estimate=QUICK,
    )(dkv_sum, dkv_near)
    return grad_query, grad_key, grad_value


def solution(mesh):
    tokens = P(("outer", "inner"), None)
    return jax.shard_map(
        on_device,
        mesh=mesh,
        in_specs=(tokens,) * 5 + (P(None, ("outer", "inner")), P(("outer", "inner"))),
        out_specs=(tokens,) * 3,
        check_vma=False,
    )
```

```python
import functools
import math

import jax
import jax.numpy as jnp
from jax import lax
from jax.experimental import pallas as pl
from jax.experimental.pallas import tpu as pltpu
from jax.sharding import PartitionSpec as P

BF = jnp.bfloat16
F32 = jnp.float32
RUN = 64
LOG2E = math.log2(math.e)
VMEM = pl.BlockSpec(memory_space=pltpu.VMEM)
SMALL = pltpu.CompilerParams(vmem_limit_bytes=16 * 1024 * 1024)
NN = (((1,), (0,)), ((), ()))
NT = (((1,), (1,)), ((), ()))
QUICK = pl.CostEstimate(flops=1000, bytes_accessed=1000, transcendentals=0)
COLS = 512


def swapped(block, axis, mask):
    pairs = [(i, i ^ mask) for i in range(lax.axis_size(axis))]
    return lax.ppermute(block, axis, pairs)


def three_parts(x):
    hi = x.astype(BF)
    rest = x - hi.astype(F32)
    mid = rest.astype(BF)
    low = (rest - mid.astype(F32)).astype(BF)
    return [hi, mid, low]


def dot(a, b, dims=NN):
    return lax.dot_general(a, b, dims, preferred_element_type=F32)


def pack_kernel(q_ref, k_ref, v_ref, o_ref, g_ref, lse_ref, pos_ref, x_ref, kv_ref, o_s, lse_s, pos_s, sems):
    rows, width = k_ref.shape
    heads = q_ref.shape[1] // width
    moves = [(lse_ref, lse_s), (pos_ref, pos_s), (o_ref, o_s)]
    for h in range(heads):
        cols = pl.ds(h * width, width)
        moves.append((g_ref.at[:, cols], x_ref.at[pl.ds((heads + h) * rows, rows), :]))
    for h in range(heads):
        cols = pl.ds(h * width, width)
        moves.append((q_ref.at[:, cols], x_ref.at[pl.ds(h * rows, rows), :]))
    moves.append((k_ref, kv_ref.at[pl.ds(0, rows), :]))
    moves.append((v_ref, kv_ref.at[pl.ds(rows, rows), :]))
    copies = [pltpu.make_async_copy(a, b, sems.at[n]) for n, (a, b) in enumerate(moves)]
    for copy in copies:
        copy.start()
    for copy in copies[: 3 + heads]:
        copy.wait()
    ones = jnp.ones((8, width), BF)
    deltas = []
    for h in range(heads):
        g = x_ref[(heads + h) * rows : (heads + h + 1) * rows, :]
        prod = g.astype(F32) * o_s[:, h * width : (h + 1) * width].astype(F32)
        hi = prod.astype(BF)
        low = (prod - hi.astype(F32)).astype(BF)
        deltas.append((dot(ones, hi, NT) + dot(ones, low, NT))[:1])
    run = (pos_s[...] // RUN).astype(F32)
    extra = (
        three_parts(lse_s[...] * LOG2E)
        + three_parts(jnp.concatenate(deltas, axis=0))
        + [run.astype(BF), jnp.zeros((32 - 6 * heads - 1, rows), BF)]
    )
    x_ref[2 * heads * rows :, :] = jnp.concatenate([e.astype(F32) for e in extra], axis=0).astype(BF)
    lane = lax.broadcasted_iota(jnp.int32, run.shape, 1)
    ids = [
        jnp.max(jnp.where(lane == r * RUN, run, 0.0), axis=1, keepdims=True)
        for r in range(rows // RUN)
    ]
    wide = [jnp.broadcast_to(i, (1, width)) for i in ids]
    wide.append(jnp.zeros((16 - len(ids), width), F32))
    kv_ref[2 * rows :, :] = jnp.concatenate(wide, axis=0).astype(BF)
    for copy in copies[3 + heads :]:
        copy.wait()


def blocks_kernel(plan, rows, heads, scale, *refs):
    refs = list(refs)
    x_refs = []
    for parts in plan["parts"]:
        whole = refs.pop(0)
        x_refs.append((whole, whole.at[heads * rows :, :] if parts == 1 else refs.pop(0)))
    kv_refs = [refs.pop(0) for _ in range(plan["kv"])]
    acc_refs = [refs.pop(0) for _ in range(plan["acc"])]
    dq_in = [refs.pop(0) for _ in range(plan["dq_in"])]
    dq_refs, dkv_ref = refs[:-1], refs[-1]
    width = x_refs[0][0].shape[1]
    hr = heads * rows
    per = rows // RUN
    step = COLS // rows
    slots = plan["slots"]
    rowed = []
    for _, g_ref in x_refs:
        e = g_ref[hr:, :].astype(F32)
        lse = e[0:heads] + e[heads : 2 * heads] + e[2 * heads : 3 * heads]
        delta = e[3 * heads : 4 * heads] + e[4 * heads : 5 * heads] + e[5 * heads : 6 * heads]
        rowed.append((lse, delta, e[6 * heads : 6 * heads + 1]))
    group = 3 if len(slots) == 3 else 2
    loaded = {}

    def chunk(c):
        if c not in loaded:
            ks, vs, runs = [], [], []
            for n in slots[c : c + group]:
                ks.append(kv_refs[n][:rows, :])
                vs.append(kv_refs[n][rows : 2 * rows, :])
                e = kv_refs[n][2 * rows :, :].astype(F32)
                runs += [e[r : r + 1] for r in range(per)]
            kt = jnp.concatenate([b.astype(F32).T.astype(BF) for b in ks], axis=1)
            loaded[c] = (jnp.concatenate(ks, axis=0), jnp.concatenate(vs, axis=0), kt, runs)
        return loaded[c]

    def products(c, b, n):
        k, v, _, _ = chunk(c)
        q_ref, g_ref = x_refs[b]
        q = q_ref[n * COLS : (n + 1) * COLS, :]
        g = g_ref[n * COLS : (n + 1) * COLS, :]
        return q, g, dot(k, q, NT), dot(v, g, NT)

    def weights(c, b, n, st, dpt):
        lse, delta, run = rowed[b]
        p_rows, d_rows = [], []
        for r, krun in enumerate(chunk(c)[3]):
            sl = slice(r * RUN, (r + 1) * RUN)
            p_heads, d_heads = [], []
            for h in range(step):
                hl = slice(h * rows, (h + 1) * rows)
                head = n * step + h
                row = jnp.where(krun <= run, lse[head : head + 1], 1e30)
                arg = st[sl, hl] * (scale * LOG2E) - row
                if plan["diagonal"] and b == 0 and c == 0 and r < per:
                    i = lax.broadcasted_iota(jnp.int32, (RUN, rows), 1) - r * RUN
                    j = lax.broadcasted_iota(jnp.int32, (RUN, rows), 0)
                    arg = jnp.where((i >= 0) & (i < j), -1e30, arg)
                p = jnp.exp2(arg)
                p_heads.append(p.astype(BF))
                d_heads.append((p * (dpt[sl, hl] - delta[head : head + 1])).astype(BF))
            p_rows.append(jnp.concatenate(p_heads, axis=1))
            d_rows.append(jnp.concatenate(d_heads, axis=1))
        return jnp.concatenate(p_rows, axis=0), jnp.concatenate(d_rows, axis=0)

    def plus(total, part):
        return part if total is None else total + part

    dqt = [[None] * (hr // COLS) for _ in x_refs]
    units = [
        (c, b, n)
        for c in range(0, len(slots), group)
        for b in range(len(x_refs))
        for n in range(hr // COLS)
    ]
    dk = dv = None
    ahead = products(*units[0])
    for at, (c, b, n) in enumerate(units):
        q, g, st, dpt = ahead
        if at + 1 < len(units):
            ahead = products(*units[at + 1])
        p, d = weights(c, b, n, st, dpt)
        dv, dk = plus(dv, dot(p, g)), plus(dk, dot(d, q))
        dqt[b][n] = plus(dqt[b][n], dot(chunk(c)[2], d))
        if at + 1 < len(units) and units[at + 1][0] == c:
            continue
        for j, slot in enumerate(slots[c : c + group]):
            dk_j, dv_j = dk[j * rows : (j + 1) * rows], dv[j * rows : (j + 1) * rows]
            if plan["acc"]:
                acc_ref, place = acc_refs[plan["at"][slot][0]], plan["at"][slot][1]
                dk_j += acc_ref[place, :rows, :]
                dv_j += acc_ref[place, rows:, :]
            dkv_ref[c + j, :rows, :] = dk_j.astype(dkv_ref.dtype)
            dkv_ref[c + j, rows:, :] = dv_j.astype(dkv_ref.dtype)
        dk = dv = None
    for b, dq_ref in enumerate(dq_refs):
        for n in range(hr // COLS):
            cols = slice(n * COLS, (n + 1) * COLS)
            total = dqt[b][n] + dq_in[b][:, cols] if dq_in else dqt[b][n]
            dq_ref[:, cols] = total.astype(dq_ref.dtype)


def blocks_call(xs, kvs, slots, rows, heads, scale, dkv_type, dq_type, acc=(), dq_in=(), diagonal=False):
    sds = jax.ShapeDtypeStruct
    width = kvs[0].shape[1]
    xs = [x if isinstance(x, list) else [x] for x in xs]
    slots = list(slots)
    totals = []
    for a, _ in acc:
        if all(a is not t for t in totals):
            totals.append(a)
    at = [([a is t for t in totals].index(True), n) for a, n in acc]
    plan = {
        "parts": [len(x) for x in xs],
        "kv": len(kvs),
        "acc": len(totals),
        "at": at,
        "dq_in": len(dq_in),
        "slots": slots,
        "diagonal": diagonal,
    }
    args = (*sum(xs, []), *kvs, *totals, *dq_in)
    types = dq_type if isinstance(dq_type, list) else [dq_type] * len(xs)
    outs = tuple(sds((width, heads * rows), t) for t in types)
    outs += (sds((len(slots), 2 * rows, width), dkv_type),)
    return pl.pallas_call(
        functools.partial(blocks_kernel, plan, rows, heads, scale),
        out_shape=outs,
        in_specs=[VMEM] * len(args),
        out_specs=(VMEM,) * len(outs),
        compiler_params=SMALL,
        cost_estimate=QUICK,
    )(*args)


def add_kernel(own_ref, got_ref, *refs):
    for n, ref in enumerate(refs):
        ref[...] = (own_ref[n] + got_ref[n].astype(F32)).astype(ref.dtype)


def add_call(own, got, types):
    return pl.pallas_call(
        add_kernel,
        out_shape=tuple(jax.ShapeDtypeStruct(own.shape[1:], t) for t in types),
        in_specs=[VMEM] * 2,
        out_specs=(VMEM,) * len(types),
        compiler_params=SMALL,
        cost_estimate=QUICK,
    )(own, got)


def sum_kernel(own_ref, *refs):
    total = own_ref[...]
    for ref in refs[:-1]:
        total = total + ref[...].astype(F32)
    refs[-1][...] = total


def sum_call(own, got, flops):
    return pl.pallas_call(
        sum_kernel,
        out_shape=jax.ShapeDtypeStruct(own.shape, F32),
        in_specs=[VMEM] * (1 + len(got)),
        out_specs=VMEM,
        compiler_params=SMALL,
        cost_estimate=pl.CostEstimate(flops=flops, bytes_accessed=1000, transcendentals=0),
    )(own, *got)


def query_kernel(rows, heads, scale, dq_ref, *refs):
    dq_refs, (gq_ref, part_s, sems) = refs[:-3], refs[-3:]
    copies = []
    for h in range(heads):
        at = slice(h * rows, (h + 1) * rows)
        dq = dq_ref[:, at]
        for ref in dq_refs:
            dq = dq + ref[:, at].astype(F32)
        part_s[h] = (scale * dq).T.astype(BF)
        width = part_s.shape[2]
        copies.append(pltpu.make_async_copy(part_s.at[h], gq_ref.at[:, pl.ds(h * width, width)], sems.at[h]))
        copies[-1].start()
    for copy in copies:
        copy.wait()


def key_kernel(rows, scale, dkv_ref, near_ref, gk_ref, gv_ref):
    gk_ref[...] = (scale * (dkv_ref[:rows, :] + near_ref[:rows, :].astype(F32))).astype(BF)
    gv_ref[...] = (dkv_ref[rows:, :] + near_ref[rows:, :].astype(F32)).astype(BF)


def crossed(block, t, other):
    pairs = []
    for i in range(lax.axis_size("inner")):
        chip, core = i // 2, i % 2
        pairs.append((i, 2 * (chip ^ (2 * t + (core if other else 1 - core))) + core))
    return lax.ppermute(block, "inner", pairs)


def on_device(query, key, value, out, grad_out, lse, positions):
    rows, width = key.shape
    heads = query.shape[1] // width
    hr = heads * rows
    scale = width ** (-0.5)
    nq = lax.axis_size("outer")
    nz = lax.axis_size("inner") // 2
    sds = jax.ShapeDtypeStruct
    inputs = (query, key, value, out, grad_out, lse, positions[None, :])
    x, kv = pl.pallas_call(
        pack_kernel,
        out_shape=(sds((2 * hr + 32, width), BF), sds((2 * rows + 16, width), BF)),
        in_specs=[pl.BlockSpec(memory_space=pltpu.HBM)] * 7,
        out_specs=(VMEM, VMEM),
        scratch_shapes=[
            pltpu.VMEM(out.shape, BF),
            pltpu.VMEM(lse.shape, F32),
            pltpu.VMEM((1, rows), jnp.int32),
            pltpu.SemaphoreType.DMA((5 + 2 * heads,)),
        ],
        compiler_params=SMALL,
        cost_estimate=QUICK,
    )(*[pltpu.with_memory_space_constraint(a, pltpu.HBM) for a in inputs])

    common = (rows, heads, scale)
    sib = swapped(kv, "inner", 1)
    near = swapped(kv, "inner", 2)
    direct = [crossed(block, t, False) for t in range(1, nz // 2) for block in (kv, sib)]
    early = [kv, sib, near]
    dq_own, acc = blocks_call([x], early, range(3), *common, F32, F32, diagonal=True)

    xs = [swapped(x, "outer", s) for s in range(1, nq - 1)]
    *xs, acc = lax.optimization_barrier((*xs, acc))
    halves = [xs[nq - 3][:hr], xs[((nq - 1) ^ (nq // 2)) - 1][hr:]]
    corner = [swapped(halves[0], "outer", 1), swapped(halves[1], "outer", nq // 2)]
    *dqs, acc = blocks_call(xs, early, range(3), *common, F32, F32, acc=[(acc, n) for n in range(3)])
    dqs = [dq_own, *dqs]

    *direct, acc = lax.optimization_barrier((*direct, acc))
    traded = [swapped(block, "inner", 1) for block in direct]
    direct = [swapped(near, "inner", 1), *direct]
    xs = [x, *xs]
    n_d, n_t = len(direct), len(traded)
    *dqs, acc_d = blocks_call(xs, direct, range(n_d), *common, F32, F32, dq_in=dqs)
    types = [F32] + [BF] * (nq - 2)
    dq_own, *dqs, acc_t = blocks_call(xs, traded, range(n_t), *common, F32, types, dq_in=dqs)

    arrays = [*early, *direct, *traded]
    accs = [(a, n) for a, count in ((acc, 3), (acc_d, n_d), (acc_t, n_t)) for n in range(count)]
    theirs, ours = [1, 3], [0, 2]
    for t in range(0, n_t, 2):
        theirs += [3 + n_d + t, 4 + t + 1]
        ours += [4 + t, 3 + n_d + t + 1]
    dq_last, dkv_sib = blocks_call([corner], arrays, theirs, *common, BF, F32, acc=accs)
    dkv_got = swapped(dkv_sib, "inner", 1)
    dq_last, dkv_own = blocks_call([corner], arrays, ours, *common, F32, BF, acc=accs, dq_in=[dq_last])
    dq_far = swapped(dq_last, "outer", nq - 1)
    dkv_own, dkv_near, *far = add_call(dkv_own, dkv_got, [F32] + [BF] * (nz - 1))
    got = [swapped(dq, "outer", s + 1) for s, dq in enumerate(dqs)]
    dkv = []
    for t in range(1, nz // 2):
        dkv.append(crossed(far[2 * t - 2], t, False))
        dkv.append(crossed(far[2 * t - 1], t, True))
    dkv_near = swapped(dkv_near, "inner", 2)

    dkv_sum = sum_call(dkv_own, dkv, 1_500_000_000)
    dq_sum = sum_call(dq_own, [dq_far], 100_000_000)
    dq_sum, dkv_sum = lax.optimization_barrier((dq_sum, dkv_sum))
    grad_query = pl.pallas_call(
        functools.partial(query_kernel, rows, heads, scale),
        out_shape=sds((rows, heads * width), BF),
        in_specs=[VMEM] * (1 + len(got)),
        out_specs=pl.BlockSpec(memory_space=pltpu.HBM),
        scratch_shapes=[pltpu.VMEM((heads, rows, width), BF), pltpu.SemaphoreType.DMA((heads,))],
        compiler_params=SMALL,
        cost_estimate=QUICK,
    )(dq_sum, *got)
    dkv_near, grad_query = lax.optimization_barrier((dkv_near, grad_query))
    grad_key, grad_value = pl.pallas_call(
        functools.partial(key_kernel, rows, scale),
        out_shape=(sds((rows, width), BF),) * 2,
        in_specs=[VMEM] * 2,
        out_specs=(VMEM,) * 2,
        compiler_params=SMALL,
        cost_estimate=QUICK,
    )(dkv_sum, dkv_near)
    return grad_query, grad_key, grad_value


def solution(mesh):
    tokens = P(("outer", "inner"), None)
    return jax.shard_map(
        on_device,
        mesh=mesh,
        in_specs=(tokens,) * 5 + (P(None, ("outer", "inner")), P(("outer", "inner"))),
        out_specs=(tokens,) * 3,
        check_vma=False,
    )
```

```python
import functools
import math

import jax
import jax.numpy as jnp
from jax import lax
from jax.experimental import pallas as pl
from jax.experimental.pallas import tpu as pltpu
from jax.sharding import PartitionSpec as P

BF = jnp.bfloat16
F32 = jnp.float32
RUN = 64
LOG2E = math.log2(math.e)
VMEM = pl.BlockSpec(memory_space=pltpu.VMEM)
SMALL = pltpu.CompilerParams(vmem_limit_bytes=16 * 1024 * 1024)
NN = (((1,), (0,)), ((), ()))
NT = (((1,), (1,)), ((), ()))
QUICK = pl.CostEstimate(flops=1000, bytes_accessed=1000, transcendentals=0)
COLS = 512


def swapped(block, axis, mask):
    pairs = [(i, i ^ mask) for i in range(lax.axis_size(axis))]
    return lax.ppermute(block, axis, pairs)


def three_parts(x):
    hi = x.astype(BF)
    rest = x - hi.astype(F32)
    mid = rest.astype(BF)
    low = (rest - mid.astype(F32)).astype(BF)
    return [hi, mid, low]


def dot(a, b, dims=NN):
    return lax.dot_general(a, b, dims, preferred_element_type=F32)


def pack_kernel(q_ref, k_ref, v_ref, o_ref, g_ref, lse_ref, pos_ref, x_ref, kv_ref, o_s, lse_s, pos_s, sems):
    rows, width = k_ref.shape
    heads = q_ref.shape[1] // width
    moves = [(o_ref, o_s), (lse_ref, lse_s), (pos_ref, pos_s)]
    for h in range(heads):
        cols = pl.ds(h * width, width)
        moves.append((g_ref.at[:, cols], x_ref.at[pl.ds((heads + h) * rows, rows), :]))
    for h in range(heads):
        cols = pl.ds(h * width, width)
        moves.append((q_ref.at[:, cols], x_ref.at[pl.ds(h * rows, rows), :]))
    moves.append((k_ref, kv_ref.at[pl.ds(0, rows), :]))
    moves.append((v_ref, kv_ref.at[pl.ds(rows, rows), :]))
    copies = [pltpu.make_async_copy(a, b, sems.at[n]) for n, (a, b) in enumerate(moves)]
    for copy in copies:
        copy.start()
    for copy in copies[: 3 + heads]:
        copy.wait()
    ones = jnp.ones((8, width), BF)
    deltas = []
    for h in range(heads):
        g = x_ref[(heads + h) * rows : (heads + h + 1) * rows, :]
        prod = g.astype(F32) * o_s[:, h * width : (h + 1) * width].astype(F32)
        hi = prod.astype(BF)
        low = (prod - hi.astype(F32)).astype(BF)
        deltas.append((dot(ones, hi, NT) + dot(ones, low, NT))[:1])
    run = (pos_s[...] // RUN).astype(F32)
    extra = (
        three_parts(lse_s[...] * LOG2E)
        + three_parts(jnp.concatenate(deltas, axis=0))
        + [run.astype(BF), jnp.zeros((32 - 6 * heads - 1, rows), BF)]
    )
    x_ref[2 * heads * rows :, :] = jnp.concatenate([e.astype(F32) for e in extra], axis=0).astype(BF)
    lane = lax.broadcasted_iota(jnp.int32, run.shape, 1)
    ids = [
        jnp.max(jnp.where(lane == r * RUN, run, 0.0), axis=1, keepdims=True)
        for r in range(rows // RUN)
    ]
    wide = [jnp.broadcast_to(i, (1, width)) for i in ids]
    wide.append(jnp.zeros((16 - len(ids), width), F32))
    kv_ref[2 * rows :, :] = jnp.concatenate(wide, axis=0).astype(BF)
    for copy in copies[3 + heads :]:
        copy.wait()


def blocks_kernel(plan, rows, heads, scale, *refs):
    refs = list(refs)
    x_refs = []
    for parts in plan["parts"]:
        whole = refs.pop(0)
        x_refs.append((whole, whole.at[heads * rows :, :] if parts == 1 else refs.pop(0)))
    kv_refs = [refs.pop(0) for _ in range(plan["kv"])]
    acc_refs = [refs.pop(0) for _ in range(plan["acc"])]
    dq_in = [refs.pop(0) for _ in range(plan["dq_in"])]
    dq_refs, dkv_ref = refs[:-1], refs[-1]
    width = x_refs[0][0].shape[1]
    hr = heads * rows
    per = rows // RUN
    step = COLS // rows
    slots = plan["slots"]
    rowed = []
    for _, g_ref in x_refs:
        e = g_ref[hr:, :].astype(F32)
        lse = e[0:heads] + e[heads : 2 * heads] + e[2 * heads : 3 * heads]
        delta = e[3 * heads : 4 * heads] + e[4 * heads : 5 * heads] + e[5 * heads : 6 * heads]
        rowed.append((lse, delta, e[6 * heads : 6 * heads + 1]))
    group = len(slots) if len(slots) <= 4 else 2
    loaded = {}

    def chunk(c):
        if c not in loaded:
            ks, vs, runs = [], [], []
            for n in slots[c : c + group]:
                ks.append(kv_refs[n][:rows, :])
                vs.append(kv_refs[n][rows : 2 * rows, :])
                e = kv_refs[n][2 * rows :, :].astype(F32)
                runs += [e[r : r + 1] for r in range(per)]
            kt = jnp.concatenate([b.astype(F32).T.astype(BF) for b in ks], axis=1)
            loaded[c] = (jnp.concatenate(ks, axis=0), jnp.concatenate(vs, axis=0), kt, runs)
        return loaded[c]

    def products(c, b, n):
        k, v, _, _ = chunk(c)
        q_ref, g_ref = x_refs[b]
        q = q_ref[n * COLS : (n + 1) * COLS, :]
        g = g_ref[n * COLS : (n + 1) * COLS, :]
        return q, g, dot(k, q, NT), dot(v, g, NT)

    def weights(c, b, n, st, dpt):
        lse, delta, run = rowed[b]
        p_rows, d_rows = [], []
        for r, krun in enumerate(chunk(c)[3]):
            sl = slice(r * RUN, (r + 1) * RUN)
            p_heads, d_heads = [], []
            for h in range(step):
                hl = slice(h * rows, (h + 1) * rows)
                head = n * step + h
                row = jnp.where(krun <= run, lse[head : head + 1], 1e30)
                arg = st[sl, hl] * (scale * LOG2E) - row
                if plan["diagonal"] and b == 0 and c == 0 and r < per:
                    i = lax.broadcasted_iota(jnp.int32, (RUN, rows), 1) - r * RUN
                    j = lax.broadcasted_iota(jnp.int32, (RUN, rows), 0)
                    arg = jnp.where((i >= 0) & (i < j), -1e30, arg)
                p = jnp.exp2(arg)
                p_heads.append(p.astype(BF))
                d_heads.append((p * (dpt[sl, hl] - delta[head : head + 1])).astype(BF))
            p_rows.append(jnp.concatenate(p_heads, axis=1))
            d_rows.append(jnp.concatenate(d_heads, axis=1))
        return jnp.concatenate(p_rows, axis=0), jnp.concatenate(d_rows, axis=0)

    def plus(total, part):
        return part if total is None else total + part

    dqt = [[None] * (hr // COLS) for _ in x_refs]
    units = [
        (c, b, n)
        for c in range(0, len(slots), group)
        for b in range(len(x_refs))
        for n in range(hr // COLS)
    ]
    dk = dv = None
    ahead = products(*units[0])
    for at, (c, b, n) in enumerate(units):
        q, g, st, dpt = ahead
        if at + 1 < len(units):
            ahead = products(*units[at + 1])
        p, d = weights(c, b, n, st, dpt)
        dv, dk = plus(dv, dot(p, g)), plus(dk, dot(d, q))
        dqt[b][n] = plus(dqt[b][n], dot(chunk(c)[2], d))
        if at + 1 < len(units) and units[at + 1][0] == c:
            continue
        for j, slot in enumerate(slots[c : c + group]):
            dk_j, dv_j = dk[j * rows : (j + 1) * rows], dv[j * rows : (j + 1) * rows]
            if plan["acc"]:
                acc_ref, place = acc_refs[plan["at"][slot][0]], plan["at"][slot][1]
                dk_j += acc_ref[place, :rows, :]
                dv_j += acc_ref[place, rows:, :]
            dkv_ref[c + j, :rows, :] = dk_j.astype(dkv_ref.dtype)
            dkv_ref[c + j, rows:, :] = dv_j.astype(dkv_ref.dtype)
        dk = dv = None
    for b, dq_ref in enumerate(dq_refs):
        for n in range(hr // COLS):
            cols = slice(n * COLS, (n + 1) * COLS)
            total = dqt[b][n] + dq_in[b][:, cols] if dq_in else dqt[b][n]
            dq_ref[:, cols] = total.astype(dq_ref.dtype)


def blocks_call(xs, kvs, slots, rows, heads, scale, dkv_type, dq_type, acc=(), dq_in=(), diagonal=False):
    sds = jax.ShapeDtypeStruct
    width = kvs[0].shape[1]
    xs = [x if isinstance(x, list) else [x] for x in xs]
    slots = list(slots)
    totals = []
    for a, _ in acc:
        if all(a is not t for t in totals):
            totals.append(a)
    at = [([a is t for t in totals].index(True), n) for a, n in acc]
    plan = {
        "parts": [len(x) for x in xs],
        "kv": len(kvs),
        "acc": len(totals),
        "at": at,
        "dq_in": len(dq_in),
        "slots": slots,
        "diagonal": diagonal,
    }
    args = (*sum(xs, []), *kvs, *totals, *dq_in)
    types = dq_type if isinstance(dq_type, list) else [dq_type] * len(xs)
    outs = tuple(sds((width, heads * rows), t) for t in types)
    outs += (sds((len(slots), 2 * rows, width), dkv_type),)
    return pl.pallas_call(
        functools.partial(blocks_kernel, plan, rows, heads, scale),
        out_shape=outs,
        in_specs=[VMEM] * len(args),
        out_specs=(VMEM,) * len(outs),
        compiler_params=SMALL,
        cost_estimate=QUICK,
    )(*args)


def add_kernel(own_ref, got_ref, *refs):
    for n, ref in enumerate(refs):
        ref[...] = (own_ref[n] + got_ref[n].astype(F32)).astype(ref.dtype)


def add_call(own, got, types):
    return pl.pallas_call(
        add_kernel,
        out_shape=tuple(jax.ShapeDtypeStruct(own.shape[1:], t) for t in types),
        in_specs=[VMEM] * 2,
        out_specs=(VMEM,) * len(types),
        compiler_params=SMALL,
        cost_estimate=QUICK,
    )(own, got)


def sum_kernel(own_ref, *refs):
    total = own_ref[...]
    for ref in refs[:-1]:
        total = total + ref[...].astype(F32)
    refs[-1][...] = total


def sum_call(own, got, flops):
    return pl.pallas_call(
        sum_kernel,
        out_shape=jax.ShapeDtypeStruct(own.shape, F32),
        in_specs=[VMEM] * (1 + len(got)),
        out_specs=VMEM,
        compiler_params=SMALL,
        cost_estimate=pl.CostEstimate(flops=flops, bytes_accessed=1000, transcendentals=0),
    )(own, *got)


def query_kernel(rows, heads, scale, dq_ref, *refs):
    dq_refs, (gq_ref, part_s, sems) = refs[:-3], refs[-3:]
    copies = []
    for h in range(heads):
        at = slice(h * rows, (h + 1) * rows)
        dq = dq_ref[:, at]
        for ref in dq_refs:
            dq = dq + ref[:, at].astype(F32)
        part_s[h] = (scale * dq).T.astype(BF)
        width = part_s.shape[2]
        copies.append(pltpu.make_async_copy(part_s.at[h], gq_ref.at[:, pl.ds(h * width, width)], sems.at[h]))
        copies[-1].start()
    for copy in copies:
        copy.wait()


def key_kernel(rows, scale, dkv_ref, near_ref, gk_ref, gv_ref):
    gk_ref[...] = (scale * (dkv_ref[:rows, :] + near_ref[:rows, :].astype(F32))).astype(BF)
    gv_ref[...] = (dkv_ref[rows:, :] + near_ref[rows:, :].astype(F32)).astype(BF)


def crossed(block, t, other):
    pairs = []
    for i in range(lax.axis_size("inner")):
        chip, core = i // 2, i % 2
        pairs.append((i, 2 * (chip ^ (2 * t + (core if other else 1 - core))) + core))
    return lax.ppermute(block, "inner", pairs)


def on_device(query, key, value, out, grad_out, lse, positions):
    rows, width = key.shape
    heads = query.shape[1] // width
    hr = heads * rows
    scale = width ** (-0.5)
    nq = lax.axis_size("outer")
    nz = lax.axis_size("inner") // 2
    sds = jax.ShapeDtypeStruct
    inputs = (query, key, value, out, grad_out, lse, positions[None, :])
    x, kv = pl.pallas_call(
        pack_kernel,
        out_shape=(sds((2 * hr + 32, width), BF), sds((2 * rows + 16, width), BF)),
        in_specs=[pl.BlockSpec(memory_space=pltpu.HBM)] * 7,
        out_specs=(VMEM, VMEM),
        scratch_shapes=[
            pltpu.VMEM(out.shape, BF),
            pltpu.VMEM(lse.shape, F32),
            pltpu.VMEM((1, rows), jnp.int32),
            pltpu.SemaphoreType.DMA((5 + 2 * heads,)),
        ],
        compiler_params=SMALL,
        cost_estimate=QUICK,
    )(*[pltpu.with_memory_space_constraint(a, pltpu.HBM) for a in inputs])

    common = (rows, heads, scale)
    sib = swapped(kv, "inner", 1)
    near = swapped(kv, "inner", 2)
    direct = [crossed(block, t, False) for t in range(1, nz // 2) for block in (kv, sib)]
    early = [kv, sib, near]
    dq_own, acc = blocks_call([x], early, range(3), *common, F32, F32, diagonal=True)

    xs = [swapped(x, "outer", s) for s in range(1, nq - 1)]
    *xs, acc = lax.optimization_barrier((*xs, acc))
    halves = [xs[nq - 3][:hr], xs[((nq - 1) ^ (nq // 2)) - 1][hr:]]
    corner = [swapped(halves[0], "outer", 1), swapped(halves[1], "outer", nq // 2)]
    *dqs, acc = blocks_call(xs, early, range(3), *common, F32, F32, acc=[(acc, n) for n in range(3)])
    dqs = [dq_own, *dqs]

    *direct, acc = lax.optimization_barrier((*direct, acc))
    traded = [swapped(block, "inner", 1) for block in direct]
    direct = [swapped(near, "inner", 1), *direct]
    xs = [x, *xs]
    n_d, n_t = len(direct), len(traded)
    *dqs, acc_d = blocks_call(xs, direct, range(n_d), *common, F32, F32, dq_in=dqs)
    types = [F32] + [BF] * (nq - 2)
    dq_own, *dqs, acc_t = blocks_call(xs, traded, range(n_t), *common, F32, types, dq_in=dqs)

    arrays = [*early, *direct, *traded]
    accs = [(a, n) for a, count in ((acc, 3), (acc_d, n_d), (acc_t, n_t)) for n in range(count)]
    theirs, ours = [1, 3], [0, 2]
    for t in range(0, n_t, 2):
        theirs += [3 + n_d + t, 4 + t + 1]
        ours += [4 + t, 3 + n_d + t + 1]
    dq_last, dkv_sib = blocks_call([corner], arrays, theirs, *common, BF, F32, acc=accs)
    dkv_got = swapped(dkv_sib, "inner", 1)
    dq_last, dkv_own = blocks_call([corner], arrays, ours, *common, F32, BF, acc=accs, dq_in=[dq_last])
    dq_far = swapped(dq_last, "outer", nq - 1)
    dkv_own, dkv_near, *far = add_call(dkv_own, dkv_got, [F32] + [BF] * (nz - 1))
    got = [swapped(dq, "outer", s + 1) for s, dq in enumerate(dqs)]
    dkv = []
    for t in range(1, nz // 2):
        dkv.append(crossed(far[2 * t - 2], t, False))
        dkv.append(crossed(far[2 * t - 1], t, True))
    dkv_near = swapped(dkv_near, "inner", 2)

    dkv_sum = sum_call(dkv_own, dkv, 1_500_000_000)
    dq_sum = sum_call(dq_own, [dq_far], 100_000_000)
    dq_sum, dkv_sum = lax.optimization_barrier((dq_sum, dkv_sum))
    grad_query = pl.pallas_call(
        functools.partial(query_kernel, rows, heads, scale),
        out_shape=sds((rows, heads * width), BF),
        in_specs=[VMEM] * (1 + len(got)),
        out_specs=pl.BlockSpec(memory_space=pltpu.HBM),
        scratch_shapes=[pltpu.VMEM((heads, rows, width), BF), pltpu.SemaphoreType.DMA((heads,))],
        compiler_params=SMALL,
        cost_estimate=QUICK,
    )(dq_sum, *got)
    dkv_near, grad_query = lax.optimization_barrier((dkv_near, grad_query))
    grad_key, grad_value = pl.pallas_call(
        functools.partial(key_kernel, rows, scale),
        out_shape=(sds((rows, width), BF),) * 2,
        in_specs=[VMEM] * 2,
        out_specs=(VMEM,) * 2,
        compiler_params=SMALL,
        cost_estimate=QUICK,
    )(dkv_sum, dkv_near)
    return grad_query, grad_key, grad_value


def solution(mesh):
    tokens = P(("outer", "inner"), None)
    return jax.shard_map(
        on_device,
        mesh=mesh,
        in_specs=(tokens,) * 5 + (P(None, ("outer", "inner")), P(("outer", "inner"))),
        out_specs=(tokens,) * 3,
        check_vma=False,
    )
```
